32 devices in a mesh: leaf: 16 (over z, y, core), samp: 2 (over x).
Axes of the slice: x: 2, y: 2, z: 4, core: 2. Of those that a mesh axis runs over, the one named last changes fastest.
Arguments:
- stiffness_block_row: bfloat16 [256, 8, 128, 128], P('leaf'), may hold values from -2 to 2
- stored_block_column: int32 [256, 8], P('leaf'), may hold values from 0 to 255, as said below
- samples_t: bfloat16 [256, 32768], P('samp', 'leaf'), may hold values from -8 to 8
Outputs:
- products: float32 [256, 32768], P('samp', 'leaf')
- bases: float32 [256, 32768], P('samp', 'leaf')
- transfer_one: float32 [4096, 256], P('leaf', 'samp')
- transfer_two: float32 [4096, 256], P('leaf', 'samp')
- transfer_three: float32 [4096, 256], P('leaf', 'samp')
- top_factor: float32 [4096, 256], P('leaf', 'samp')
The draws below stay inside these ranges and needn't reach their ends.
Inputs may be any that keep to these rules, and one draw needn't show every extreme that they name: `stored_block_column`: slot 0 of block row r names block column r; the other slots name block columns of the same leaf, or of a neighbouring leaf within 4 block rows of the boundary that the two leaves share; the first block row of every leaf that has a neighbour on a side reaches exactly 4 block rows into it, and every one of those 4 block rows is named by some block row of the leaf.
All inputs are finite; a program needn't handle non-finite values.
Results may differ from the reference program's by a relative error of at most 0.0003.
Values may be sent and summed in bfloat16 or wider, within the bound.
No kernel may reach another device: no remote copies, remote signals or barrier semaphores. Data moves between devices by JAX's collectives and lax.ppermute only.
A program may use at most 64 MiB of HBM per device.

```python
import math
import jax
import jax.numpy as jnp
from jax import lax

S = 256
BS = 128
NB = 8
HB = 4
LEVELS = 3
RDEV = 2048
N = 32768
BROWS = 256
NODEROWS = 4096
N_LEAF = 16


def draw_stored_block_column(key, part):
    per_leaf = RDEV // BS
    leaf_total = BROWS // per_leaf
    row_index = jnp.arange(BROWS, dtype=jnp.int32)
    leaf_number = (row_index // per_leaf)[:, None]
    leaf_start = leaf_number * per_leaf
    row_in_leaf = (row_index % per_leaf)[:, None]
    key_own = jax.random.fold_in(key, 11)
    key_below = jax.random.fold_in(key, 23)
    key_above = jax.random.fold_in(key, 37)
    own_cols = leaf_start + jax.random.randint(key_own, (BROWS, 5), 0, per_leaf, dtype=jnp.int32)
    below_cols = leaf_start - HB + jax.random.randint(key_below, (BROWS, 2), 0, HB, dtype=jnp.int32)
    above_cols = leaf_start + per_leaf + jax.random.randint(key_above, (BROWS, 2), 0, HB, dtype=jnp.int32)
    first_slot = (jnp.arange(2, dtype=jnp.int32) == 0)[None, :]
    below_cycle = leaf_start - HB + row_in_leaf % HB
    above_cycle = leaf_start + per_leaf + (row_in_leaf + HB - 1) % HB
    below_cols = jnp.where(first_slot, below_cycle, below_cols)
    above_cols = jnp.where(first_slot, above_cycle, above_cols)
    below_cols = jnp.where(leaf_number > 0, below_cols, own_cols[:, 3:5])
    above_cols = jnp.where(leaf_number < leaf_total - 1, above_cols, own_cols[:, 3:5])
    joined = jnp.concatenate([row_index[:, None], own_cols[:, 0:3], below_cols, above_cols], axis=1)
    return joined.astype(jnp.int32)


def draw_stiffness_block_row(key, part):
    key_noise = jax.random.fold_in(key, 101)
    spread = 0.5 / (NB * BS) ** 0.5
    noise = jax.random.normal(key_noise, (BROWS, NB, BS, BS), jnp.float32)
    diagonal = jnp.eye(BS, dtype=jnp.float32)[None, None, :, :] / NB ** 0.5
    return (noise * spread + diagonal).astype(jnp.bfloat16)


def draw_samples_t(key, part):
    key_noise = jax.random.fold_in(key, 201)
    values = jnp.clip(jax.random.normal(key_noise, (S, N), jnp.float32), -6.0, 6.0)
    return values.astype(jnp.bfloat16)


def setup_inputs(seed: int = 0) -> dict:
    streams_of = jax.random.split(jax.random.key(seed), 4)
    stiffness_block_row = draw_stiffness_block_row(jax.random.fold_in(streams_of[3], 71), 0)
    stored_block_column = draw_stored_block_column(jax.random.fold_in(streams_of[3], 71), 0)
    samples_t = draw_samples_t(jax.random.fold_in(streams_of[3], 71), 0)
    return dict(stiffness_block_row=stiffness_block_row, stored_block_column=stored_block_column, samples_t=samples_t)


def lower_solve(factor, right_side):
    return jax.scipy.linalg.solve_triangular(factor, right_side, lower=True)

def reference(stiffness_block_row, stored_block_column, samples_t):
    per_leaf = RDEV // BS
    sample_blocks = samples_t.reshape(S, BROWS, BS)

    def one_leaf(leaf_input_vectors):
        leaf_blocks, leaf_cols, leaf_number = leaf_input_vectors
        picked = jnp.take(sample_blocks, leaf_cols.reshape(-1), axis=1).reshape(S, per_leaf, NB, BS)
        inside = leaf_cols // per_leaf == leaf_number
        terms = jnp.einsum('rkij,srkj->srki', leaf_blocks.astype(jnp.float32), picked.astype(jnp.float32))
        whole_sum = lax.optimization_barrier(jnp.sum(terms, axis=2))
        remote_sum = lax.optimization_barrier(jnp.sum(jnp.where(inside[None, :, :, None], jnp.zeros_like(terms), terms), axis=2))
        return (whole_sum.reshape(S, RDEV), remote_sum.reshape(S, RDEV))
    whole_sum, distant_portion = lax.map(one_leaf, (stiffness_block_row.reshape(N_LEAF, per_leaf, NB, BS, BS), stored_block_column.reshape(N_LEAF, per_leaf, NB), jnp.arange(N_LEAF, dtype=jnp.int32)))
    products = jnp.transpose(whole_sum, (1, 0, 2)).reshape(S, N)
    gramian_product = jnp.einsum('fjd,fwd->fjw', distant_portion, distant_portion, precision=lax.Precision.HIGHEST)
    factor = jnp.linalg.cholesky(gramian_product)
    leaf_basis = jax.vmap(lower_solve)(factor, distant_portion) * math.sqrt(RDEV)
    bases = jnp.transpose(leaf_basis, (1, 0, 2)).reshape(S, N)
    results = []
    for height in range(LEVELS):
        pairs = gramian_product.reshape(-1, 2, S, S)
        parent = pairs[:, 0] + pairs[:, 1]
        parent_low = jnp.linalg.cholesky(parent)
        blocks = jax.vmap(lower_solve)(jnp.repeat(parent_low, 2, axis=0), factor)
        results.append(jnp.repeat(blocks, 2 ** height, axis=0).reshape(NODEROWS, S))
        gramian_product, factor = (parent, parent_low)
    top_factor = jnp.repeat(factor, 2 ** LEVELS, axis=0).reshape(NODEROWS, S) / math.sqrt(2 ** LEVELS * RDEV)
    return (products, bases, results[0], results[1], results[2], top_factor)
```

```python
import functools
import math

import jax
import jax.numpy as jnp
from jax import lax
from jax.experimental import pallas as pl
from jax.experimental.pallas import tpu as pltpu
from jax.sharding import PartitionSpec as P

HB = 4
LEVELS = 3
LANES = 128
GROUP = 8
PANEL = 32
ROWS_A_STEP = 2
VMEM_LIMIT = 48 * 1024 * 1024
F32 = jnp.float32
BF16 = jnp.bfloat16
NN = (((1,), (0,)), ((), ()))
NT = (((1,), (1,)), ((), ()))
TN = (((0,), (0,)), ((), ()))


def dot(a, b, dims):
    return lax.dot_general(a, b, dims, preferred_element_type=F32)


def split_two(x):
    high = x.astype(BF16)
    return high, (x - high.astype(F32)).astype(BF16)


def split_three(x):
    high = x.astype(BF16)
    rest = x - high.astype(F32)
    middle = rest.astype(BF16)
    return high, middle, (rest - middle.astype(F32)).astype(BF16)


def dot_split(a, b, dims):
    (a_high, a_low), (b_high, b_low) = a, b
    return dot(a_high, b_high, dims) + (dot(a_high, b_low, dims) + dot(a_low, b_high, dims))


def block_row_product(window, chosen, blocks, rr):
    total = None
    count = blocks.shape[1]
    width = blocks.shape[3]
    for k in range(0, count, 2):
        taken = [window[:, pl.ds(pl.multiple_of(chosen(k + e) * width, LANES), width)] for e in (0, 1)]
        left = jnp.concatenate(taken, axis=1)
        right = jnp.concatenate([blocks[rr, k], blocks[rr, k + 1]], axis=1)
        term = dot(left, right, NT)
        total = term if total is None else total + term
    return total


def near_kernel(place, columns, blocks, samples, near, window):
    step = pl.program_id(0)
    width = blocks.shape[3]
    rows_step = blocks.shape[0]
    count = rows_step * pl.num_programs(0)

    @pl.when(step == 0)
    def _():
        window[:, : samples.shape[1]] = samples[...]
        window[:, samples.shape[1] :] = jnp.zeros((samples.shape[0], width), BF16)

    for rr in range(rows_step):

        def chosen(k):
            local = columns[step * rows_step + rr, k] - place[0] * count
            return jnp.where((local >= 0) & (local < count), local, count)

        near[:, rr * width : (rr + 1) * width] = block_row_product(window, chosen, blocks, rr)


def far_kernel(sample_parts, place, columns, blocks, *refs):
    pieces = refs[: 2 * sample_parts]
    near, products, z_high, z_low, packed, window, z_scr, gram, cross = refs[2 * sample_parts :]
    step = pl.program_id(0)
    steps = pl.num_programs(0)
    width = blocks.shape[3]
    rows_step = blocks.shape[0]
    count = rows_step * steps
    own = near.shape[0]
    reach = HB * width

    @pl.when(step == 0)
    def _():
        for d in range(sample_parts):
            source = lax.rem(place[1] + sample_parts - d, sample_parts)
            rows = pl.ds(pl.multiple_of(source * own, own), own)
            window[rows, :reach] = pieces[2 * d][...]
            window[rows, reach : 2 * reach] = pieces[2 * d + 1][...]
        window[:, 2 * reach :] = jnp.zeros((window.shape[0], width), BF16)
        gram[...] = jnp.zeros_like(gram)
        cross[...] = jnp.zeros_like(cross)

    for rr in range(rows_step):

        def chosen(k):
            local = columns[step * rows_step + rr, k] - place[0] * count
            below = jnp.clip(local + HB, 0, HB - 1)
            above = jnp.clip(local - count + HB, HB, 2 * HB - 1)
            return jnp.where(local < 0, below, jnp.where(local < count, 2 * HB, above))

        z_scr[:, rr * width : (rr + 1) * width] = block_row_product(window, chosen, blocks, rr)
    remote = z_scr[...]
    high, low = split_two(remote)
    z_high[...] = high
    z_low[...] = low
    products[...] = near[...] + z_scr[pl.ds(pl.multiple_of(place[1] * own, own), own), :]
    gram[...] += dot(high, high, NT)
    cross[...] += dot(high, low, NT)

    @pl.when(step == steps - 1)
    def _():
        pack_symmetric(packed, gram[...] + (cross[...] + cross[...].T))


def square_iota(n):
    return lax.broadcasted_iota(jnp.int32, (n, n), 0), lax.broadcasted_iota(jnp.int32, (n, n), 1)


def pack_symmetric(packed, full):
    h = full.shape[0] // 2
    row, col = square_iota(h)
    first = full[:h, :h]
    packed[:h, :] = full[:h, h:]
    packed[h : 2 * h, :] = jnp.where(row > col, first, full[h:, h:])
    diagonal = jnp.sum(jnp.where(row == col, first, 0.0), axis=0, keepdims=True)
    packed[2 * h :, :] = jnp.broadcast_to(diagonal, (GROUP, h))


def unpack_symmetric(packed, full, b):
    h = packed.shape[1]
    row, col = square_iota(h)
    shared = packed[h : 2 * h, :]
    lower = jnp.where(row > col, shared, 0.0)
    diagonal = jnp.where(row == col, jnp.broadcast_to(packed[2 * h : 2 * h + 1, :], (h, h)), 0.0)
    upper = jnp.where(row <= col, shared, 0.0)
    full[b, :h, :h] = lower + lower.T + diagonal
    full[b, h:, h:] = upper + jnp.where(row < col, upper, 0.0).T
    full[b, :h, h:] = packed[:h, :]


def row_of(x, j):
    return jnp.broadcast_to(x[:, j : j + 1, :], x.shape)


def factor(a, m):
    batch, n, _ = a.shape
    chunks = n // LANES
    groups = PANEL // GROUP
    tile = (batch, GROUP, LANES)
    sub = lax.broadcasted_iota(jnp.int32, tile, 1)
    lane = lax.broadcasted_iota(jnp.int32, tile, 2)
    for c in range(chunks):
        for b in range(batch):
            row, col = square_iota(LANES)
            for e in range(c + 1):
                m[b, c * LANES : (c + 1) * LANES, e * LANES : (e + 1) * LANES] = (
                    (row == col).astype(F32) if e == c else jnp.zeros((LANES, LANES), F32)
                )
            for e in range(c + 1, chunks):
                m[b, c * LANES : (c + 1) * LANES, e * LANES : (e + 1) * LANES] = jnp.zeros((LANES, LANES), F32)
    for p in range(0, n, PANEL):
        ch = p // LANES
        parts = [(a, c) for c in range(ch, chunks)] + [(m, c) for c in range(ch + 1)]
        rows = [slice(p + GROUP * g, p + GROUP * (g + 1)) for g in range(groups)]
        r = [[ref[:, rows[g], c * LANES : (c + 1) * LANES] for ref, c in parts] for g in range(groups)]
        for g0 in range(groups):
            at = p - ch * LANES + GROUP * g0
            v = [
                [jnp.broadcast_to(r[g][0][:, :, at + k : at + k + 1], tile) for k in range(GROUP)]
                if g >= g0
                else None
                for g in range(groups)
            ]
            head, top = v[g0], r[g0]
            recips, v_rows, r_rows = [], [], []
            pivots = None
            for j in range(GROUP):
                d = row_of(head[j], j)
                rc = 1.0 / d
                recips.append(rc)
                pivots = d if pivots is None else jnp.where(sub == j, d, pivots)
                v_rows.append([row_of(head[k], j) if k > j else None for k in range(GROUP)])
                r_rows.append([row_of(x, j) for x in top])
                if j < GROUP - 1:
                    below = jnp.where(sub > j, head[j], 0.0)
                    scaled = below * rc
                    for k in range(j + 1, GROUP):
                        if k == j + 1:
                            head[k] = head[k] - (below * v_rows[j][k]) * rc
                        else:
                            head[k] = head[k] - scaled * v_rows[j][k]
                    for x in range(len(top)):
                        top[x] = top[x] - scaled * r_rows[j][x]
            for g in range(g0 + 1, groups):
                for j in range(GROUP):
                    scaled = v[g][j] * recips[j]
                    for k in range(j + 1, GROUP):
                        v[g][k] = v[g][k] - scaled * v_rows[j][k]
                    for x in range(len(top)):
                        r[g][x] = r[g][x] - scaled * r_rows[j][x]
            scale = lax.rsqrt(pivots)
            for x, (ref, c) in enumerate(parts):
                done = top[x] * scale
                if ref is a and c == ch:
                    done = jnp.where(lane >= sub + at, done, 0.0)
                r[g0][x] = done
                ref[:, rows[g0], c * LANES : (c + 1) * LANES] = done
        if p + PANEL == n:
            break
        for b in range(batch):
            panel = jnp.concatenate(
                [jnp.concatenate([r[g][x][b] for g in range(groups)], axis=0) for x in range(len(parts))], axis=1
            )
            h, mid, low = split_three(panel)
            left = jnp.concatenate([h, h, mid, mid, h, low], axis=0)
            right = jnp.concatenate([h, mid, h, mid, low, h], axis=0)
            for c in range(ch, chunks):
                start = max(p + PANEL, c * LANES)
                stop = (c + 1) * LANES
                if start >= stop:
                    continue
                x0 = c - ch
                update = dot(left[:, x0 * LANES : (x0 + 1) * LANES], right, TN)[start - c * LANES :, :]
                for x, (ref, e) in enumerate(parts):
                    if ref is a and e < c:
                        continue
                    lanes = slice(e * LANES, (e + 1) * LANES)
                    ref[b, start:stop, lanes] = ref[b, start:stop, lanes] - update[:, x * LANES : (x + 1) * LANES]
    for b in range(batch):
        for c in range(1, chunks):
            for e in range(c):
                a[b, c * LANES : (c + 1) * LANES, e * LANES : (e + 1) * LANES] = jnp.zeros((LANES, LANES), F32)


def leaf_kernel(scale, place, packed, z_high, z_low, bases, upper_own, a, m):
    unpack_symmetric(packed, a, 0)
    factor(a, m)
    own = upper_own.shape[0]
    rows = pl.ds(pl.multiple_of(place[1] * own, own), own)
    upper_own[...] = a[0, rows, :]
    inverse = split_two(m[0, rows, :] * scale)
    for c in range(0, z_high.shape[1], 512):
        lanes = slice(c, c + 512)
        bases[:, lanes] = dot_split(inverse, (z_high[:, lanes], z_low[:, lanes]), NN)


def tree_kernel(top_scale, place, upper_own, *refs):
    levels = (len(refs) - 3) // 2
    packed = refs[:levels]
    transfers = refs[levels : 2 * levels]
    top, a, m = refs[2 * levels :]
    for b in range(levels):
        unpack_symmetric(packed[b], a, b)
    factor(a, m)
    own = upper_own.shape[0]
    rows = pl.ds(pl.multiple_of(place[1] * own, own), own)
    for b in range(levels):
        child = upper_own[...] if b == 0 else a[b - 1, rows, :]
        transfers[b][...] = dot_split(split_two(m[b]), split_two(child), NT)
    top[...] = (a[levels - 1, rows, :] * top_scale).T


def whole():
    return pl.BlockSpec(memory_space=pltpu.VMEM)


def params():
    return pltpu.CompilerParams(vmem_limit_bytes=VMEM_LIMIT)


def from_partner(block, axis, bit):
    count = lax.axis_size(axis)
    route = []
    for low in range(count):
        high = low | 1 << bit
        if high != low and high < count:
            route += [(low, high), (high, low)]
    return lax.ppermute(block, axis, route)


def halo_pieces(samples, reach):
    leaves, parts = lax.axis_size("leaf"), lax.axis_size("samp")
    head = samples[:, :reach]
    tail = samples[:, samples.shape[1] - reach :]
    pieces = []
    for d in range(parts):
        up, down = [], []
        for leaf in range(leaves):
            for part in range(parts):
                source = leaf * parts + part
                other = (part + d) % parts
                if leaf + 1 < leaves:
                    up.append((source, (leaf + 1) * parts + other))
                if leaf > 0:
                    down.append((source, (leaf - 1) * parts + other))
        pieces.append(lax.ppermute(tail, ("leaf", "samp"), up))
        pieces.append(lax.ppermute(head, ("leaf", "samp"), down))
    return pieces


def shards(stiffness, columns, samples):
    blocks_here, slots, width, _ = stiffness.shape
    own, row_count = samples.shape
    parts = lax.axis_size("samp")
    total = own * parts
    reach = HB * width
    place = jnp.stack([lax.axis_index("leaf"), lax.axis_index("samp")]).astype(jnp.int32)
    steps = blocks_here // ROWS_A_STEP
    step_lanes = ROWS_A_STEP * width
    shape = jax.ShapeDtypeStruct

    pieces = halo_pieces(samples, reach)

    block_spec = pl.BlockSpec((ROWS_A_STEP, slots, width, width), lambda i, *_: (i, 0, 0, 0))
    own_spec = pl.BlockSpec((own, step_lanes), lambda i, *_: (0, i))
    all_spec = pl.BlockSpec((total, step_lanes), lambda i, *_: (0, i))

    def fixed(*dims):
        return pl.BlockSpec(dims, lambda i, *_: (0,) * len(dims))

    near = pl.pallas_call(
        near_kernel,
        grid_spec=pltpu.PrefetchScalarGridSpec(
            num_scalar_prefetch=2,
            grid=(steps,),
            in_specs=[block_spec, fixed(own, row_count)],
            out_specs=own_spec,
            scratch_shapes=[pltpu.VMEM((own, row_count + width), BF16)],
        ),
        out_shape=shape((own, row_count), F32),
        compiler_params=params(),
        cost_estimate=pl.CostEstimate(
            flops=2 * own * slots * width * row_count, bytes_accessed=6 * 1024 * 1024, transcendentals=0
        ),
        name="near",
    )(place, columns, stiffness, samples)

    packed_shape = (total + GROUP, total // 2)
    products, z_high, z_low, packed = pl.pallas_call(
        functools.partial(far_kernel, parts),
        grid_spec=pltpu.PrefetchScalarGridSpec(
            num_scalar_prefetch=2,
            grid=(steps,),
            in_specs=[block_spec] + [fixed(own, reach)] * (2 * parts) + [own_spec],
            out_specs=[own_spec, all_spec, all_spec, fixed(*packed_shape)],
            scratch_shapes=[
                pltpu.VMEM((total, 2 * reach + width), BF16),
                pltpu.VMEM((total, step_lanes), F32),
                pltpu.VMEM((total, total), F32),
                pltpu.VMEM((total, total), F32),
            ],
        ),
        out_shape=[
            shape((own, row_count), F32),
            shape((total, row_count), BF16),
            shape((total, row_count), BF16),
            shape(packed_shape, F32),
        ],
        compiler_params=params(),
        name="far",
    )(place, columns, stiffness, *pieces, near)

    smem = pl.BlockSpec(memory_space=pltpu.SMEM)
    grams = []
    current = packed
    for height in range(LEVELS):
        current = current + from_partner(current, "leaf", height)
        grams.append(current)

    def factor_scratch(batch):
        return [pltpu.VMEM((batch, total, total), F32)] * 2

    bases, upper_own = pl.pallas_call(
        functools.partial(leaf_kernel, math.sqrt(row_count)),
        in_specs=[smem] + [whole()] * 3,
        out_specs=[whole()] * 2,
        out_shape=[shape((own, row_count), F32), shape((own, total), F32)],
        scratch_shapes=factor_scratch(1),
        compiler_params=params(),
        name="leaf",
    )(place, packed, z_high, z_low)

    outs = pl.pallas_call(
        functools.partial(tree_kernel, 1.0 / math.sqrt(2**LEVELS * row_count)),
        in_specs=[smem, whole()] + [whole()] * LEVELS,
        out_specs=[whole()] * (LEVELS + 1),
        out_shape=[shape((total, own), F32)] * (LEVELS + 1),
        scratch_shapes=factor_scratch(LEVELS),
        compiler_params=params(),
        name="tree",
    )(place, upper_own, *grams)
    return (products, bases, *outs)


def solution(mesh):
    return jax.shard_map(
        shards,
        mesh=mesh,
        in_specs=(P("leaf", None, None, None), P("leaf", None), P("samp", "leaf")),
        out_specs=(
            P("samp", "leaf"),
            P("samp", "leaf"),
            P("leaf", "samp"),
            P("leaf", "samp"),
            P("leaf", "samp"),
            P("leaf", "samp"),
        ),
        check_vma=False,
    )
```

```python
import functools
import math

import jax
import jax.numpy as jnp
from jax import lax
from jax.experimental import pallas as pl
from jax.experimental.pallas import tpu as pltpu
from jax.sharding import PartitionSpec as P

HB = 4
LEVELS = 3
LANES = 128
GROUP = 8
PANEL = 32
ROWS_A_STEP = 4
VMEM_LIMIT = 48 * 1024 * 1024
F32 = jnp.float32
BF16 = jnp.bfloat16
NN = (((1,), (0,)), ((), ()))
NT = (((1,), (1,)), ((), ()))
TN = (((0,), (0,)), ((), ()))


def dot(a, b, dims):
    return lax.dot_general(a, b, dims, preferred_element_type=F32)


def split_two(x):
    high = x.astype(BF16)
    return high, (x - high.astype(F32)).astype(BF16)


def split_three(x):
    high = x.astype(BF16)
    rest = x - high.astype(F32)
    middle = rest.astype(BF16)
    return high, middle, (rest - middle.astype(F32)).astype(BF16)


def dot_split(a, b, dims):
    (a_high, a_low), (b_high, b_low) = a, b
    return dot(a_high, b_high, dims) + (dot(a_high, b_low, dims) + dot(a_low, b_high, dims))


def taken(window, chosen, slots, width):
    lanes = [pl.ds(pl.multiple_of(chosen(k) * width, LANES), width) for k in range(slots)]
    return jnp.concatenate([window[:, at] for at in lanes], axis=1)


def block_row(blocks, rr):
    return jnp.concatenate([blocks[rr, k] for k in range(blocks.shape[1])], axis=1)


def far_position(local, count, odd):
    lower = jnp.where(odd, 0, HB)
    below = jnp.clip(local + HB, 0, HB - 1) + lower
    above = jnp.clip(local - count, 0, HB - 1) + (HB - lower)
    return jnp.where(local < 0, below, jnp.where(local < count, 2 * HB, above))


def own_kernel(place, columns, blocks, samples, halo, products, z_high, z_low, near_window, far_window):
    step = pl.program_id(0)
    rows_step, slots, width, _ = blocks.shape
    count = rows_step * pl.num_programs(0)
    own = samples.shape[0]
    odd = lax.rem(place[0], 2) == 1

    @pl.when(step == 0)
    def _():
        near_window[:, : samples.shape[1]] = samples[...]
        near_window[:, samples.shape[1] :] = jnp.zeros((own, width), BF16)
        far_window[:, : halo.shape[1]] = halo[...]
        far_window[:, halo.shape[1] :] = jnp.zeros((own, width), BF16)

    for rr in range(rows_step):

        def local(k):
            return columns[k, step * rows_step + rr] - place[0] * count

        def near(k):
            return jnp.where((local(k) >= 0) & (local(k) < count), local(k), count)

        def far(k):
            return far_position(local(k), count, odd)

        left = jnp.concatenate(
            [taken(near_window, near, slots, width), taken(far_window, far, slots, width)], axis=0
        )
        both = dot(left, block_row(blocks, rr), NT)
        lanes = slice(rr * width, (rr + 1) * width)
        products[:, lanes] = both[:own] + both[own:]
        z_high[:, lanes], z_low[:, lanes] = split_two(both[own:])


def others_kernel(parts, place, columns, blocks, *refs):
    halos = refs[: parts - 1]
    own_high, own_low, z_high, z_low, packed, window, gram, cross = refs[parts - 1 :]
    step = pl.program_id(0)
    rows_step, slots, width, _ = blocks.shape
    count = rows_step * pl.num_programs(0)
    own = own_high.shape[0]
    odd = lax.rem(place[0], 2) == 1
    rows = [
        pl.ds(pl.multiple_of(lax.rem(place[1] + parts - d, parts) * own, own), own) for d in range(parts)
    ]

    @pl.when(step == 0)
    def _():
        for d in range(1, parts):
            window[(d - 1) * own : d * own, : 2 * HB * width] = halos[d - 1][...]
        window[:, 2 * HB * width :] = jnp.zeros((window.shape[0], width), BF16)
        gram[...] = jnp.zeros_like(gram)
        cross[...] = jnp.zeros_like(cross)

    z_high[rows[0], :] = own_high[...]
    z_low[rows[0], :] = own_low[...]
    for rr in range(rows_step):

        def far(k):
            return far_position(columns[k, step * rows_step + rr] - place[0] * count, count, odd)

        remote = dot(taken(window, far, slots, width), block_row(blocks, rr), NT)
        high, low = split_two(remote)
        lanes = slice(rr * width, (rr + 1) * width)
        for d in range(1, parts):
            z_high[rows[d], lanes] = high[(d - 1) * own : d * own]
            z_low[rows[d], lanes] = low[(d - 1) * own : d * own]
        if rr % 2 == 1:
            pair = slice((rr - 1) * width, (rr + 1) * width)
            high, low = z_high[:, pair], z_low[:, pair]
            gram[...] += dot(high, high, NT)
            cross[...] += dot(high, low, NT)

    @pl.when(step == pl.num_programs(0) - 1)
    def _():
        pack_symmetric(packed, gram[...] + (cross[...] + cross[...].T))


def square_iota(n):
    return lax.broadcasted_iota(jnp.int32, (n, n), 0), lax.broadcasted_iota(jnp.int32, (n, n), 1)


def pack_symmetric(packed, full):
    h = full.shape[0] // 2
    row, col = square_iota(h)
    first = full[:h, :h]
    packed[:h, :] = full[:h, h:]
    packed[h : 2 * h, :] = jnp.where(row > col, first, full[h:, h:])
    diagonal = jnp.sum(jnp.where(row == col, first, 0.0), axis=0, keepdims=True)
    packed[2 * h :, :] = jnp.broadcast_to(diagonal, (GROUP, h))


def unpack_symmetric(packed, full, b):
    h = packed.shape[1]
    row, col = square_iota(h)
    shared = packed[h : 2 * h, :]
    lower = jnp.where(row > col, shared, 0.0)
    diagonal = jnp.where(row == col, jnp.broadcast_to(packed[2 * h : 2 * h + 1, :], (h, h)), 0.0)
    upper = jnp.where(row <= col, shared, 0.0)
    full[b, :h, :h] = lower + lower.T + diagonal
    full[b, h:, h:] = upper + jnp.where(row < col, upper, 0.0).T
    full[b, :h, h:] = packed[:h, :]


def row_of(x, j):
    return jnp.broadcast_to(x[:, j : j + 1, :], x.shape)


def start_inverse(m):
    batch, n, _ = m.shape
    row, col = square_iota(LANES)
    for b in range(batch):
        for c in range(0, n, LANES):
            for e in range(0, n, LANES):
                m[b, c : c + LANES, e : e + LANES] = (
                    (row == col).astype(F32) if e == c else jnp.zeros((LANES, LANES), F32)
                )


def clear_lower(a):
    batch, n, _ = a.shape
    for b in range(batch):
        for c in range(LANES, n, LANES):
            a[b, c : c + LANES, :c] = jnp.zeros((LANES, c), F32)


def factor(a, m, first, last):
    batch, n, _ = a.shape
    chunks = n // LANES
    groups = PANEL // GROUP
    tile = (batch, GROUP, LANES)
    sub = lax.broadcasted_iota(jnp.int32, tile, 1)
    lane = lax.broadcasted_iota(jnp.int32, tile, 2)
    for p in range(first, last, PANEL):
        ch = p // LANES
        parts = [(a, c) for c in range(ch, chunks)] + [(m, c) for c in range(ch + 1)]
        rows = [slice(p + GROUP * g, p + GROUP * (g + 1)) for g in range(groups)]
        r = [[ref[:, rows[g], c * LANES : (c + 1) * LANES] for ref, c in parts] for g in range(groups)]
        for g0 in range(groups):
            at = p - ch * LANES + GROUP * g0
            v = [
                [jnp.broadcast_to(r[g][0][:, :, at + k : at + k + 1], tile) for k in range(GROUP)]
                if g >= g0
                else None
                for g in range(groups)
            ]
            head, top = v[g0], r[g0]
            recips, v_rows, r_rows = [], [], []
            pivots = None
            for j in range(GROUP):
                d = row_of(head[j], j)
                rc = invert(d)
                recips.append(rc)
                pivots = d if pivots is None else jnp.where(sub == j, d, pivots)
                v_rows.append([row_of(head[k], j) if k > j else None for k in range(GROUP)])
                r_rows.append([row_of(x, j) for x in top])
                if j < GROUP - 1:
                    below = jnp.where(sub > j, head[j], 0.0)
                    scaled = below * rc
                    for k in range(j + 1, GROUP):
                        if k == j + 1:
                            head[k] = head[k] - (below * v_rows[j][k]) * rc
                        else:
                            head[k] = head[k] - scaled * v_rows[j][k]
                    for x in range(len(top)):
                        top[x] = top[x] - scaled * r_rows[j][x]
            for g in range(g0 + 1, groups):
                for j in range(GROUP):
                    scaled = v[g][j] * recips[j]
                    for k in range(j + 1, GROUP):
                        v[g][k] = v[g][k] - scaled * v_rows[j][k]
                    for x in range(len(top)):
                        r[g][x] = r[g][x] - scaled * r_rows[j][x]
            scale = lax.rsqrt(pivots)
            for x, (ref, c) in enumerate(parts):
                done = top[x] * scale
                if ref is a and c == ch:
                    done = jnp.where(lane >= sub + at, done, 0.0)
                r[g0][x] = done
                ref[:, rows[g0], c * LANES : (c + 1) * LANES] = done
        if p + PANEL == n:
            break
        for b in range(batch):
            panel = jnp.concatenate(
                [jnp.concatenate([r[g][x][b] for g in range(groups)], axis=0) for x in range(len(parts))], axis=1
            )
            h, mid, low = split_three(panel)
            left = jnp.concatenate([h, h, mid, mid, h, low], axis=0)
            right = jnp.concatenate([h, mid, h, mid, low, h], axis=0)
            for c in range(ch, chunks):
                start = max(p + PANEL, c * LANES)
                stop = (c + 1) * LANES
                if start >= stop:
                    continue
                x0 = c - ch
                update = dot(left[:, x0 * LANES : (x0 + 1) * LANES], right, TN)[start - c * LANES :, :]
                for x, (ref, e) in enumerate(parts):
                    if ref is a and e < c:
                        continue
                    lanes = slice(e * LANES, (e + 1) * LANES)
                    ref[b, start:stop, lanes] = ref[b, start:stop, lanes] - update[:, x * LANES : (x + 1) * LANES]


def invert(x):
    guess = pl.reciprocal(x, approx=True)
    return guess * (2.0 - x * guess)


def own_rows(place, own):
    return pl.ds(pl.multiple_of(place[1] * own, own), own)


def first_kernel(packed_zero, packed_one, a, m):
    unpack_symmetric(packed_zero, a, 0)
    unpack_symmetric(packed_one, a, 1)
    start_inverse(m)
    factor(a, m, 0, a.shape[1] // 2)


def second_kernel(scale, place, a_in, m_in, z_high, z_low, bases, transfer, upper_own, a, m):
    del a_in, m_in
    n = a.shape[1]
    factor(a, m, n // 2, n)
    clear_lower(a)
    own = upper_own.shape[0]
    rows = own_rows(place, own)
    upper_own[...] = a[1, rows, :]
    transfer[...] = dot_split(split_two(m[1]), split_two(a[0, rows, :]), NT)
    inverse = split_two(m[0, rows, :] * scale)
    for c in range(0, z_high.shape[1], 512):
        lanes = slice(c, c + 512)
        bases[:, lanes] = dot_split(inverse, (z_high[:, lanes], z_low[:, lanes]), NN)


def tree_kernel(top_scale, place, upper_own, *refs):
    levels = (len(refs) - 3) // 2
    packed = refs[:levels]
    transfers = refs[levels : 2 * levels]
    top, a, m = refs[2 * levels :]
    for b in range(levels):
        unpack_symmetric(packed[b], a, b)
    start_inverse(m)
    factor(a, m, 0, a.shape[1])
    clear_lower(a)
    own = upper_own.shape[0]
    rows = own_rows(place, own)
    for b in range(levels):
        child = upper_own[...] if b == 0 else a[b - 1, rows, :]
        transfers[b][...] = dot_split(split_two(m[b]), split_two(child), NT)
    top[...] = (a[levels - 1, rows, :] * top_scale).T


def whole():
    return pl.BlockSpec(memory_space=pltpu.VMEM)


def params():
    return pltpu.CompilerParams(vmem_limit_bytes=VMEM_LIMIT)


def from_partner(block, axis, bit):
    count = lax.axis_size(axis)
    route = []
    for low in range(count):
        high = low | 1 << bit
        if high != low and high < count:
            route += [(low, high), (high, low)]
    return lax.ppermute(block, axis, route)


def swap_across(block, odd_start):
    count = lax.axis_size("leaf")
    route = []
    for low in range(odd_start, count - 1, 2):
        route += [(low, low + 1), (low + 1, low)]
    return lax.ppermute(block, "leaf", route)


def sample_shift(block, d):
    count = lax.axis_size("samp")
    return lax.ppermute(block, "samp", [(i, (i + d) % count) for i in range(count)])


def shards(stiffness, columns, samples):
    blocks_here, slots, width, _ = stiffness.shape
    own, row_count = samples.shape
    parts = lax.axis_size("samp")
    total = own * parts
    reach = HB * width
    leaf = lax.axis_index("leaf")
    place = jnp.stack([leaf, lax.axis_index("samp")]).astype(jnp.int32)
    steps = blocks_here // ROWS_A_STEP
    step_lanes = ROWS_A_STEP * width
    shape = jax.ShapeDtypeStruct
    columns = columns.T

    far_end = row_count - reach
    even = leaf % 2 == 0
    first = lax.dynamic_slice_in_dim(samples, jnp.where(even, far_end, 0), reach, 1)
    second = lax.dynamic_slice_in_dim(samples, jnp.where(even, 0, far_end), reach, 1)
    halo = jnp.concatenate([swap_across(first, 0), swap_across(second, 1)], axis=1)
    other_halos = [sample_shift(halo, d) for d in range(1, parts)]

    block_spec = pl.BlockSpec((ROWS_A_STEP, slots, width, width), lambda i, *_: (i, 0, 0, 0))
    own_spec = pl.BlockSpec((own, step_lanes), lambda i, *_: (0, i))
    all_spec = pl.BlockSpec((total, step_lanes), lambda i, *_: (0, i))

    def fixed(*dims):
        return pl.BlockSpec(dims, lambda i, *_: (0,) * len(dims))

    products, own_high, own_low = pl.pallas_call(
        own_kernel,
        grid_spec=pltpu.PrefetchScalarGridSpec(
            num_scalar_prefetch=2,
            grid=(steps,),
            in_specs=[block_spec, fixed(own, row_count), fixed(own, 2 * reach)],
            out_specs=[own_spec] * 3,
            scratch_shapes=[pltpu.VMEM((own, row_count + width), BF16), pltpu.VMEM((own, 2 * reach + width), BF16)],
        ),
        out_shape=[shape((own, row_count), F32), shape((own, row_count), BF16), shape((own, row_count), BF16)],
        compiler_params=params(),
        cost_estimate=pl.CostEstimate(
            flops=4 * own * slots * width * row_count, bytes_accessed=7 * 1024 * 1024, transcendentals=0
        ),
        name="own",
    )(place, columns, stiffness, samples, halo)

    packed_shape = (total + GROUP, total // 2)
    z_high, z_low, packed = pl.pallas_call(
        functools.partial(others_kernel, parts),
        grid_spec=pltpu.PrefetchScalarGridSpec(
            num_scalar_prefetch=2,
            grid=(steps,),
            in_specs=[block_spec] + [fixed(own, 2 * reach)] * (parts - 1) + [own_spec] * 2,
            out_specs=[all_spec, all_spec, fixed(*packed_shape)],
            scratch_shapes=[
                pltpu.VMEM((total - own, 2 * reach + width), BF16),
                pltpu.VMEM((total, total), F32),
                pltpu.VMEM((total, total), F32),
            ],
        ),
        out_shape=[shape((total, row_count), BF16), shape((total, row_count), BF16), shape(packed_shape, F32)],
        compiler_params=params(),
        name="others",
    )(place, columns, stiffness, *other_halos, own_high, own_low)

    smem = pl.BlockSpec(memory_space=pltpu.SMEM)
    square = shape((2, total, total), F32)
    transfer_shape = shape((total, own), F32)
    gram_one = packed + from_partner(packed, "leaf", 0)
    gram_two = gram_one + from_partner(gram_one, "leaf", 1)
    a, m = pl.pallas_call(
        first_kernel,
        in_specs=[whole()] * 2,
        out_specs=[whole()] * 2,
        out_shape=[square] * 2,
        compiler_params=params(),
        cost_estimate=pl.CostEstimate(flops=3 * 10**9, bytes_accessed=1024 * 1024, transcendentals=0),
        name="first",
    )(packed, gram_one)
    gram_three = gram_two + from_partner(gram_two, "leaf", 2)
    bases, transfer_one, upper_own, _, _ = pl.pallas_call(
        functools.partial(second_kernel, math.sqrt(row_count)),
        in_specs=[smem] + [whole()] * 4,
        out_specs=[whole()] * 5,
        out_shape=[shape((own, row_count), F32), transfer_shape, shape((own, total), F32), square, square],
        input_output_aliases={1: 3, 2: 4},
        compiler_params=params(),
        cost_estimate=pl.CostEstimate(flops=3 * 10**9, bytes_accessed=1024 * 1024, transcendentals=0),
        name="second",
    )(place, a, m, z_high, z_low)
    transfer_two, transfer_three, top_factor = pl.pallas_call(
        functools.partial(tree_kernel, 1.0 / math.sqrt(2**LEVELS * row_count)),
        in_specs=[smem] + [whole()] * 3,
        out_specs=[whole()] * 3,
        out_shape=[transfer_shape] * 3,
        scratch_shapes=[pltpu.VMEM((2, total, total), F32)] * 2,
        compiler_params=params(),
        name="tree",
    )(place, upper_own, gram_two, gram_three)
    return (products, bases, transfer_one, transfer_two, transfer_three, top_factor)


def solution(mesh):
    return jax.shard_map(
        shards,
        mesh=mesh,
        in_specs=(P("leaf", None, None, None), P("leaf", None), P("samp", "leaf")),
        out_specs=(
            P("samp", "leaf"),
            P("samp", "leaf"),
            P("leaf", "samp"),
            P("leaf", "samp"),
            P("leaf", "samp"),
            P("leaf", "samp"),
        ),
        check_vma=False,
    )
```

```python
import functools
import math

import jax
import jax.numpy as jnp
from jax import lax
from jax.experimental import pallas as pl
from jax.experimental.pallas import tpu as pltpu
from jax.sharding import PartitionSpec as P

HB = 4
LEVELS = 3
LANES = 128
GROUP = 8
PANEL = 32
ROWS_A_STEP = 4
VMEM_LIMIT = 48 * 1024 * 1024
VMEM_NEARLY_ALL = 61 * 1024 * 1024
F32 = jnp.float32
BF16 = jnp.bfloat16
NN = (((1,), (0,)), ((), ()))
NT = (((1,), (1,)), ((), ()))
TN = (((0,), (0,)), ((), ()))


def dot(a, b, dims):
    return lax.dot_general(a, b, dims, preferred_element_type=F32)


def split_two(x):
    high = x.astype(BF16)
    return high, (x - high.astype(F32)).astype(BF16)


def split_three(x):
    high = x.astype(BF16)
    rest = x - high.astype(F32)
    middle = rest.astype(BF16)
    return high, middle, (rest - middle.astype(F32)).astype(BF16)


def dot_split(a, b, dims):
    (a_high, a_low), (b_high, b_low) = a, b
    return dot(a_high, b_high, dims) + (dot(a_high, b_low, dims) + dot(a_low, b_high, dims))


def taken(window, chosen, slots, width):
    lanes = [pl.ds(pl.multiple_of(chosen(k) * width, LANES), width) for k in range(slots)]
    return jnp.concatenate([window[:, at] for at in lanes], axis=1)


def block_row(blocks, rr):
    return jnp.concatenate([blocks[rr, k] for k in range(blocks.shape[1])], axis=1)


def far_position(local, count, odd):
    lower = jnp.where(odd, 0, HB)
    below = jnp.clip(local + HB, 0, HB - 1) + lower
    above = jnp.clip(local - count, 0, HB - 1) + (HB - lower)
    return jnp.where(local < 0, below, jnp.where(local < count, 2 * HB, above))


def local_column(place, columns, blocks, rr, k):
    rows_step = blocks.shape[0]
    steps = pl.num_programs(0)
    return columns[k, pl.program_id(0) * rows_step + rr] - place[0] * (rows_step * steps)


def near_kernel(place, columns, blocks, samples, near, window):
    rows_step, slots, width, _ = blocks.shape
    count = rows_step * pl.num_programs(0)

    @pl.when(pl.program_id(0) == 0)
    def _():
        window[:, : samples.shape[1]] = samples[...]
        window[:, samples.shape[1] :] = jnp.zeros((samples.shape[0], width), BF16)

    for rr in range(rows_step):

        def chosen(k):
            local = local_column(place, columns, blocks, rr, k)
            return jnp.where((local >= 0) & (local < count), local, count)

        lanes = slice(rr * width, (rr + 1) * width)
        near[:, lanes] = dot(taken(window, chosen, slots, width), block_row(blocks, rr), NT)


def fill_window(window, halos):
    own, reach = halos[0].shape
    for at in range(0, len(halos), 2):
        rows = slice(at // 2 * own, (at // 2 + 1) * own)
        window[rows, :reach] = halos[at][...]
        window[rows, reach : 2 * reach] = halos[at + 1][...]
    window[:, 2 * reach :] = jnp.zeros((window.shape[0], window.shape[1] - 2 * reach), BF16)


def far_row(place, columns, blocks, window, rr):
    rows_step, slots, width, _ = blocks.shape
    count = rows_step * pl.num_programs(0)
    odd = lax.rem(place[0], 2) == 1

    def chosen(k):
        return far_position(local_column(place, columns, blocks, rr, k), count, odd)

    return dot(taken(window, chosen, slots, width), block_row(blocks, rr), NT)


def own_kernel(place, columns, blocks, first, second, near, products, z_high, z_low, gram, window):
    rows_step, _, width, _ = blocks.shape
    step = pl.program_id(0)

    @pl.when(step == 0)
    def _():
        fill_window(window, (first, second))
        gram[...] = jnp.zeros_like(gram)

    for rr in range(rows_step):
        remote = far_row(place, columns, blocks, window, rr)
        lanes = slice(rr * width, (rr + 1) * width)
        products[:, lanes] = near[:, lanes] + remote
        z_high[:, lanes], z_low[:, lanes] = split_two(remote)
    halves = z_high[...], z_low[...]
    gram[...] += dot_split(halves, halves, NT)


def others_kernel(parts, place, columns, blocks, *refs):
    halos = refs[: 2 * (parts - 1)]
    own_high, own_low, own_gram, z_high, z_low, packed, window, gram_rows, full = refs[2 * (parts - 1) :]
    rows_step, _, width, _ = blocks.shape
    step = pl.program_id(0)
    own = own_high.shape[0]

    @pl.when(step == 0)
    def _():
        fill_window(window, halos)
        gram_rows[...] = jnp.zeros_like(gram_rows)

    for rr in range(rows_step):
        lanes = slice(rr * width, (rr + 1) * width)
        z_high[:, lanes], z_low[:, lanes] = split_two(far_row(place, columns, blocks, window, rr))
    high, low = z_high[...], z_low[...]
    all_high = jnp.concatenate([own_high[...], high], axis=0)
    all_low = jnp.concatenate([own_low[...], low], axis=0)
    gram_rows[...] += dot_split((high, low), (all_high, all_low), NT)

    @pl.when(step == pl.num_programs(0) - 1)
    def _():
        full[:own, :own] = own_gram[...]
        full[own:, :] = gram_rows[...]
        full[:own, own:] = gram_rows[:, :own].T
        shift = place[1] * own
        pack_symmetric(packed, pltpu.roll(pltpu.roll(full[...], shift, 0), shift, 1))


def square_iota(n):
    return lax.broadcasted_iota(jnp.int32, (n, n), 0), lax.broadcasted_iota(jnp.int32, (n, n), 1)


def pack_symmetric(packed, full):
    h = full.shape[0] // 2
    row, col = square_iota(h)
    first = full[:h, :h]
    packed[:h, :] = full[:h, h:]
    packed[h : 2 * h, :] = jnp.where(row > col, first, full[h:, h:])
    diagonal = jnp.sum(jnp.where(row == col, first, 0.0), axis=0, keepdims=True)
    packed[2 * h :, :] = jnp.broadcast_to(diagonal, (GROUP, h))


def unpack_symmetric(packed, full, b):
    h = packed.shape[1]
    row, col = square_iota(h)
    shared = packed[h : 2 * h, :]
    lower = jnp.where(row > col, shared, 0.0)
    diagonal = jnp.where(row == col, jnp.broadcast_to(packed[2 * h : 2 * h + 1, :], (h, h)), 0.0)
    upper = jnp.where(row <= col, shared, 0.0)
    full[b, :h, :h] = lower + lower.T + diagonal
    full[b, h:, h:] = upper + jnp.where(row < col, upper, 0.0).T
    full[b, :h, h:] = packed[:h, :]


def row_of(x, j):
    return jnp.broadcast_to(x[:, j : j + 1, :], x.shape)


def start_inverse(m):
    batch, n, _ = m.shape
    row, col = square_iota(LANES)
    for b in range(batch):
        for c in range(0, n, LANES):
            for e in range(0, n, LANES):
                m[b, c : c + LANES, e : e + LANES] = (
                    (row == col).astype(F32) if e == c else jnp.zeros((LANES, LANES), F32)
                )


def clear_lower(a):
    batch, n, _ = a.shape
    for b in range(batch):
        for c in range(LANES, n, LANES):
            a[b, c : c + LANES, :c] = jnp.zeros((LANES, c), F32)


def factor(a, m, first, last):
    batch, n, _ = a.shape
    chunks = n // LANES
    groups = PANEL // GROUP
    tile = (batch, GROUP, LANES)
    sub = lax.broadcasted_iota(jnp.int32, tile, 1)
    lane = lax.broadcasted_iota(jnp.int32, tile, 2)
    for p in range(first, last, PANEL):
        ch = p // LANES
        parts = [(a, c) for c in range(ch, chunks)] + [(m, c) for c in range(ch + 1)]
        rows = [slice(p + GROUP * g, p + GROUP * (g + 1)) for g in range(groups)]
        r = [[ref[:, rows[g], c * LANES : (c + 1) * LANES] for ref, c in parts] for g in range(groups)]
        for g0 in range(groups):
            at = p - ch * LANES + GROUP * g0
            v = [
                [jnp.broadcast_to(r[g][0][:, :, at + k : at + k + 1], tile) for k in range(GROUP)]
                if g >= g0
                else None
                for g in range(groups)
            ]
            head, top = v[g0], r[g0]
            recips, v_rows, r_rows = [], [], []
            pivots = None
            for j in range(GROUP):
                d = row_of(head[j], j)
                rc = invert(d)
                recips.append(rc)
                pivots = d if pivots is None else jnp.where(sub == j, d, pivots)
                v_rows.append([row_of(head[k], j) if k > j else None for k in range(GROUP)])
                r_rows.append([row_of(x, j) for x in top])
                if j < GROUP - 1:
                    below = jnp.where(sub > j, head[j], 0.0)
                    scaled = below * rc
                    for k in range(j + 1, GROUP):
                        if k == j + 1:
                            head[k] = head[k] - (below * v_rows[j][k]) * rc
                        else:
                            head[k] = head[k] - scaled * v_rows[j][k]
                    for x in range(len(top)):
                        top[x] = top[x] - scaled * r_rows[j][x]
            for g in range(g0 + 1, groups):
                for j in range(GROUP):
                    scaled = v[g][j] * recips[j]
                    for k in range(j + 1, GROUP):
                        v[g][k] = v[g][k] - scaled * v_rows[j][k]
                    for x in range(len(top)):
                        r[g][x] = r[g][x] - scaled * r_rows[j][x]
            scale = lax.rsqrt(pivots)
            for x, (ref, c) in enumerate(parts):
                done = top[x] * scale
                if ref is a and c == ch:
                    done = jnp.where(lane >= sub + at, done, 0.0)
                r[g0][x] = done
                ref[:, rows[g0], c * LANES : (c + 1) * LANES] = done
        if p + PANEL == n:
            break
        for b in range(batch):
            panel = jnp.concatenate(
                [jnp.concatenate([r[g][x][b] for g in range(groups)], axis=0) for x in range(len(parts))], axis=1
            )
            h, mid, low = split_three(panel)
            left = jnp.concatenate([h, h, mid, mid, h, low], axis=0)
            right = jnp.concatenate([h, mid, h, mid, low, h], axis=0)
            for c in range(ch, chunks):
                start = max(p + PANEL, c * LANES)
                stop = (c + 1) * LANES
                if start >= stop:
                    continue
                x0 = c - ch
                update = dot(left[:, x0 * LANES : (x0 + 1) * LANES], right, TN)[start - c * LANES :, :]
                for x, (ref, e) in enumerate(parts):
                    if ref is a and e < c:
                        continue
                    lanes = slice(e * LANES, (e + 1) * LANES)
                    ref[b, start:stop, lanes] = ref[b, start:stop, lanes] - update[:, x * LANES : (x + 1) * LANES]


def invert(x):
    guess = pl.reciprocal(x, approx=True)
    return guess * (2.0 - x * guess)


def own_rows(place, own):
    return pl.ds(pl.multiple_of(place[1] * own, own), own)


def first_kernel(packed_zero, packed_one, a, m):
    unpack_symmetric(packed_zero, a, 0)
    unpack_symmetric(packed_one, a, 1)
    start_inverse(m)
    factor(a, m, 0, a.shape[1] // 2)


def second_kernel(scale, place, a_in, m_in, own_high, own_low, rest_high, rest_low, bases, transfer, upper_own, a, m):
    del a_in, m_in
    n = a.shape[1]
    factor(a, m, n // 2, n)
    clear_lower(a)
    own = upper_own.shape[0]
    rows = own_rows(place, own)
    upper_own[...] = a[1, rows, :]
    transfer[...] = dot_split(split_two(m[1]), split_two(a[0, rows, :]), NT)
    turned = pltpu.roll(m[0, rows, :] * scale, lax.rem(n - place[1] * own, n), 1)
    inverse = split_two(turned)
    for c in range(0, own_high.shape[1], 512):
        lanes = slice(c, c + 512)
        high = jnp.concatenate([own_high[:, lanes], rest_high[:, lanes]], axis=0)
        low = jnp.concatenate([own_low[:, lanes], rest_low[:, lanes]], axis=0)
        bases[:, lanes] = dot_split(inverse, (high, low), NN)


def tree_kernel(top_scale, place, upper_own, *refs):
    levels = (len(refs) - 3) // 2
    packed = refs[:levels]
    transfers = refs[levels : 2 * levels]
    top, a, m = refs[2 * levels :]
    for b in range(levels):
        unpack_symmetric(packed[b], a, b)
    start_inverse(m)
    factor(a, m, 0, a.shape[1])
    clear_lower(a)
    own = upper_own.shape[0]
    rows = own_rows(place, own)
    for b in range(levels):
        child = upper_own[...] if b == 0 else a[b - 1, rows, :]
        transfers[b][...] = dot_split(split_two(m[b]), split_two(child), NT)
    top[...] = (a[levels - 1, rows, :] * top_scale).T


def whole():
    return pl.BlockSpec(memory_space=pltpu.VMEM)


def params(limit=VMEM_LIMIT):
    return pltpu.CompilerParams(vmem_limit_bytes=limit)


def from_partner(block, axis, bit):
    count = lax.axis_size(axis)
    route = []
    for low in range(count):
        high = low | 1 << bit
        if high != low and high < count:
            route += [(low, high), (high, low)]
    return lax.ppermute(block, axis, route)


def swap_across(block, odd_start):
    count = lax.axis_size("leaf")
    route = []
    for low in range(odd_start, count - 1, 2):
        route += [(low, low + 1), (low + 1, low)]
    return lax.ppermute(block, "leaf", route)


def sample_shift(block, d):
    count = lax.axis_size("samp")
    return lax.ppermute(block, "samp", [(i, (i - d) % count) for i in range(count)])


def shards(stiffness, columns, samples):
    blocks_here, slots, width, _ = stiffness.shape
    own, row_count = samples.shape
    parts = lax.axis_size("samp")
    total = own * parts
    reach = HB * width
    leaf = lax.axis_index("leaf")
    place = jnp.stack([leaf, lax.axis_index("samp")]).astype(jnp.int32)
    steps = blocks_here // ROWS_A_STEP
    step_lanes = ROWS_A_STEP * width
    shape = jax.ShapeDtypeStruct
    columns = columns.T

    far_end = row_count - reach
    even = leaf % 2 == 0
    first = lax.dynamic_slice_in_dim(samples, jnp.where(even, far_end, 0), reach, 1)
    second = lax.dynamic_slice_in_dim(samples, jnp.where(even, 0, far_end), reach, 1)
    halos = [swap_across(first, 0), swap_across(second, 1)]
    other_halos = [sample_shift(halo, d) for d in range(1, parts) for halo in halos]

    block_spec = pl.BlockSpec((ROWS_A_STEP, slots, width, width), lambda i, *_: (i, 0, 0, 0))
    own_spec = pl.BlockSpec((own, step_lanes), lambda i, *_: (0, i))
    rest = total - own
    rest_spec = pl.BlockSpec((rest, step_lanes), lambda i, *_: (0, i))
    product_cost = pl.CostEstimate(
        flops=2 * own * slots * width * row_count, bytes_accessed=6 * 1024 * 1024, transcendentals=0
    )

    def fixed(*dims):
        return pl.BlockSpec(dims, lambda i, *_: (0,) * len(dims))

    near = pl.pallas_call(
        near_kernel,
        grid_spec=pltpu.PrefetchScalarGridSpec(
            num_scalar_prefetch=2,
            grid=(steps,),
            in_specs=[block_spec, fixed(own, row_count)],
            out_specs=own_spec,
            scratch_shapes=[pltpu.VMEM((own, row_count + width), BF16)],
        ),
        out_shape=shape((own, row_count), F32),
        compiler_params=params(VMEM_NEARLY_ALL),
        cost_estimate=product_cost,
        name="near",
    )(place, columns, stiffness, samples)

    products, own_high, own_low, own_gram = pl.pallas_call(
        own_kernel,
        grid_spec=pltpu.PrefetchScalarGridSpec(
            num_scalar_prefetch=2,
            grid=(steps,),
            in_specs=[block_spec] + [fixed(own, reach)] * 2 + [own_spec],
            out_specs=[own_spec] * 3 + [fixed(own, own)],
            scratch_shapes=[pltpu.VMEM((own, 2 * reach + width), BF16)],
        ),
        out_shape=[
            shape((own, row_count), F32),
            shape((own, row_count), BF16),
            shape((own, row_count), BF16),
            shape((own, own), F32),
        ],
        compiler_params=params(),
        cost_estimate=product_cost,
        name="own",
    )(place, columns, stiffness, *halos, near)

    packed_shape = (total + GROUP, total // 2)
    rest_high, rest_low, packed = pl.pallas_call(
        functools.partial(others_kernel, parts),
        grid_spec=pltpu.PrefetchScalarGridSpec(
            num_scalar_prefetch=2,
            grid=(steps,),
            in_specs=[block_spec] + [fixed(own, reach)] * (2 * (parts - 1)) + [own_spec] * 2 + [fixed(own, own)],
            out_specs=[rest_spec, rest_spec, fixed(*packed_shape)],
            scratch_shapes=[
                pltpu.VMEM((rest, 2 * reach + width), BF16),
                pltpu.VMEM((rest, total), F32),
                pltpu.VMEM((total, total), F32),
            ],
        ),
        out_shape=[shape((rest, row_count), BF16), shape((rest, row_count), BF16), shape(packed_shape, F32)],
        compiler_params=params(),
        name="others",
    )(place, columns, stiffness, *other_halos, own_high, own_low, own_gram)

    smem = pl.BlockSpec(memory_space=pltpu.SMEM)
    square = shape((2, total, total), F32)
    transfer_shape = shape((total, own), F32)
    gram_one = packed + from_partner(packed, "leaf", 0)
    gram_two = gram_one + from_partner(gram_one, "leaf", 1)
    a, m = pl.pallas_call(
        first_kernel,
        in_specs=[whole()] * 2,
        out_specs=[whole()] * 2,
        out_shape=[square] * 2,
        compiler_params=params(),
        cost_estimate=pl.CostEstimate(flops=3 * 10**9, bytes_accessed=1024 * 1024, transcendentals=0),
        name="first",
    )(packed, gram_one)
    gram_three = gram_two + from_partner(gram_two, "leaf", 2)
    bases, transfer_one, upper_own, _, _ = pl.pallas_call(
        functools.partial(second_kernel, math.sqrt(row_count)),
        in_specs=[smem] + [whole()] * 6,
        out_specs=[whole()] * 5,
        out_shape=[shape((own, row_count), F32), transfer_shape, shape((own, total), F32), square, square],
        input_output_aliases={1: 3, 2: 4},
        compiler_params=params(),
        cost_estimate=pl.CostEstimate(flops=3 * 10**9, bytes_accessed=1024 * 1024, transcendentals=0),
        name="second",
    )(place, a, m, own_high, own_low, rest_high, rest_low)
    transfer_two, transfer_three, top_factor = pl.pallas_call(
        functools.partial(tree_kernel, 1.0 / math.sqrt(2**LEVELS * row_count)),
        in_specs=[smem] + [whole()] * 3,
        out_specs=[whole()] * 3,
        out_shape=[transfer_shape] * 3,
        scratch_shapes=[pltpu.VMEM((2, total, total), F32)] * 2,
        compiler_params=params(),
        name="tree",
    )(place, upper_own, gram_two, gram_three)
    return (products, bases, transfer_one, transfer_two, transfer_three, top_factor)


def solution(mesh):
    return jax.shard_map(
        shards,
        mesh=mesh,
        in_specs=(P("leaf", None, None, None), P("leaf", None), P("samp", "leaf")),
        out_specs=(
            P("samp", "leaf"),
            P("samp", "leaf"),
            P("leaf", "samp"),
            P("leaf", "samp"),
            P("leaf", "samp"),
            P("leaf", "samp"),
        ),
        check_vma=False,
    )
```

```python
import functools
import math

import jax
import jax.numpy as jnp
from jax import lax
from jax.experimental import pallas as pl
from jax.experimental.pallas import tpu as pltpu
from jax.sharding import PartitionSpec as P

HB = 4
LEVELS = 3
LANES = 128
GROUP = 8
PANEL = 32
ROWS_A_STEP = 4
VMEM_LIMIT = 20 * 1024 * 1024
VMEM_NEAR = 48 * 1024 * 1024
F32 = jnp.float32
BF16 = jnp.bfloat16
NN = (((1,), (0,)), ((), ()))
NT = (((1,), (1,)), ((), ()))
TN = (((0,), (0,)), ((), ()))


def dot(a, b, dims):
    return lax.dot_general(a, b, dims, preferred_element_type=F32)


def split_two(x):
    high = x.astype(BF16)
    return high, (x - high.astype(F32)).astype(BF16)


def split_three(x):
    high = x.astype(BF16)
    rest = x - high.astype(F32)
    middle = rest.astype(BF16)
    return high, middle, (rest - middle.astype(F32)).astype(BF16)


def dot_split(a, b, dims):
    (a_high, a_low), (b_high, b_low) = a, b
    return dot(a_high, b_high, dims) + (dot(a_high, b_low, dims) + dot(a_low, b_high, dims))


def far_position(local, count, odd):
    lower = jnp.where(odd, 0, HB)
    below = jnp.clip(local + HB, 0, HB - 1) + lower
    above = jnp.clip(local - count, 0, HB - 1) + (HB - lower)
    return jnp.where(local < 0, below, jnp.where(local < count, 2 * HB, above))


def block_rows(place, columns, blocks, window, position, emit, before=None):
    count, slots, width, _ = blocks.shape

    def body(step, carry):
        if before is not None:
            before(step)
        for rr in range(ROWS_A_STEP):
            row = step * ROWS_A_STEP + rr
            picked = []
            for k in range(slots):
                at = position(columns[k, row] - place[0] * count) * width
                picked.append(window[:, pl.ds(pl.multiple_of(at, LANES), width)])
            stored = jnp.concatenate([blocks[row, k] for k in range(slots)], axis=1)
            product = dot(jnp.concatenate(picked, axis=1), stored, NT)
            emit(pl.ds(pl.multiple_of(row * width, LANES), width), product)
        return carry

    lax.fori_loop(0, count // ROWS_A_STEP, body, 0)


def near_kernel(place, columns, blocks_hbm, samples, near, blocks, window, arrived):
    count, _, width, _ = blocks.shape

    def chunk(step):
        rows = pl.ds(step * ROWS_A_STEP, ROWS_A_STEP)
        return pltpu.make_async_copy(blocks_hbm.at[rows], blocks.at[rows], arrived.at[step])

    for step in range(count // ROWS_A_STEP):
        chunk(step).start()
    window[:, : samples.shape[1]] = samples[...]
    window[:, samples.shape[1] :] = jnp.zeros((samples.shape[0], width), BF16)

    def position(local):
        return jnp.where((local >= 0) & (local < count), local, count)

    def emit(lanes, product):
        near[:, lanes] = product

    block_rows(place, columns, blocks, window, position, emit, lambda step: chunk(step).wait())


def fill_window(window, halos):
    own, lanes = halos[0].shape
    for at, halo in enumerate(halos):
        window[at * own : (at + 1) * own, :lanes] = halo[...]
    window[:, lanes:] = jnp.zeros((window.shape[0], window.shape[1] - lanes), BF16)


def far_rows(place, columns, blocks, window, emit):
    odd = lax.rem(place[0], 2) == 1
    count = blocks.shape[0]
    block_rows(place, columns, blocks, window, lambda local: far_position(local, count, odd), emit)


def own_kernel(place, columns, blocks, halo, near, products, z_high, z_low, gram, window):
    fill_window(window, (halo,))

    def emit(lanes, remote):
        products[:, lanes] = near[:, lanes] + remote
        z_high[:, lanes], z_low[:, lanes] = split_two(remote)

    far_rows(place, columns, blocks, window, emit)
    halves = z_high[...], z_low[...]
    gram[...] = dot_split(halves, halves, NT)


def others_kernel(parts, place, columns, blocks, *refs):
    halos = refs[: parts - 1]
    own_high, own_low, own_gram, z_high, z_low, packed, window, full = refs[parts - 1 :]
    own = own_high.shape[0]
    fill_window(window, halos)

    def emit(lanes, remote):
        z_high[:, lanes], z_low[:, lanes] = split_two(remote)

    far_rows(place, columns, blocks, window, emit)
    high, low = z_high[...], z_low[...]
    all_high = jnp.concatenate([own_high[...], high], axis=0)
    all_low = jnp.concatenate([own_low[...], low], axis=0)
    gram_rows = dot_split((high, low), (all_high, all_low), NT)
    full[:own, :own] = own_gram[...]
    full[own:, :] = gram_rows
    full[:own, own:] = gram_rows[:, :own].T
    shift = place[1] * own
    pack_symmetric(packed, pltpu.roll(pltpu.roll(full[...], shift, 0), shift, 1))


def square_iota(n):
    return lax.broadcasted_iota(jnp.int32, (n, n), 0), lax.broadcasted_iota(jnp.int32, (n, n), 1)


def pack_symmetric(packed, full):
    h = full.shape[0] // 2
    row, col = square_iota(h)
    first = full[:h, :h]
    packed[:h, :] = full[:h, h:]
    packed[h : 2 * h, :] = jnp.where(row > col, first, full[h:, h:])
    diagonal = jnp.sum(jnp.where(row == col, first, 0.0), axis=0, keepdims=True)
    packed[2 * h :, :] = jnp.broadcast_to(diagonal, (GROUP, h))


def unpack_symmetric(packed, full, b):
    h = packed.shape[1]
    row, col = square_iota(h)
    shared = packed[h : 2 * h, :]
    lower = jnp.where(row > col, shared, 0.0)
    diagonal = jnp.where(row == col, jnp.broadcast_to(packed[2 * h : 2 * h + 1, :], (h, h)), 0.0)
    upper = jnp.where(row <= col, shared, 0.0)
    full[b, :h, :h] = lower + lower.T + diagonal
    full[b, h:, h:] = upper + jnp.where(row < col, upper, 0.0).T
    full[b, :h, h:] = packed[:h, :]


def row_of(x, j):
    return jnp.broadcast_to(x[:, j : j + 1, :], x.shape)


def start_inverse(m):
    batch, n, _ = m.shape
    row, col = square_iota(LANES)
    for b in range(batch):
        for c in range(0, n, LANES):
            for e in range(0, n, LANES):
                m[b, c : c + LANES, e : e + LANES] = (
                    (row == col).astype(F32) if e == c else jnp.zeros((LANES, LANES), F32)
                )


def clear_lower(a):
    batch, n, _ = a.shape
    for b in range(batch):
        for c in range(LANES, n, LANES):
            a[b, c : c + LANES, :c] = jnp.zeros((LANES, c), F32)


def factor(a, m, first, last):
    batch, n, _ = a.shape
    chunks = n // LANES
    groups = PANEL // GROUP
    tile = (batch, GROUP, LANES)
    sub = lax.broadcasted_iota(jnp.int32, tile, 1)
    lane = lax.broadcasted_iota(jnp.int32, tile, 2)
    for p in range(first, last, PANEL):
        ch = p // LANES
        parts = [(a, c) for c in range(ch, chunks)] + [(m, c) for c in range(ch + 1)]
        rows = [slice(p + GROUP * g, p + GROUP * (g + 1)) for g in range(groups)]
        r = [[ref[:, rows[g], c * LANES : (c + 1) * LANES] for ref, c in parts] for g in range(groups)]
        for g0 in range(groups):
            at = p - ch * LANES + GROUP * g0
            v = [
                [jnp.broadcast_to(r[g][0][:, :, at + k : at + k + 1], tile) for k in range(GROUP)]
                if g >= g0
                else None
                for g in range(groups)
            ]
            head, top = v[g0], r[g0]
            recips, v_rows, r_rows = [], [], []
            pivots = None
            for j in range(GROUP):
                d = row_of(head[j], j)
                rc = invert(d)
                recips.append(rc)
                pivots = d if pivots is None else jnp.where(sub == j, d, pivots)
                v_rows.append([row_of(head[k], j) if k > j else None for k in range(GROUP)])
                r_rows.append([row_of(x, j) for x in top])
                if j < GROUP - 1:
                    below = jnp.where(sub > j, head[j], 0.0)
                    scaled = below * rc
                    for k in range(j + 1, GROUP):
                        if k == j + 1:
                            head[k] = head[k] - (below * v_rows[j][k]) * rc
                        else:
                            head[k] = head[k] - scaled * v_rows[j][k]
                    for x in range(len(top)):
                        top[x] = top[x] - scaled * r_rows[j][x]
            for g in range(g0 + 1, groups):
                for j in range(GROUP):
                    scaled = v[g][j] * recips[j]
                    for k in range(j + 1, GROUP):
                        v[g][k] = v[g][k] - scaled * v_rows[j][k]
                    for x in range(len(top)):
                        r[g][x] = r[g][x] - scaled * r_rows[j][x]
            scale = lax.rsqrt(pivots)
            for x, (ref, c) in enumerate(parts):
                done = top[x] * scale
                if ref is a and c == ch:
                    done = jnp.where(lane >= sub + at, done, 0.0)
                r[g0][x] = done
                ref[:, rows[g0], c * LANES : (c + 1) * LANES] = done
        if p + PANEL == n:
            break
        for b in range(batch):
            panel = jnp.concatenate(
                [jnp.concatenate([r[g][x][b] for g in range(groups)], axis=0) for x in range(len(parts))], axis=1
            )
            h, mid, low = split_three(panel)
            left = jnp.concatenate([h, h, mid, mid, h, low], axis=0)
            right = jnp.concatenate([h, mid, h, mid, low, h], axis=0)
            for c in range(ch, chunks):
                start = max(p + PANEL, c * LANES)
                stop = (c + 1) * LANES
                if start >= stop:
                    continue
                x0 = c - ch
                update = dot(left[:, x0 * LANES : (x0 + 1) * LANES], right, TN)[start - c * LANES :, :]
                for x, (ref, e) in enumerate(parts):
                    if ref is a and e < c:
                        continue
                    lanes = slice(e * LANES, (e + 1) * LANES)
                    ref[b, start:stop, lanes] = ref[b, start:stop, lanes] - update[:, x * LANES : (x + 1) * LANES]


def invert(x):
    guess = pl.reciprocal(x, approx=True)
    return guess * (2.0 - x * guess)


def own_rows(place, own):
    return pl.ds(pl.multiple_of(place[1] * own, own), own)


def first_kernel(packed_zero, packed_one, a, m):
    unpack_symmetric(packed_zero, a, 0)
    unpack_symmetric(packed_one, a, 1)
    start_inverse(m)
    factor(a, m, 0, a.shape[1] // 2)


def second_kernel(scale, place, a_in, m_in, own_high, own_low, rest_high, rest_low, bases, transfer, upper_own, a, m):
    del a_in, m_in
    n = a.shape[1]
    factor(a, m, n // 2, n)
    clear_lower(a)
    own = upper_own.shape[0]
    rows = own_rows(place, own)
    upper_own[...] = a[1, rows, :]
    transfer[...] = dot_split(split_two(m[1]), split_two(a[0, rows, :]), NT)
    turned = pltpu.roll(m[0, rows, :] * scale, lax.rem(n - place[1] * own, n), 1)
    inverse = split_two(turned)
    for c in range(0, own_high.shape[1], 512):
        lanes = slice(c, c + 512)
        high = jnp.concatenate([own_high[:, lanes], rest_high[:, lanes]], axis=0)
        low = jnp.concatenate([own_low[:, lanes], rest_low[:, lanes]], axis=0)
        bases[:, lanes] = dot_split(inverse, (high, low), NN)


def tree_kernel(top_scale, place, upper_own, *refs):
    levels = (len(refs) - 3) // 2
    packed = refs[:levels]
    transfers = refs[levels : 2 * levels]
    top, a, m = refs[2 * levels :]
    for b in range(levels):
        unpack_symmetric(packed[b], a, b)
    start_inverse(m)
    factor(a, m, 0, a.shape[1])
    clear_lower(a)
    own = upper_own.shape[0]
    rows = own_rows(place, own)
    for b in range(levels):
        child = upper_own[...] if b == 0 else a[b - 1, rows, :]
        transfers[b][...] = dot_split(split_two(m[b]), split_two(child), NT)
    top[...] = (a[levels - 1, rows, :] * top_scale).T


def whole():
    return pl.BlockSpec(memory_space=pltpu.VMEM)


def params(limit=VMEM_LIMIT):
    return pltpu.CompilerParams(vmem_limit_bytes=limit)


def from_partner(block, axis, bit):
    count = lax.axis_size(axis)
    route = []
    for low in range(count):
        high = low | 1 << bit
        if high != low and high < count:
            route += [(low, high), (high, low)]
    return lax.ppermute(block, axis, route)


def swap_across(block, odd_start):
    count = lax.axis_size("leaf")
    route = []
    for low in range(odd_start, count - 1, 2):
        route += [(low, low + 1), (low + 1, low)]
    return lax.ppermute(block, "leaf", route)


def sample_shift(block, d):
    count = lax.axis_size("samp")
    return lax.ppermute(block, "samp", [(i, (i - d) % count) for i in range(count)])


def shards(stiffness, columns, samples):
    blocks_here, slots, width, _ = stiffness.shape
    own, row_count = samples.shape
    parts = lax.axis_size("samp")
    total = own * parts
    reach = HB * width
    leaf = lax.axis_index("leaf")
    place = jnp.stack([leaf, lax.axis_index("samp")]).astype(jnp.int32)
    shape = jax.ShapeDtypeStruct
    columns = columns.T

    far_end = row_count - reach
    even = leaf % 2 == 0
    first = lax.dynamic_slice_in_dim(samples, jnp.where(even, far_end, 0), reach, 1)
    second = lax.dynamic_slice_in_dim(samples, jnp.where(even, 0, far_end), reach, 1)
    smem = pl.BlockSpec(memory_space=pltpu.SMEM)
    rest = total - own
    window_lanes = 2 * reach + width
    product_cost = pl.CostEstimate(
        flops=2 * own * slots * width * row_count, bytes_accessed=6 * 1024 * 1024, transcendentals=0
    )

    near, blocks = pl.pallas_call(
        near_kernel,
        in_specs=[smem, smem, pl.BlockSpec(memory_space=pltpu.HBM), whole()],
        out_specs=[whole()] * 2,
        out_shape=[shape((own, row_count), F32), shape(stiffness.shape, BF16)],
        scratch_shapes=[
            pltpu.VMEM((own, row_count + width), BF16),
            pltpu.SemaphoreType.DMA((blocks_here // ROWS_A_STEP,)),
        ],
        compiler_params=params(VMEM_NEAR),
        cost_estimate=product_cost,
        name="near",
    )(place, columns, stiffness, samples)

    second_halo, near = lax.optimization_barrier((swap_across(second, 1), near))
    halo = jnp.concatenate([swap_across(first, 0), second_halo], axis=1)
    other_halos = [sample_shift(halo, d) for d in range(1, parts)]

    products, own_high, own_low, own_gram = pl.pallas_call(
        own_kernel,
        in_specs=[smem, smem] + [whole()] * 3,
        out_specs=[whole()] * 4,
        out_shape=[
            shape((own, row_count), F32),
            shape((own, row_count), BF16),
            shape((own, row_count), BF16),
            shape((own, own), F32),
        ],
        scratch_shapes=[pltpu.VMEM((own, window_lanes), BF16)],
        compiler_params=params(),
        cost_estimate=product_cost,
        name="own",
    )(place, columns, blocks, halo, near)

    packed_shape = (total + GROUP, total // 2)
    rest_high, rest_low, packed = pl.pallas_call(
        functools.partial(others_kernel, parts),
        in_specs=[smem, smem] + [whole()] * (parts + 3),
        out_specs=[whole()] * 3,
        out_shape=[shape((rest, row_count), BF16), shape((rest, row_count), BF16), shape(packed_shape, F32)],
        scratch_shapes=[pltpu.VMEM((rest, window_lanes), BF16), pltpu.VMEM((total, total), F32)],
        compiler_params=params(),
        name="others",
    )(place, columns, blocks, *other_halos, own_high, own_low, own_gram)

    square = shape((2, total, total), F32)
    transfer_shape = shape((total, own), F32)
    gram_one = packed + from_partner(packed, "leaf", 0)
    gram_two = gram_one + from_partner(gram_one, "leaf", 1)
    a, m = pl.pallas_call(
        first_kernel,
        in_specs=[whole()] * 2,
        out_specs=[whole()] * 2,
        out_shape=[square] * 2,
        compiler_params=params(),
        cost_estimate=pl.CostEstimate(flops=3 * 10**9, bytes_accessed=1024 * 1024, transcendentals=0),
        name="first",
    )(packed, gram_one)
    gram_three = gram_two + from_partner(gram_two, "leaf", 2)
    bases, transfer_one, upper_own, _, _ = pl.pallas_call(
        functools.partial(second_kernel, math.sqrt(row_count)),
        in_specs=[smem] + [whole()] * 6,
        out_specs=[whole()] * 5,
        out_shape=[shape((own, row_count), F32), transfer_shape, shape((own, total), F32), square, square],
        input_output_aliases={1: 3, 2: 4},
        compiler_params=params(),
        cost_estimate=pl.CostEstimate(flops=3 * 10**9, bytes_accessed=1024 * 1024, transcendentals=0),
        name="second",
    )(place, a, m, own_high, own_low, rest_high, rest_low)
    transfer_two, transfer_three, top_factor = pl.pallas_call(
        functools.partial(tree_kernel, 1.0 / math.sqrt(2**LEVELS * row_count)),
        in_specs=[smem] + [whole()] * 3,
        out_specs=[whole()] * 3,
        out_shape=[transfer_shape] * 3,
        scratch_shapes=[pltpu.VMEM((2, total, total), F32)] * 2,
        compiler_params=params(),
        name="tree",
    )(place, upper_own, gram_two, gram_three)
    return (products, bases, transfer_one, transfer_two, transfer_three, top_factor)


def solution(mesh):
    return jax.shard_map(
        shards,
        mesh=mesh,
        in_specs=(P("leaf", None, None, None), P("leaf", None), P("samp", "leaf")),
        out_specs=(
            P("samp", "leaf"),
            P("samp", "leaf"),
            P("leaf", "samp"),
            P("leaf", "samp"),
            P("leaf", "samp"),
            P("leaf", "samp"),
        ),
        check_vma=False,
    )
```

```python
import functools
import math

import jax
import jax.numpy as jnp
from jax import lax
from jax.experimental import pallas as pl
from jax.experimental.pallas import tpu as pltpu
from jax.sharding import PartitionSpec as P

HB = 4
LEVELS = 3
LANES = 128
GROUP = 8
PANEL = 32
ROWS_A_STEP = 4
VMEM_LIMIT = 20 * 1024 * 1024
VMEM_NEAR = 48 * 1024 * 1024
F32 = jnp.float32
BF16 = jnp.bfloat16
NN = (((1,), (0,)), ((), ()))
NT = (((1,), (1,)), ((), ()))
TN = (((0,), (0,)), ((), ()))


def dot(a, b, dims):
    return lax.dot_general(a, b, dims, preferred_element_type=F32)


def split_two(x):
    high = x.astype(BF16)
    return high, (x - high.astype(F32)).astype(BF16)


def split_three(x):
    high = x.astype(BF16)
    rest = x - high.astype(F32)
    middle = rest.astype(BF16)
    return high, middle, (rest - middle.astype(F32)).astype(BF16)


def dot_split(a, b, dims):
    (a_high, a_low), (b_high, b_low) = a, b
    return dot(a_high, b_high, dims) + (dot(a_high, b_low, dims) + dot(a_low, b_high, dims))


def far_position(local, count, odd):
    lower = jnp.where(odd, 0, HB)
    below = jnp.clip(local + HB, 0, HB - 1) + lower
    above = jnp.clip(local - count, 0, HB - 1) + (HB - lower)
    return jnp.where(local < 0, below, jnp.where(local < count, 2 * HB, above))


def block_rows(place, columns, blocks, window, position, emit, before=None):
    count, slots, width, _ = blocks.shape

    def body(step, carry):
        if before is not None:
            before(step)
        for rr in range(ROWS_A_STEP):
            row = step * ROWS_A_STEP + rr
            picked = []
            for k in range(slots):
                at = position(columns[k, row] - place[0] * count) * width
                picked.append(window[:, pl.ds(pl.multiple_of(at, LANES), width)])
            stored = jnp.concatenate([blocks[row, k] for k in range(slots)], axis=1)
            product = dot(jnp.concatenate(picked, axis=1), stored, NT)
            emit(pl.ds(pl.multiple_of(row * width, LANES), width), product)
        return carry

    lax.fori_loop(0, count // ROWS_A_STEP, body, 0)


def near_kernel(place, columns, blocks_hbm, samples, near, blocks, window, arrived):
    count, _, width, _ = blocks.shape

    def chunk(step):
        rows = pl.ds(step * ROWS_A_STEP, ROWS_A_STEP)
        return pltpu.make_async_copy(blocks_hbm.at[rows], blocks.at[rows], arrived.at[step])

    for step in range(count // ROWS_A_STEP):
        chunk(step).start()
    window[:, : samples.shape[1]] = samples[...]
    window[:, samples.shape[1] :] = jnp.zeros((samples.shape[0], width), BF16)

    def position(local):
        return jnp.where((local >= 0) & (local < count), local, count)

    def emit(lanes, product):
        near[:, lanes] = product

    block_rows(place, columns, blocks, window, position, emit, lambda step: chunk(step).wait())


def far_kernel(place, columns, blocks, first, second, near, products, z_high, z_low, packed, window, total_own, leaving):
    count, _, width, _ = blocks.shape
    own = near.shape[0]
    reach = first.shape[1]
    odd = lax.rem(place[0], 2) == 1
    window[:, :reach] = first[...]
    window[:, reach : 2 * reach] = second[...]
    window[:, 2 * reach :] = jnp.zeros((window.shape[0], width), BF16)

    def emit(lanes, remote):
        total_own[:, lanes] = near[:, lanes] + remote[:own]
        z_high[:, lanes], z_low[:, lanes] = split_two(remote)

    block_rows(place, columns, blocks, window, lambda local: far_position(local, count, odd), emit)
    leave = pltpu.make_async_copy(total_own, products, leaving)
    leave.start()
    halves = z_high[...], z_low[...]
    gram = dot_split(halves, halves, NT)
    shift = place[1] * own
    pack_symmetric(packed, pltpu.roll(pltpu.roll(gram, shift, 0), shift, 1))
    leave.wait()


def square_iota(n):
    return lax.broadcasted_iota(jnp.int32, (n, n), 0), lax.broadcasted_iota(jnp.int32, (n, n), 1)


def pack_symmetric(packed, full):
    h = full.shape[0] // 2
    row, col = square_iota(h)
    first = full[:h, :h]
    packed[:h, :] = full[:h, h:]
    packed[h : 2 * h, :] = jnp.where(row > col, first, full[h:, h:])
    diagonal = jnp.sum(jnp.where(row == col, first, 0.0), axis=0, keepdims=True)
    packed[2 * h :, :] = jnp.broadcast_to(diagonal, (GROUP, h))


def unpack_symmetric(packed, full, b):
    h = packed.shape[1]
    row, col = square_iota(h)
    shared = packed[h : 2 * h, :]
    lower = jnp.where(row > col, shared, 0.0)
    diagonal = jnp.where(row == col, jnp.broadcast_to(packed[2 * h : 2 * h + 1, :], (h, h)), 0.0)
    upper = jnp.where(row <= col, shared, 0.0)
    full[b, :h, :h] = lower + lower.T + diagonal
    full[b, h:, h:] = upper + jnp.where(row < col, upper, 0.0).T
    full[b, :h, h:] = packed[:h, :]


def row_of(x, j):
    return jnp.broadcast_to(x[:, j : j + 1, :], x.shape)


def start_inverse(m):
    batch, n, _ = m.shape
    row, col = square_iota(LANES)
    for b in range(batch):
        for c in range(0, n, LANES):
            for e in range(0, n, LANES):
                m[b, c : c + LANES, e : e + LANES] = (
                    (row == col).astype(F32) if e == c else jnp.zeros((LANES, LANES), F32)
                )


def clear_lower(a):
    batch, n, _ = a.shape
    for b in range(batch):
        for c in range(LANES, n, LANES):
            a[b, c : c + LANES, :c] = jnp.zeros((LANES, c), F32)


def factor(a, m, first, last):
    batch, n, _ = a.shape
    chunks = n // LANES
    groups = PANEL // GROUP
    tile = (batch, GROUP, LANES)
    sub = lax.broadcasted_iota(jnp.int32, tile, 1)
    lane = lax.broadcasted_iota(jnp.int32, tile, 2)
    for p in range(first, last, PANEL):
        ch = p // LANES
        parts = [(a, c) for c in range(ch, chunks)] + [(m, c) for c in range(ch + 1)]
        rows = [slice(p + GROUP * g, p + GROUP * (g + 1)) for g in range(groups)]
        r = [[ref[:, rows[g], c * LANES : (c + 1) * LANES] for ref, c in parts] for g in range(groups)]
        for g0 in range(groups):
            at = p - ch * LANES + GROUP * g0
            v = [
                [jnp.broadcast_to(r[g][0][:, :, at + k : at + k + 1], tile) for k in range(GROUP)]
                if g >= g0
                else None
                for g in range(groups)
            ]
            head, top = v[g0], r[g0]
            recips, v_rows, r_rows = [], [], []
            pivots = None
            for j in range(GROUP):
                d = row_of(head[j], j)
                rc = invert(d)
                recips.append(rc)
                pivots = d if pivots is None else jnp.where(sub == j, d, pivots)
                v_rows.append([row_of(head[k], j) if k > j else None for k in range(GROUP)])
                r_rows.append([row_of(x, j) for x in top])
                if j < GROUP - 1:
                    below = jnp.where(sub > j, head[j], 0.0)
                    scaled = below * rc
                    for k in range(j + 1, GROUP):
                        if k == j + 1:
                            head[k] = head[k] - (below * v_rows[j][k]) * rc
                        else:
                            head[k] = head[k] - scaled * v_rows[j][k]
                    for x in range(len(top)):
                        top[x] = top[x] - scaled * r_rows[j][x]
            for g in range(g0 + 1, groups):
                for j in range(GROUP):
                    scaled = v[g][j] * recips[j]
                    for k in range(j + 1, GROUP):
                        v[g][k] = v[g][k] - scaled * v_rows[j][k]
                    for x in range(len(top)):
                        r[g][x] = r[g][x] - scaled * r_rows[j][x]
            scale = lax.rsqrt(pivots)
            for x, (ref, c) in enumerate(parts):
                done = top[x] * scale
                if ref is a and c == ch:
                    done = jnp.where(lane >= sub + at, done, 0.0)
                r[g0][x] = done
                ref[:, rows[g0], c * LANES : (c + 1) * LANES] = done
        if p + PANEL == n:
            break
        for b in range(batch):
            panel = jnp.concatenate(
                [jnp.concatenate([r[g][x][b] for g in range(groups)], axis=0) for x in range(len(parts))], axis=1
            )
            h, mid, low = split_three(panel)
            left = jnp.concatenate([h, h, mid, mid, h, low], axis=0)
            right = jnp.concatenate([h, mid, h, mid, low, h], axis=0)
            for c in range(ch, chunks):
                start = max(p + PANEL, c * LANES)
                stop = (c + 1) * LANES
                if start >= stop:
                    continue
                x0 = c - ch
                update = dot(left[:, x0 * LANES : (x0 + 1) * LANES], right, TN)[start - c * LANES :, :]
                for x, (ref, e) in enumerate(parts):
                    if ref is a and e < c:
                        continue
                    lanes = slice(e * LANES, (e + 1) * LANES)
                    ref[b, start:stop, lanes] = ref[b, start:stop, lanes] - update[:, x * LANES : (x + 1) * LANES]


def invert(x):
    guess = pl.reciprocal(x, approx=True)
    return guess * (2.0 - x * guess)


def own_rows(place, own):
    return pl.ds(pl.multiple_of(place[1] * own, own), own)


def first_kernel(packed_zero, packed_one, a, m):
    unpack_symmetric(packed_zero, a, 0)
    unpack_symmetric(packed_one, a, 1)
    start_inverse(m)
    factor(a, m, 0, a.shape[1] // 2)


def second_kernel(scale, place, a_in, m_in, z_high, z_low, bases, transfer, upper_own, a, m):
    del a_in, m_in
    n = a.shape[1]
    factor(a, m, n // 2, n)
    clear_lower(a)
    own = upper_own.shape[0]
    rows = own_rows(place, own)
    upper_own[...] = a[1, rows, :]
    transfer[...] = dot_split(split_two(m[1]), split_two(a[0, rows, :]), NT)
    turned = pltpu.roll(m[0, rows, :] * scale, lax.rem(n - place[1] * own, n), 1)
    inverse = split_two(turned)
    for c in range(0, z_high.shape[1], 512):
        lanes = slice(c, c + 512)
        bases[:, lanes] = dot_split(inverse, (z_high[:, lanes], z_low[:, lanes]), NN)


def tree_kernel(top_scale, place, upper_own, *refs):
    levels = (len(refs) - 3) // 2
    packed = refs[:levels]
    transfers = refs[levels : 2 * levels]
    top, a, m = refs[2 * levels :]
    for b in range(levels):
        unpack_symmetric(packed[b], a, b)
    start_inverse(m)
    factor(a, m, 0, a.shape[1])
    clear_lower(a)
    own = upper_own.shape[0]
    rows = own_rows(place, own)
    for b in range(levels):
        child = upper_own[...] if b == 0 else a[b - 1, rows, :]
        transfers[b][...] = dot_split(split_two(m[b]), split_two(child), NT)
    top[...] = (a[levels - 1, rows, :] * top_scale).T


def whole():
    return pl.BlockSpec(memory_space=pltpu.VMEM)


def params(limit=VMEM_LIMIT):
    return pltpu.CompilerParams(vmem_limit_bytes=limit)


def from_partner(block, axis, bit):
    count = lax.axis_size(axis)
    route = []
    for low in range(count):
        high = low | 1 << bit
        if high != low and high < count:
            route += [(low, high), (high, low)]
    return lax.ppermute(block, axis, route)


def swap_across(block, odd_start):
    count = lax.axis_size("leaf")
    route = []
    for low in range(odd_start, count - 1, 2):
        route += [(low, low + 1), (low + 1, low)]
    return lax.ppermute(block, "leaf", route)


def with_other_parts(block):
    count = lax.axis_size("samp")
    rows = [block]
    for d in range(1, count):
        rows.append(lax.ppermute(block, "samp", [(i, (i - d) % count) for i in range(count)]))
    return jnp.concatenate(rows, axis=0)


def shards(stiffness, columns, samples):
    blocks_here, slots, width, _ = stiffness.shape
    own, row_count = samples.shape
    parts = lax.axis_size("samp")
    total = own * parts
    reach = HB * width
    leaf = lax.axis_index("leaf")
    place = jnp.stack([leaf, lax.axis_index("samp")]).astype(jnp.int32)
    shape = jax.ShapeDtypeStruct
    columns = columns.T

    far_end = row_count - reach
    even = leaf % 2 == 0
    first = lax.dynamic_slice_in_dim(samples, jnp.where(even, far_end, 0), reach, 1)
    second = lax.dynamic_slice_in_dim(samples, jnp.where(even, 0, far_end), reach, 1)
    smem = pl.BlockSpec(memory_space=pltpu.SMEM)
    product_cost = pl.CostEstimate(
        flops=2 * own * slots * width * row_count, bytes_accessed=6 * 1024 * 1024, transcendentals=0
    )

    second_all = with_other_parts(second)
    first_all = with_other_parts(first)
    second_all, place = lax.optimization_barrier((second_all, place))
    near, blocks = pl.pallas_call(
        near_kernel,
        in_specs=[smem, smem, pl.BlockSpec(memory_space=pltpu.HBM), whole()],
        out_specs=[whole()] * 2,
        out_shape=[shape((own, row_count), F32), shape(stiffness.shape, BF16)],
        scratch_shapes=[
            pltpu.VMEM((own, row_count + width), BF16),
            pltpu.SemaphoreType.DMA((blocks_here // ROWS_A_STEP,)),
        ],
        compiler_params=params(VMEM_NEAR),
        cost_estimate=product_cost,
        name="near",
    )(place, columns, stiffness, samples)

    second_all = swap_across(second_all, 1)
    first_all, near = lax.optimization_barrier((first_all, near))
    first_all = swap_across(first_all, 0)

    packed_shape = (total + GROUP, total // 2)
    products, z_high, z_low, packed = pl.pallas_call(
        far_kernel,
        in_specs=[smem, smem] + [whole()] * 4,
        out_specs=[pl.BlockSpec(memory_space=pltpu.HBM)] + [whole()] * 3,
        out_shape=[
            shape((own, row_count), F32),
            shape((total, row_count), BF16),
            shape((total, row_count), BF16),
            shape(packed_shape, F32),
        ],
        scratch_shapes=[
            pltpu.VMEM((total, 2 * reach + width), BF16),
            pltpu.VMEM((own, row_count), F32),
            pltpu.SemaphoreType.DMA,
        ],
        compiler_params=params(),
        name="far",
    )(place, columns, blocks, first_all, second_all, near)

    square = shape((2, total, total), F32)
    transfer_shape = shape((total, own), F32)
    gram_one = packed + from_partner(packed, "leaf", 0)
    gram_two = gram_one + from_partner(gram_one, "leaf", 1)
    a, m = pl.pallas_call(
        first_kernel,
        in_specs=[whole()] * 2,
        out_specs=[whole()] * 2,
        out_shape=[square] * 2,
        compiler_params=params(),
        cost_estimate=pl.CostEstimate(flops=3 * 10**9, bytes_accessed=1024 * 1024, transcendentals=0),
        name="first",
    )(packed, gram_one)
    gram_three = gram_two + from_partner(gram_two, "leaf", 2)
    bases, transfer_one, upper_own, _, _ = pl.pallas_call(
        functools.partial(second_kernel, math.sqrt(row_count)),
        in_specs=[smem] + [whole()] * 4,
        out_specs=[whole()] * 5,
        out_shape=[shape((own, row_count), F32), transfer_shape, shape((own, total), F32), square, square],
        input_output_aliases={1: 3, 2: 4},
        compiler_params=params(),
        cost_estimate=pl.CostEstimate(flops=3 * 10**9, bytes_accessed=1024 * 1024, transcendentals=0),
        name="second",
    )(place, a, m, z_high, z_low)
    transfer_two, transfer_three, top_factor = pl.pallas_call(
        functools.partial(tree_kernel, 1.0 / math.sqrt(2**LEVELS * row_count)),
        in_specs=[smem] + [whole()] * 3,
        out_specs=[whole()] * 3,
        out_shape=[transfer_shape] * 3,
        scratch_shapes=[pltpu.VMEM((2, total, total), F32)] * 2,
        compiler_params=params(),
        name="tree",
    )(place, upper_own, gram_two, gram_three)
    return (products, bases, transfer_one, transfer_two, transfer_three, top_factor)


def solution(mesh):
    return jax.shard_map(
        shards,
        mesh=mesh,
        in_specs=(P("leaf", None, None, None), P("leaf", None), P("samp", "leaf")),
        out_specs=(
            P("samp", "leaf"),
            P("samp", "leaf"),
            P("leaf", "samp"),
            P("leaf", "samp"),
            P("leaf", "samp"),
            P("leaf", "samp"),
        ),
        check_vma=False,
    )
```

```python
import functools
import math

import jax
import jax.numpy as jnp
from jax import lax
from jax.experimental import pallas as pl
from jax.experimental.pallas import tpu as pltpu
from jax.sharding import PartitionSpec as P

HB = 4
LEVELS = 3
LANES = 128
GROUP = 8
PANEL = 32
ROWS_A_STEP = 4
VMEM_LIMIT = 20 * 1024 * 1024
VMEM_NEAR = 48 * 1024 * 1024
F32 = jnp.float32
BF16 = jnp.bfloat16
NN = (((1,), (0,)), ((), ()))
NT = (((1,), (1,)), ((), ()))
TN = (((0,), (0,)), ((), ()))


def dot(a, b, dims):
    return lax.dot_general(a, b, dims, preferred_element_type=F32)


def split_two(x):
    high = x.astype(BF16)
    return high, (x - high.astype(F32)).astype(BF16)


def split_three(x):
    high = x.astype(BF16)
    rest = x - high.astype(F32)
    middle = rest.astype(BF16)
    return high, middle, (rest - middle.astype(F32)).astype(BF16)


def dot_split(a, b, dims):
    (a_high, a_low), (b_high, b_low) = a, b
    return dot(a_high, b_high, dims) + (dot(a_high, b_low, dims) + dot(a_low, b_high, dims))


def far_position(local, count, odd):
    lower = jnp.where(odd, 0, HB)
    below = jnp.clip(local + HB, 0, HB - 1) + lower
    above = jnp.clip(local - count, 0, HB - 1) + (HB - lower)
    return jnp.where(local < 0, below, jnp.where(local < count, 2 * HB, above))


def block_rows(place, columns, blocks, windows, emit, before=None):
    count, slots, width, _ = blocks.shape

    def body(step, carry):
        if before is not None:
            before(step)
        for rr in range(ROWS_A_STEP):
            row = step * ROWS_A_STEP + rr
            local = [columns[k, row] - place[0] * count for k in range(slots)]
            picked = []
            for window, position in windows:
                ats = [pl.multiple_of(position(at) * width, LANES) for at in local]
                picked.append(jnp.concatenate([window[:, pl.ds(at, width)] for at in ats], axis=1))
            stored = jnp.concatenate([blocks[row, k] for k in range(slots)], axis=1)
            product = dot(jnp.concatenate(picked, axis=0), stored, NT)
            emit(pl.ds(pl.multiple_of(row * width, LANES), width), product)
        return carry

    lax.fori_loop(0, count // ROWS_A_STEP, body, 0)


def prepare_kernel(at, samples, copied, first, second, arrived):
    reach = first.shape[1]
    copies = [
        pltpu.make_async_copy(samples.at[:, pl.ds(pl.multiple_of(at[0], LANES), reach)], first, arrived.at[0]),
        pltpu.make_async_copy(samples.at[:, pl.ds(pl.multiple_of(at[1], LANES), reach)], second, arrived.at[1]),
        pltpu.make_async_copy(samples, copied, arrived.at[2]),
    ]
    for copy in copies:
        copy.start()
    for copy in copies:
        copy.wait()


def fill_window(window, halos):
    own, reach = halos[0].shape
    for at in range(0, len(halos), 2):
        rows = slice(at // 2 * own, (at // 2 + 1) * own)
        window[rows, :reach] = halos[at][...]
        window[rows, reach : 2 * reach] = halos[at + 1][...]
    window[:, 2 * reach :] = jnp.zeros((window.shape[0], window.shape[1] - 2 * reach), BF16)


def far_pick(place, blocks, window):
    odd = lax.rem(place[0], 2) == 1
    count = blocks.shape[0]
    return window, lambda local: far_position(local, count, odd)


def own_kernel(
    place, columns, blocks_hbm, samples, first, second,
    products, blocks, z_high, z_low, gram, near_window, far_window, sums, arrived, leaving,
):
    count, _, width, _ = blocks.shape
    own = samples.shape[0]

    def chunk(step):
        rows = pl.ds(step * ROWS_A_STEP, ROWS_A_STEP)
        return pltpu.make_async_copy(blocks_hbm.at[rows], blocks.at[rows], arrived.at[step])

    for step in range(count // ROWS_A_STEP):
        chunk(step).start()
    near_window[:, : samples.shape[1]] = samples[...]
    near_window[:, samples.shape[1] :] = jnp.zeros((own, width), BF16)
    fill_window(far_window, (first, second))

    def near_position(local):
        return jnp.where((local >= 0) & (local < count), local, count)

    def emit(lanes, both):
        remote = both[own:]
        sums[:, lanes] = both[:own] + remote
        z_high[:, lanes], z_low[:, lanes] = split_two(remote)

    windows = [(near_window, near_position), far_pick(place, blocks, far_window)]
    block_rows(place, columns, blocks, windows, emit, lambda step: chunk(step).wait())
    leave = pltpu.make_async_copy(sums, products, leaving)
    leave.start()
    halves = z_high[...], z_low[...]
    gram[...] = dot_split(halves, halves, NT)
    leave.wait()


def others_kernel(parts, place, columns, blocks, *refs):
    halos = refs[: 2 * (parts - 1)]
    own_high, own_low, own_gram, z_high, z_low, packed, window, full = refs[2 * (parts - 1) :]
    own = own_high.shape[0]
    fill_window(window, halos)

    def emit(lanes, remote):
        z_high[:, lanes], z_low[:, lanes] = split_two(remote)

    block_rows(place, columns, blocks, [far_pick(place, blocks, window)], emit)
    high, low = z_high[...], z_low[...]
    all_high = jnp.concatenate([own_high[...], high], axis=0)
    all_low = jnp.concatenate([own_low[...], low], axis=0)
    gram_rows = dot_split((high, low), (all_high, all_low), NT)
    full[:own, :own] = own_gram[...]
    full[own:, :] = gram_rows
    full[:own, own:] = gram_rows[:, :own].T
    shift = place[1] * own
    pack_symmetric(packed, pltpu.roll(pltpu.roll(full[...], shift, 0), shift, 1))


def square_iota(n):
    return lax.broadcasted_iota(jnp.int32, (n, n), 0), lax.broadcasted_iota(jnp.int32, (n, n), 1)


def pack_symmetric(packed, full):
    h = full.shape[0] // 2
    row, col = square_iota(h)
    first = full[:h, :h]
    packed[:h, :] = full[:h, h:]
    packed[h : 2 * h, :] = jnp.where(row > col, first, full[h:, h:])
    diagonal = jnp.sum(jnp.where(row == col, first, 0.0), axis=0, keepdims=True)
    packed[2 * h :, :] = jnp.broadcast_to(diagonal, (GROUP, h))


def unpack_symmetric(packed, full, b):
    h = packed.shape[1]
    row, col = square_iota(h)
    shared = packed[h : 2 * h, :]
    lower = jnp.where(row > col, shared, 0.0)
    diagonal = jnp.where(row == col, jnp.broadcast_to(packed[2 * h : 2 * h + 1, :], (h, h)), 0.0)
    upper = jnp.where(row <= col, shared, 0.0)
    full[b, :h, :h] = lower + lower.T + diagonal
    full[b, h:, h:] = upper + jnp.where(row < col, upper, 0.0).T
    full[b, :h, h:] = packed[:h, :]


def row_of(x, j):
    return jnp.broadcast_to(x[:, j : j + 1, :], x.shape)


def start_inverse(m):
    batch, n, _ = m.shape
    row, col = square_iota(LANES)
    for b in range(batch):
        for c in range(0, n, LANES):
            for e in range(0, n, LANES):
                m[b, c : c + LANES, e : e + LANES] = (
                    (row == col).astype(F32) if e == c else jnp.zeros((LANES, LANES), F32)
                )


def clear_lower(a):
    batch, n, _ = a.shape
    for b in range(batch):
        for c in range(LANES, n, LANES):
            a[b, c : c + LANES, :c] = jnp.zeros((LANES, c), F32)


def factor(a, m, first, last):
    batch, n, _ = a.shape
    chunks = n // LANES
    groups = PANEL // GROUP
    tile = (batch, GROUP, LANES)
    sub = lax.broadcasted_iota(jnp.int32, tile, 1)
    lane = lax.broadcasted_iota(jnp.int32, tile, 2)
    for p in range(first, last, PANEL):
        ch = p // LANES
        parts = [(a, c) for c in range(ch, chunks)] + [(m, c) for c in range(ch + 1)]
        rows = [slice(p + GROUP * g, p + GROUP * (g + 1)) for g in range(groups)]
        r = [[ref[:, rows[g], c * LANES : (c + 1) * LANES] for ref, c in parts] for g in range(groups)]
        for g0 in range(groups):
            at = p - ch * LANES + GROUP * g0
            v = [
                [jnp.broadcast_to(r[g][0][:, :, at + k : at + k + 1], tile) for k in range(GROUP)]
                if g >= g0
                else None
                for g in range(groups)
            ]
            head, top = v[g0], r[g0]
            recips, v_rows, r_rows = [], [], []
            pivots = None
            for j in range(GROUP):
                d = row_of(head[j], j)
                rc = invert(d)
                recips.append(rc)
                pivots = d if pivots is None else jnp.where(sub == j, d, pivots)
                v_rows.append([row_of(head[k], j) if k > j else None for k in range(GROUP)])
                r_rows.append([row_of(x, j) for x in top])
                if j < GROUP - 1:
                    below = jnp.where(sub > j, head[j], 0.0)
                    scaled = below * rc
                    for k in range(j + 1, GROUP):
                        if k == j + 1:
                            head[k] = head[k] - (below * v_rows[j][k]) * rc
                        else:
                            head[k] = head[k] - scaled * v_rows[j][k]
                    for x in range(len(top)):
                        top[x] = top[x] - scaled * r_rows[j][x]
            for g in range(g0 + 1, groups):
                for j in range(GROUP):
                    scaled = v[g][j] * recips[j]
                    for k in range(j + 1, GROUP):
                        v[g][k] = v[g][k] - scaled * v_rows[j][k]
                    for x in range(len(top)):
                        r[g][x] = r[g][x] - scaled * r_rows[j][x]
            scale = lax.rsqrt(pivots)
            for x, (ref, c) in enumerate(parts):
                done = top[x] * scale
                if ref is a and c == ch:
                    done = jnp.where(lane >= sub + at, done, 0.0)
                r[g0][x] = done
                ref[:, rows[g0], c * LANES : (c + 1) * LANES] = done
        if p + PANEL == n:
            break
        for b in range(batch):
            panel = jnp.concatenate(
                [jnp.concatenate([r[g][x][b] for g in range(groups)], axis=0) for x in range(len(parts))], axis=1
            )
            h, mid, low = split_three(panel)
            left = jnp.concatenate([h, h, mid, mid, h, low], axis=0)
            right = jnp.concatenate([h, mid, h, mid, low, h], axis=0)
            for c in range(ch, chunks):
                start = max(p + PANEL, c * LANES)
                stop = (c + 1) * LANES
                if start >= stop:
                    continue
                x0 = c - ch
                update = dot(left[:, x0 * LANES : (x0 + 1) * LANES], right, TN)[start - c * LANES :, :]
                for x, (ref, e) in enumerate(parts):
                    if ref is a and e < c:
                        continue
                    lanes = slice(e * LANES, (e + 1) * LANES)
                    ref[b, start:stop, lanes] = ref[b, start:stop, lanes] - update[:, x * LANES : (x + 1) * LANES]


def invert(x):
    guess = pl.reciprocal(x, approx=True)
    return guess * (2.0 - x * guess)


def own_rows(place, own):
    return pl.ds(pl.multiple_of(place[1] * own, own), own)


def first_kernel(packed_zero, packed_one, a, m):
    unpack_symmetric(packed_zero, a, 0)
    unpack_symmetric(packed_one, a, 1)
    start_inverse(m)
    factor(a, m, 0, a.shape[1] // 2)


def second_kernel(scale, place, a_in, m_in, own_high, own_low, rest_high, rest_low, bases, transfer, upper_own, a, m):
    del a_in, m_in
    n = a.shape[1]
    factor(a, m, n // 2, n)
    clear_lower(a)
    own = upper_own.shape[0]
    rows = own_rows(place, own)
    upper_own[...] = a[1, rows, :]
    transfer[...] = dot_split(split_two(m[1]), split_two(a[0, rows, :]), NT)
    turned = pltpu.roll(m[0, rows, :] * scale, lax.rem(n - place[1] * own, n), 1)
    inverse = split_two(turned)
    for c in range(0, own_high.shape[1], 512):
        lanes = slice(c, c + 512)
        high = jnp.concatenate([own_high[:, lanes], rest_high[:, lanes]], axis=0)
        low = jnp.concatenate([own_low[:, lanes], rest_low[:, lanes]], axis=0)
        bases[:, lanes] = dot_split(inverse, (high, low), NN)


def tree_kernel(top_scale, place, upper_own, *refs):
    levels = (len(refs) - 3) // 2
    packed = refs[:levels]
    transfers = refs[levels : 2 * levels]
    top, a, m = refs[2 * levels :]
    for b in range(levels):
        unpack_symmetric(packed[b], a, b)
    start_inverse(m)
    factor(a, m, 0, a.shape[1])
    clear_lower(a)
    own = upper_own.shape[0]
    rows = own_rows(place, own)
    for b in range(levels):
        child = upper_own[...] if b == 0 else a[b - 1, rows, :]
        transfers[b][...] = dot_split(split_two(m[b]), split_two(child), NT)
    top[...] = (a[levels - 1, rows, :] * top_scale).T


def whole():
    return pl.BlockSpec(memory_space=pltpu.VMEM)


def params(limit=VMEM_LIMIT):
    return pltpu.CompilerParams(vmem_limit_bytes=limit)


def from_partner(block, axis, bit):
    count = lax.axis_size(axis)
    route = []
    for low in range(count):
        high = low | 1 << bit
        if high != low and high < count:
            route += [(low, high), (high, low)]
    return lax.ppermute(block, axis, route)


def swap_across(block, odd_start):
    count = lax.axis_size("leaf")
    route = []
    for low in range(odd_start, count - 1, 2):
        route += [(low, low + 1), (low + 1, low)]
    return lax.ppermute(block, "leaf", route)


def sample_shift(block, d):
    count = lax.axis_size("samp")
    return lax.ppermute(block, "samp", [(i, (i - d) % count) for i in range(count)])


def shards(stiffness, columns, samples):
    blocks_here, slots, width, _ = stiffness.shape
    own, row_count = samples.shape
    parts = lax.axis_size("samp")
    total = own * parts
    reach = HB * width
    leaf = lax.axis_index("leaf")
    place = jnp.stack([leaf, lax.axis_index("samp")]).astype(jnp.int32)
    shape = jax.ShapeDtypeStruct
    columns = columns.T

    smem = pl.BlockSpec(memory_space=pltpu.SMEM)
    hbm = pl.BlockSpec(memory_space=pltpu.HBM)
    rest = total - own
    window_lanes = 2 * reach + width
    far_end = row_count - reach
    odd = lax.rem(leaf, 2)
    reach_shape = shape((own, reach), BF16)
    samples, first, second = pl.pallas_call(
        prepare_kernel,
        in_specs=[smem, hbm],
        out_specs=[whole()] * 3,
        out_shape=[shape(samples.shape, BF16), reach_shape, reach_shape],
        scratch_shapes=[pltpu.SemaphoreType.DMA((3,))],
        compiler_params=params(VMEM_NEAR),
        name="prepare",
    )(jnp.stack([far_end * (1 - odd), far_end * odd]).astype(jnp.int32), samples)

    halos = [swap_across(first, 0), swap_across(second, 1)]
    other_halos = [sample_shift(halo, d) for d in range(1, parts) for halo in halos]

    products, blocks, own_high, own_low, own_gram = pl.pallas_call(
        own_kernel,
        in_specs=[smem, smem, hbm] + [whole()] * 3,
        out_specs=[hbm] + [whole()] * 4,
        out_shape=[
            shape((own, row_count), F32),
            shape(stiffness.shape, BF16),
            shape((own, row_count), BF16),
            shape((own, row_count), BF16),
            shape((own, own), F32),
        ],
        scratch_shapes=[
            pltpu.VMEM((own, row_count + width), BF16),
            pltpu.VMEM((own, window_lanes), BF16),
            pltpu.VMEM((own, row_count), F32),
            pltpu.SemaphoreType.DMA((blocks_here // ROWS_A_STEP,)),
            pltpu.SemaphoreType.DMA,
        ],
        compiler_params=params(VMEM_NEAR),
        cost_estimate=pl.CostEstimate(
            flops=4 * own * slots * width * row_count, bytes_accessed=6 * 1024 * 1024, transcendentals=0
        ),
        name="own",
    )(place, columns, stiffness, samples, *halos)

    packed_shape = (total + GROUP, total // 2)
    rest_high, rest_low, packed = pl.pallas_call(
        functools.partial(others_kernel, parts),
        in_specs=[smem, smem] + [whole()] * (2 * parts + 2),
        out_specs=[whole()] * 3,
        out_shape=[shape((rest, row_count), BF16), shape((rest, row_count), BF16), shape(packed_shape, F32)],
        scratch_shapes=[pltpu.VMEM((rest, window_lanes), BF16), pltpu.VMEM((total, total), F32)],
        compiler_params=params(),
        name="others",
    )(place, columns, blocks, *other_halos, own_high, own_low, own_gram)

    square = shape((2, total, total), F32)
    transfer_shape = shape((total, own), F32)
    gram_one = packed + from_partner(packed, "leaf", 0)
    gram_two = gram_one + from_partner(gram_one, "leaf", 1)
    a, m = pl.pallas_call(
        first_kernel,
        in_specs=[whole()] * 2,
        out_specs=[whole()] * 2,
        out_shape=[square] * 2,
        compiler_params=params(),
        cost_estimate=pl.CostEstimate(flops=3 * 10**9, bytes_accessed=1024 * 1024, transcendentals=0),
        name="first",
    )(packed, gram_one)
    gram_three = gram_two + from_partner(gram_two, "leaf", 2)
    bases, transfer_one, upper_own, _, _ = pl.pallas_call(
        functools.partial(second_kernel, math.sqrt(row_count)),
        in_specs=[smem] + [whole()] * 6,
        out_specs=[whole()] * 5,
        out_shape=[shape((own, row_count), F32), transfer_shape, shape((own, total), F32), square, square],
        input_output_aliases={1: 3, 2: 4},
        compiler_params=params(),
        cost_estimate=pl.CostEstimate(flops=3 * 10**9, bytes_accessed=1024 * 1024, transcendentals=0),
        name="second",
    )(place, a, m, own_high, own_low, rest_high, rest_low)
    transfer_two, transfer_three, top_factor = pl.pallas_call(
        functools.partial(tree_kernel, 1.0 / math.sqrt(2**LEVELS * row_count)),
        in_specs=[smem] + [whole()] * 3,
        out_specs=[whole()] * 3,
        out_shape=[transfer_shape] * 3,
        scratch_shapes=[pltpu.VMEM((2, total, total), F32)] * 2,
        compiler_params=params(),
        name="tree",
    )(place, upper_own, gram_two, gram_three)
    return (products, bases, transfer_one, transfer_two, transfer_three, top_factor)


def solution(mesh):
    return jax.shard_map(
        shards,
        mesh=mesh,
        in_specs=(P("leaf", None, None, None), P("leaf", None), P("samp", "leaf")),
        out_specs=(
            P("samp", "leaf"),
            P("samp", "leaf"),
            P("leaf", "samp"),
            P("leaf", "samp"),
            P("leaf", "samp"),
            P("leaf", "samp"),
        ),
        check_vma=False,
    )
```

```python
import functools
import math

import jax
import jax.numpy as jnp
from jax import lax
from jax.experimental import pallas as pl
from jax.experimental.pallas import tpu as pltpu
from jax.sharding import PartitionSpec as P

HB = 4
LEVELS = 3
LANES = 128
GROUP = 8
PANEL = 32
FIRST_EIGHTHS = 5
ROWS_A_STEP = 4
VMEM_LIMIT = 20 * 1024 * 1024
VMEM_NEAR = 48 * 1024 * 1024
F32 = jnp.float32
BF16 = jnp.bfloat16
NN = (((1,), (0,)), ((), ()))
NT = (((1,), (1,)), ((), ()))
TN = (((0,), (0,)), ((), ()))


def dot(a, b, dims):
    return lax.dot_general(a, b, dims, preferred_element_type=F32)


def split_two(x):
    high = x.astype(BF16)
    return high, (x - high.astype(F32)).astype(BF16)


def split_three(x):
    high = x.astype(BF16)
    rest = x - high.astype(F32)
    middle = rest.astype(BF16)
    return high, middle, (rest - middle.astype(F32)).astype(BF16)


def dot_split(a, b, dims):
    (a_high, a_low), (b_high, b_low) = a, b
    return dot(a_high, b_high, dims) + (dot(a_high, b_low, dims) + dot(a_low, b_high, dims))


def far_position(local, count, odd):
    lower = jnp.where(odd, 0, HB)
    below = jnp.clip(local + HB, 0, HB - 1) + lower
    above = jnp.clip(local - count, 0, HB - 1) + (HB - lower)
    return jnp.where(local < 0, below, jnp.where(local < count, 2 * HB, above))


def block_rows(place, columns, blocks, windows, emit, before=None):
    count, slots, width, _ = blocks.shape

    def body(step, carry):
        if before is not None:
            before(step)
        for rr in range(ROWS_A_STEP):
            row = step * ROWS_A_STEP + rr
            local = [columns[k, row] - place[0] * count for k in range(slots)]
            picked = []
            for window, position in windows:
                ats = [pl.multiple_of(position(at) * width, LANES) for at in local]
                picked.append(jnp.concatenate([window[:, pl.ds(at, width)] for at in ats], axis=1))
            stored = jnp.concatenate([blocks[row, k] for k in range(slots)], axis=1)
            product = dot(jnp.concatenate(picked, axis=0), stored, NT)
            emit(pl.ds(pl.multiple_of(row * width, LANES), width), product)
        return carry

    lax.fori_loop(0, count // ROWS_A_STEP, body, 0)


def prepare_kernel(at, samples, copied, first, second, arrived):
    reach = first.shape[1]
    copies = [
        pltpu.make_async_copy(samples.at[:, pl.ds(pl.multiple_of(at[0], LANES), reach)], first, arrived.at[0]),
        pltpu.make_async_copy(samples.at[:, pl.ds(pl.multiple_of(at[1], LANES), reach)], second, arrived.at[1]),
        pltpu.make_async_copy(samples, copied, arrived.at[2]),
    ]
    for copy in copies:
        copy.start()
    for copy in copies:
        copy.wait()


def fill_window(window, halos):
    own, reach = halos[0].shape
    for at in range(0, len(halos), 2):
        rows = slice(at // 2 * own, (at // 2 + 1) * own)
        window[rows, :reach] = halos[at][...]
        window[rows, reach : 2 * reach] = halos[at + 1][...]
    window[:, 2 * reach :] = jnp.zeros((window.shape[0], window.shape[1] - 2 * reach), BF16)


def far_pick(place, blocks, window):
    odd = lax.rem(place[0], 2) == 1
    count = blocks.shape[0]
    return window, lambda local: far_position(local, count, odd)


def own_kernel(
    place, columns, blocks_hbm, samples, first, second,
    products, blocks, z_high, z_low, gram, near_window, far_window, sums, arrived, leaving,
):
    count, _, width, _ = blocks.shape
    own = samples.shape[0]

    def chunk(step):
        rows = pl.ds(step * ROWS_A_STEP, ROWS_A_STEP)
        return pltpu.make_async_copy(blocks_hbm.at[rows], blocks.at[rows], arrived.at[step])

    for step in range(count // ROWS_A_STEP):
        chunk(step).start()
    near_window[:, : samples.shape[1]] = samples[...]
    near_window[:, samples.shape[1] :] = jnp.zeros((own, width), BF16)
    fill_window(far_window, (first, second))

    def near_position(local):
        return jnp.where((local >= 0) & (local < count), local, count)

    def emit(lanes, both):
        remote = both[own:]
        sums[:, lanes] = both[:own] + remote
        z_high[:, lanes], z_low[:, lanes] = split_two(remote)

    windows = [(near_window, near_position), far_pick(place, blocks, far_window)]
    block_rows(place, columns, blocks, windows, emit, lambda step: chunk(step).wait())
    leave = pltpu.make_async_copy(sums, products, leaving)
    leave.start()
    halves = z_high[...], z_low[...]
    gram[...] = dot_split(halves, halves, NT)
    leave.wait()


def others_kernel(parts, place, columns, blocks, *refs):
    halos = refs[: 2 * (parts - 1)]
    own_high, own_low, own_gram, z_high, z_low, packed, window, full = refs[2 * (parts - 1) :]
    own = own_high.shape[0]
    fill_window(window, halos)

    def emit(lanes, remote):
        z_high[:, lanes], z_low[:, lanes] = split_two(remote)

    block_rows(place, columns, blocks, [far_pick(place, blocks, window)], emit)
    high, low = z_high[...], z_low[...]
    all_high = jnp.concatenate([own_high[...], high], axis=0)
    all_low = jnp.concatenate([own_low[...], low], axis=0)
    gram_rows = dot_split((high, low), (all_high, all_low), NT)
    full[:own, :own] = own_gram[...]
    full[own:, :] = gram_rows
    full[:own, own:] = gram_rows[:, :own].T
    shift = place[1] * own
    pack_symmetric(packed, pltpu.roll(pltpu.roll(full[...], shift, 0), shift, 1))


def square_iota(n):
    return lax.broadcasted_iota(jnp.int32, (n, n), 0), lax.broadcasted_iota(jnp.int32, (n, n), 1)


def pack_symmetric(packed, full):
    h = full.shape[0] // 2
    row, col = square_iota(h)
    first = full[:h, :h]
    packed[:h, :] = full[:h, h:]
    packed[h : 2 * h, :] = jnp.where(row > col, first, full[h:, h:])
    diagonal = jnp.sum(jnp.where(row == col, first, 0.0), axis=0, keepdims=True)
    packed[2 * h :, :] = jnp.broadcast_to(diagonal, (GROUP, h))


def largest(packed):
    h = packed.shape[1]
    row, col = square_iota(h)
    on_diagonal = jnp.where(row == col, packed[h : 2 * h, :], 0.0)
    rows = jnp.maximum(jnp.max(on_diagonal, axis=0, keepdims=True), packed[2 * h : 2 * h + 1, :])
    return jnp.max(rows, axis=1, keepdims=True)


def unpack_symmetric(packed, full, b):
    h = packed.shape[1]
    row, col = square_iota(h)
    over = 1.0 / largest(packed)
    shared = packed[h : 2 * h, :] * over
    lower = jnp.where(row > col, shared, 0.0)
    diagonal = jnp.where(row == col, jnp.broadcast_to(packed[2 * h : 2 * h + 1, :] * over, (h, h)), 0.0)
    upper = jnp.where(row <= col, shared, 0.0)
    full[b, :h, :h] = lower + lower.T + diagonal
    full[b, h:, h:] = upper + jnp.where(row < col, upper, 0.0).T
    full[b, :h, h:] = packed[:h, :] * over


def row_of(x, j):
    return jnp.broadcast_to(x[:, j : j + 1, :], x.shape)


def start_inverse(m):
    batch, n, _ = m.shape
    row, col = square_iota(LANES)
    for b in range(batch):
        for c in range(0, n, LANES):
            for e in range(0, n, LANES):
                m[b, c : c + LANES, e : e + LANES] = (
                    (row == col).astype(F32) if e == c else jnp.zeros((LANES, LANES), F32)
                )


def clear_lower(a):
    batch, n, _ = a.shape
    for b in range(batch):
        for c in range(LANES, n, LANES):
            a[b, c : c + LANES, :c] = jnp.zeros((LANES, c), F32)


def factor(a, m, first, last):
    batch, n, _ = a.shape
    chunks = n // LANES
    groups = PANEL // GROUP
    tile = (batch, GROUP, LANES)
    sub = lax.broadcasted_iota(jnp.int32, tile, 1)
    lane = lax.broadcasted_iota(jnp.int32, tile, 2)
    for p in range(first, last, PANEL):
        ch = p // LANES
        parts = [(a, c) for c in range(ch, chunks)] + [(m, c) for c in range(ch + 1)]
        rows = [slice(p + GROUP * g, p + GROUP * (g + 1)) for g in range(groups)]
        r = [[ref[:, rows[g], c * LANES : (c + 1) * LANES] for ref, c in parts] for g in range(groups)]
        for g0 in range(groups):
            at = p - ch * LANES + GROUP * g0
            v = [
                [jnp.broadcast_to(r[g][0][:, :, at + k : at + k + 1], tile) for k in range(GROUP)]
                if g >= g0
                else None
                for g in range(groups)
            ]
            head, top = v[g0], r[g0]
            steps, leading = [], [None] * len(top)
            pivots = cross = dets = None
            for j in range(0, GROUP, 2):
                p00, p10, p11 = row_of(head[j], j), row_of(head[j], j + 1), row_of(head[j + 1], j + 1)
                det = p00 * p11 - p10 * p10
                guess = pl.reciprocal(det, approx=True)
                refine = 2.0 - det * guess
                later = range(j + 2, GROUP)
                v_rows = {k: (row_of(head[k], j), row_of(head[k], j + 1)) for k in later}
                r_rows = [(row_of(x, j), row_of(x, j + 1)) for x in top]
                here = sub >= j
                pivots = p00 if j == 0 else jnp.where(here, p00, pivots)
                cross = p10 if j == 0 else jnp.where(here, p10, cross)
                dets = det if j == 0 else jnp.where(here, det, dets)
                leading = [x0 if j == 0 else jnp.where(here, x0, old) for (x0, _), old in zip(r_rows, leading)]
                c0 = jnp.where(sub > j + 1, head[j], 0.0)
                c1 = jnp.where(sub > j + 1, head[j + 1], 0.0)
                for k in later[:2]:
                    x0, x1 = v_rows[k]
                    term = c0 * (p11 * x0 - p10 * x1) + c1 * (p00 * x1 - p10 * x0)
                    head[k] = head[k] - (term * guess) * refine
                inverse = guess * refine
                q00, q10, q11 = p11 * inverse, p10 * inverse, p00 * inverse
                steps.append((j, q00, q10, q11, v_rows, r_rows))
                if j + 2 < GROUP:
                    w0, w1 = c0 * q00 - c1 * q10, c1 * q11 - c0 * q10
                    for k in later[2:]:
                        head[k] = head[k] - w0 * v_rows[k][0] - w1 * v_rows[k][1]
                    for x in range(len(top)):
                        top[x] = top[x] - w0 * r_rows[x][0] - w1 * r_rows[x][1]
            for g in range(g0 + 1, groups):
                for j, q00, q10, q11, v_rows, r_rows in steps:
                    c0, c1 = v[g][j], v[g][j + 1]
                    w0, w1 = c0 * q00 - c1 * q10, c1 * q11 - c0 * q10
                    for k in range(j + 2, GROUP):
                        v[g][k] = v[g][k] - w0 * v_rows[k][0] - w1 * v_rows[k][1]
                    for x in range(len(top)):
                        r[g][x] = r[g][x] - w0 * r_rows[x][0] - w1 * r_rows[x][1]
            second_row = sub % 2 == 1
            over = invert(pivots)
            ratio = jnp.where(second_row, cross * over, 0.0)
            scale = lax.rsqrt(jnp.where(second_row, dets * over, pivots))
            for x, (ref, c) in enumerate(parts):
                done = (top[x] - ratio * leading[x]) * scale
                if ref is a and c == ch:
                    done = jnp.where(lane >= sub + at, done, 0.0)
                r[g0][x] = done
                ref[:, rows[g0], c * LANES : (c + 1) * LANES] = done
        if p + PANEL == n:
            break
        for b in range(batch):
            panel = jnp.concatenate(
                [jnp.concatenate([r[g][x][b] for g in range(groups)], axis=0) for x in range(len(parts))], axis=1
            )
            h, mid, low = split_three(panel)
            left = jnp.concatenate([h, h, mid, mid, h, low], axis=0)
            right = jnp.concatenate([h, mid, h, mid, low, h], axis=0)
            for c in range(ch, chunks):
                start = max(p + PANEL, c * LANES)
                stop = (c + 1) * LANES
                if start >= stop:
                    continue
                x0 = c - ch
                update = dot(left[:, x0 * LANES : (x0 + 1) * LANES], right, TN)[start - c * LANES :, :]
                for x, (ref, e) in enumerate(parts):
                    if ref is a and e < c:
                        continue
                    lanes = slice(e * LANES, (e + 1) * LANES)
                    ref[b, start:stop, lanes] = ref[b, start:stop, lanes] - update[:, x * LANES : (x + 1) * LANES]


def invert(x):
    guess = pl.reciprocal(x, approx=True)
    return guess * (2.0 - x * guess)


def own_rows(place, own):
    return pl.ds(pl.multiple_of(place[1] * own, own), own)


def first_kernel(stop, packed_zero, packed_one, a, m):
    unpack_symmetric(packed_zero, a, 0)
    unpack_symmetric(packed_one, a, 1)
    start_inverse(m)
    factor(a, m, 0, stop)


def second_kernel(start, scale, place, packed_zero, packed_one, a_in, m_in, own_high, own_low, rest_high, rest_low,
                  bases, transfer, upper_own, a, m):
    del a_in, m_in
    n = a.shape[1]
    factor(a, m, start, n)
    clear_lower(a)
    own = upper_own.shape[0]
    rows = own_rows(place, own)
    size_zero, size_one = largest(packed_zero), largest(packed_one)
    upper_own[...] = a[1, rows, :] * jnp.sqrt(size_one)
    child = a[0, rows, :] * (jnp.sqrt(size_zero) * lax.rsqrt(size_one))
    transfer[...] = dot_split(split_two(m[1]), split_two(child), NT)
    turned = pltpu.roll(m[0, rows, :] * (lax.rsqrt(size_zero) * scale), lax.rem(n - place[1] * own, n), 1)
    inverse = split_two(turned)
    for c in range(0, own_high.shape[1], 512):
        lanes = slice(c, c + 512)
        high = jnp.concatenate([own_high[:, lanes], rest_high[:, lanes]], axis=0)
        low = jnp.concatenate([own_low[:, lanes], rest_low[:, lanes]], axis=0)
        bases[:, lanes] = dot_split(inverse, (high, low), NN)


def tree_kernel(top_scale, place, upper_own, *refs):
    levels = (len(refs) - 3) // 2
    packed = refs[:levels]
    transfers = refs[levels : 2 * levels]
    top, a, m = refs[2 * levels :]
    for b in range(levels):
        unpack_symmetric(packed[b], a, b)
    start_inverse(m)
    factor(a, m, 0, a.shape[1])
    clear_lower(a)
    own = upper_own.shape[0]
    rows = own_rows(place, own)
    sizes = [largest(ref) for ref in packed]
    child = upper_own[...]
    for b in range(levels):
        child = child * lax.rsqrt(sizes[b])
        transfers[b][...] = dot_split(split_two(m[b]), split_two(child), NT)
        child = a[b, rows, :] * jnp.sqrt(sizes[b])
    top[...] = (child * top_scale).T


def whole():
    return pl.BlockSpec(memory_space=pltpu.VMEM)


def params(limit=VMEM_LIMIT):
    return pltpu.CompilerParams(vmem_limit_bytes=limit)


def from_partner(block, axis, bit):
    count = lax.axis_size(axis)
    route = []
    for low in range(count):
        high = low | 1 << bit
        if high != low and high < count:
            route += [(low, high), (high, low)]
    return lax.ppermute(block, axis, route)


def swap_across(block, odd_start):
    count = lax.axis_size("leaf")
    route = []
    for low in range(odd_start, count - 1, 2):
        route += [(low, low + 1), (low + 1, low)]
    return lax.ppermute(block, "leaf", route)


def sample_shift(block, d):
    count = lax.axis_size("samp")
    return lax.ppermute(block, "samp", [(i, (i - d) % count) for i in range(count)])


def shards(stiffness, columns, samples):
    blocks_here, slots, width, _ = stiffness.shape
    own, row_count = samples.shape
    parts = lax.axis_size("samp")
    total = own * parts
    reach = HB * width
    leaf = lax.axis_index("leaf")
    place = jnp.stack([leaf, lax.axis_index("samp")]).astype(jnp.int32)
    shape = jax.ShapeDtypeStruct
    columns = columns.T

    smem = pl.BlockSpec(memory_space=pltpu.SMEM)
    hbm = pl.BlockSpec(memory_space=pltpu.HBM)
    rest = total - own
    window_lanes = 2 * reach + width
    far_end = row_count - reach
    odd = lax.rem(leaf, 2)
    reach_shape = shape((own, reach), BF16)
    samples, first, second = pl.pallas_call(
        prepare_kernel,
        in_specs=[smem, hbm],
        out_specs=[whole()] * 3,
        out_shape=[shape(samples.shape, BF16), reach_shape, reach_shape],
        scratch_shapes=[pltpu.SemaphoreType.DMA((3,))],
        compiler_params=params(VMEM_NEAR),
        name="prepare",
    )(jnp.stack([far_end * (1 - odd), far_end * odd]).astype(jnp.int32), samples)

    halos = [swap_across(first, 0), swap_across(second, 1)]
    other_halos = [sample_shift(halo, d) for d in range(1, parts) for halo in halos]

    products, blocks, own_high, own_low, own_gram = pl.pallas_call(
        own_kernel,
        in_specs=[smem, smem, hbm] + [whole()] * 3,
        out_specs=[hbm] + [whole()] * 4,
        out_shape=[
            shape((own, row_count), F32),
            shape(stiffness.shape, BF16),
            shape((own, row_count), BF16),
            shape((own, row_count), BF16),
            shape((own, own), F32),
        ],
        scratch_shapes=[
            pltpu.VMEM((own, row_count + width), BF16),
            pltpu.VMEM((own, window_lanes), BF16),
            pltpu.VMEM((own, row_count), F32),
            pltpu.SemaphoreType.DMA((blocks_here // ROWS_A_STEP,)),
            pltpu.SemaphoreType.DMA,
        ],
        compiler_params=params(VMEM_NEAR),
        cost_estimate=pl.CostEstimate(
            flops=4 * own * slots * width * row_count, bytes_accessed=6 * 1024 * 1024, transcendentals=0
        ),
        name="own",
    )(place, columns, stiffness, samples, *halos)

    packed_shape = (total + GROUP, total // 2)
    rest_high, rest_low, packed = pl.pallas_call(
        functools.partial(others_kernel, parts),
        in_specs=[smem, smem] + [whole()] * (2 * parts + 2),
        out_specs=[whole()] * 3,
        out_shape=[shape((rest, row_count), BF16), shape((rest, row_count), BF16), shape(packed_shape, F32)],
        scratch_shapes=[pltpu.VMEM((rest, window_lanes), BF16), pltpu.VMEM((total, total), F32)],
        compiler_params=params(),
        name="others",
    )(place, columns, blocks, *other_halos, own_high, own_low, own_gram)

    square = shape((2, total, total), F32)
    split_row = total * FIRST_EIGHTHS // 8 // PANEL * PANEL
    transfer_shape = shape((total, own), F32)
    gram_one = packed + from_partner(packed, "leaf", 0)
    gram_two = gram_one + from_partner(gram_one, "leaf", 1)
    a, m = pl.pallas_call(
        functools.partial(first_kernel, split_row),
        in_specs=[whole()] * 2,
        out_specs=[whole()] * 2,
        out_shape=[square] * 2,
        compiler_params=params(),
        cost_estimate=pl.CostEstimate(flops=3 * 10**9, bytes_accessed=1024 * 1024, transcendentals=0),
        name="first",
    )(packed, gram_one)
    gram_three = gram_two + from_partner(gram_two, "leaf", 2)
    bases, transfer_one, upper_own, _, _ = pl.pallas_call(
        functools.partial(second_kernel, split_row, math.sqrt(row_count)),
        in_specs=[smem] + [whole()] * 8,
        out_specs=[whole()] * 5,
        out_shape=[shape((own, row_count), F32), transfer_shape, shape((own, total), F32), square, square],
        input_output_aliases={3: 3, 4: 4},
        compiler_params=params(),
        cost_estimate=pl.CostEstimate(flops=3 * 10**9, bytes_accessed=1024 * 1024, transcendentals=0),
        name="second",
    )(place, packed, gram_one, a, m, own_high, own_low, rest_high, rest_low)
    transfer_two, transfer_three, top_factor = pl.pallas_call(
        functools.partial(tree_kernel, 1.0 / math.sqrt(2**LEVELS * row_count)),
        in_specs=[smem] + [whole()] * 3,
        out_specs=[whole()] * 3,
        out_shape=[transfer_shape] * 3,
        scratch_shapes=[pltpu.VMEM((2, total, total), F32)] * 2,
        compiler_params=params(),
        name="tree",
    )(place, upper_own, gram_two, gram_three)
    return (products, bases, transfer_one, transfer_two, transfer_three, top_factor)


def solution(mesh):
    return jax.shard_map(
        shards,
        mesh=mesh,
        in_specs=(P("leaf", None, None, None), P("leaf", None), P("samp", "leaf")),
        out_specs=(
            P("samp", "leaf"),
            P("samp", "leaf"),
            P("leaf", "samp"),
            P("leaf", "samp"),
            P("leaf", "samp"),
            P("leaf", "samp"),
        ),
        check_vma=False,
    )
```

```python
import functools
import math

import jax
import jax.numpy as jnp
from jax import lax
from jax.experimental import pallas as pl
from jax.experimental.pallas import tpu as pltpu
from jax.sharding import PartitionSpec as P

HB = 4
LEVELS = 3
LANES = 128
GROUP = 8
PANEL = 32
FIRST_EIGHTHS = 5
ROWS_A_STEP = 4
VMEM_LIMIT = 20 * 1024 * 1024
VMEM_NEAR = 48 * 1024 * 1024
F32 = jnp.float32
BF16 = jnp.bfloat16
NN = (((1,), (0,)), ((), ()))
NT = (((1,), (1,)), ((), ()))
TN = (((0,), (0,)), ((), ()))


def dot(a, b, dims):
    return lax.dot_general(a, b, dims, preferred_element_type=F32)


def split_two(x):
    high = x.astype(BF16)
    return high, (x - high.astype(F32)).astype(BF16)


def dot_split(a, b, dims):
    (a_high, a_low), (b_high, b_low) = a, b
    return dot(a_high, b_high, dims) + (dot(a_high, b_low, dims) + dot(a_low, b_high, dims))


def far_position(local, count, odd):
    lower = jnp.where(odd, 0, HB)
    below = jnp.clip(local + HB, 0, HB - 1) + lower
    above = jnp.clip(local - count, 0, HB - 1) + (HB - lower)
    return jnp.where(local < 0, below, jnp.where(local < count, 2 * HB, above))


def block_rows(place, columns, blocks, windows, emit, before=None):
    count, slots, width, _ = blocks.shape

    def body(step, carry):
        if before is not None:
            before(step)
        for rr in range(ROWS_A_STEP):
            row = step * ROWS_A_STEP + rr
            local = [columns[k, row] - place[0] * count for k in range(slots)]
            picked = []
            for window, position in windows:
                ats = [pl.multiple_of(position(at) * width, LANES) for at in local]
                picked.append(jnp.concatenate([window[:, pl.ds(at, width)] for at in ats], axis=1))
            stored = jnp.concatenate([blocks[row, k] for k in range(slots)], axis=1)
            product = dot(jnp.concatenate(picked, axis=0), stored, NT)
            emit(pl.ds(pl.multiple_of(row * width, LANES), width), product)
        return carry

    lax.fori_loop(0, count // ROWS_A_STEP, body, 0)


def prepare_kernel(at, samples, copied, first, second, arrived):
    reach = first.shape[1]
    copies = [
        pltpu.make_async_copy(samples.at[:, pl.ds(pl.multiple_of(at[0], LANES), reach)], first, arrived.at[0]),
        pltpu.make_async_copy(samples.at[:, pl.ds(pl.multiple_of(at[1], LANES), reach)], second, arrived.at[1]),
        pltpu.make_async_copy(samples, copied, arrived.at[2]),
    ]
    for copy in copies:
        copy.start()
    for copy in copies:
        copy.wait()


def fill_window(window, halos):
    own, reach = halos[0].shape
    for at in range(0, len(halos), 2):
        rows = slice(at // 2 * own, (at // 2 + 1) * own)
        window[rows, :reach] = halos[at][...]
        window[rows, reach : 2 * reach] = halos[at + 1][...]
    window[:, 2 * reach :] = jnp.zeros((window.shape[0], window.shape[1] - 2 * reach), BF16)


def far_pick(place, blocks, window):
    odd = lax.rem(place[0], 2) == 1
    count = blocks.shape[0]
    return window, lambda local: far_position(local, count, odd)


def own_kernel(
    place, columns, blocks_hbm, samples, first, second,
    products, blocks, z_high, z_low, gram, near_window, far_window, sums, arrived, leaving,
):
    count, _, width, _ = blocks.shape
    own = samples.shape[0]

    def chunk(step):
        rows = pl.ds(step * ROWS_A_STEP, ROWS_A_STEP)
        return pltpu.make_async_copy(blocks_hbm.at[rows], blocks.at[rows], arrived.at[step])

    for step in range(count // ROWS_A_STEP):
        chunk(step).start()
    near_window[:, : samples.shape[1]] = samples[...]
    near_window[:, samples.shape[1] :] = jnp.zeros((own, width), BF16)
    fill_window(far_window, (first, second))

    def near_position(local):
        return jnp.where((local >= 0) & (local < count), local, count)

    def emit(lanes, both):
        remote = both[own:]
        sums[:, lanes] = both[:own] + remote
        z_high[:, lanes], z_low[:, lanes] = split_two(remote)

    windows = [(near_window, near_position), far_pick(place, blocks, far_window)]
    block_rows(place, columns, blocks, windows, emit, lambda step: chunk(step).wait())
    leave = pltpu.make_async_copy(sums, products, leaving)
    leave.start()
    halves = z_high[...], z_low[...]
    gram[...] = dot_split(halves, halves, NT)
    leave.wait()


def others_kernel(parts, place, columns, blocks, *refs):
    halos = refs[: 2 * (parts - 1)]
    own_high, own_low, own_gram, z_high, z_low, packed, window, full = refs[2 * (parts - 1) :]
    own = own_high.shape[0]
    fill_window(window, halos)

    def emit(lanes, remote):
        z_high[:, lanes], z_low[:, lanes] = split_two(remote)

    block_rows(place, columns, blocks, [far_pick(place, blocks, window)], emit)
    high, low = z_high[...], z_low[...]
    all_high = jnp.concatenate([own_high[...], high], axis=0)
    all_low = jnp.concatenate([own_low[...], low], axis=0)
    gram_rows = dot_split((high, low), (all_high, all_low), NT)
    full[:own, :own] = own_gram[...]
    full[own:, :] = gram_rows
    full[:own, own:] = gram_rows[:, :own].T
    shift = place[1] * own
    pack_symmetric(packed, pltpu.roll(pltpu.roll(full[...], shift, 0), shift, 1))


def square_iota(n):
    return lax.broadcasted_iota(jnp.int32, (n, n), 0), lax.broadcasted_iota(jnp.int32, (n, n), 1)


def pack_symmetric(packed, full):
    h = full.shape[0] // 2
    row, col = square_iota(h)
    first = full[:h, :h]
    packed[:h, :] = full[:h, h:]
    packed[h : 2 * h, :] = jnp.where(row > col, first, full[h:, h:])
    diagonal = jnp.sum(jnp.where(row == col, first, 0.0), axis=0, keepdims=True)
    packed[2 * h :, :] = jnp.broadcast_to(diagonal, (GROUP, h))


def largest(packed):
    h = packed.shape[1]
    row, col = square_iota(h)
    on_diagonal = jnp.where(row == col, packed[h : 2 * h, :], 0.0)
    rows = jnp.maximum(jnp.max(on_diagonal, axis=0, keepdims=True), packed[2 * h : 2 * h + 1, :])
    return jnp.max(rows, axis=1, keepdims=True)


def unpack_symmetric(packed, full, b):
    h = packed.shape[1]
    row, col = square_iota(h)
    over = 1.0 / largest(packed)
    shared = packed[h : 2 * h, :] * over
    lower = jnp.where(row > col, shared, 0.0)
    diagonal = jnp.where(row == col, jnp.broadcast_to(packed[2 * h : 2 * h + 1, :] * over, (h, h)), 0.0)
    upper = jnp.where(row <= col, shared, 0.0)
    full[b, :h, :h] = lower + lower.T + diagonal
    full[b, h:, h:] = upper + jnp.where(row < col, upper, 0.0).T
    full[b, :h, h:] = packed[:h, :] * over


def row_of(x, j):
    return jnp.broadcast_to(x[:, j : j + 1, :], x.shape)


def start_inverse(m):
    batch, n, _ = m.shape
    row, col = square_iota(LANES)
    for b in range(batch):
        for c in range(0, n, LANES):
            for e in range(0, n, LANES):
                m[b, c : c + LANES, e : e + LANES] = (
                    (row == col).astype(F32) if e == c else jnp.zeros((LANES, LANES), F32)
                )


def clear_lower(a):
    batch, n, _ = a.shape
    for b in range(batch):
        for c in range(LANES, n, LANES):
            a[b, c : c + LANES, :c] = jnp.zeros((LANES, c), F32)


def factor(a, m, first, last):
    batch, n, _ = a.shape
    groups = PANEL // GROUP
    tile = (batch, GROUP, LANES)
    sub = lax.broadcasted_iota(jnp.int32, tile, 1)
    lane = lax.broadcasted_iota(jnp.int32, tile, 2)
    for p in range(first, last, PANEL):
        ch = p // LANES
        parts = [(a, ch), (m, ch)]
        rows = [slice(p + GROUP * g, p + GROUP * (g + 1)) for g in range(groups)]
        r = [[ref[:, rows[g], c * LANES : (c + 1) * LANES] for ref, c in parts] for g in range(groups)]
        for g0 in range(groups):
            at = p - ch * LANES + GROUP * g0
            v = [
                [jnp.broadcast_to(r[g][0][:, :, at + k : at + k + 1], tile) for k in range(GROUP)]
                if g >= g0
                else None
                for g in range(groups)
            ]
            head, top = v[g0], r[g0]
            steps, leading = [], [None] * len(top)
            pivots = cross = dets = None
            for j in range(0, GROUP, 2):
                p00, p10, p11 = row_of(head[j], j), row_of(head[j], j + 1), row_of(head[j + 1], j + 1)
                det = p00 * p11 - p10 * p10
                guess = pl.reciprocal(det, approx=True)
                refine = 2.0 - det * guess
                later = range(j + 2, GROUP)
                v_rows = {k: (row_of(head[k], j), row_of(head[k], j + 1)) for k in later}
                r_rows = [(row_of(x, j), row_of(x, j + 1)) for x in top]
                here = sub >= j
                pivots = p00 if j == 0 else jnp.where(here, p00, pivots)
                cross = p10 if j == 0 else jnp.where(here, p10, cross)
                dets = det if j == 0 else jnp.where(here, det, dets)
                leading = [x0 if j == 0 else jnp.where(here, x0, old) for (x0, _), old in zip(r_rows, leading)]
                c0 = jnp.where(sub > j + 1, head[j], 0.0)
                c1 = jnp.where(sub > j + 1, head[j + 1], 0.0)
                for k in later[:2]:
                    x0, x1 = v_rows[k]
                    term = c0 * (p11 * x0 - p10 * x1) + c1 * (p00 * x1 - p10 * x0)
                    head[k] = head[k] - (term * guess) * refine
                inverse = guess * refine
                q00, q10, q11 = p11 * inverse, p10 * inverse, p00 * inverse
                steps.append((j, q00, q10, q11, v_rows, r_rows))
                if j + 2 < GROUP:
                    w0, w1 = c0 * q00 - c1 * q10, c1 * q11 - c0 * q10
                    for k in later[2:]:
                        head[k] = head[k] - w0 * v_rows[k][0] - w1 * v_rows[k][1]
                    for x in range(len(top)):
                        top[x] = top[x] - w0 * r_rows[x][0] - w1 * r_rows[x][1]
            for g in range(g0 + 1, groups):
                for j, q00, q10, q11, v_rows, r_rows in steps:
                    c0, c1 = v[g][j], v[g][j + 1]
                    w0, w1 = c0 * q00 - c1 * q10, c1 * q11 - c0 * q10
                    for k in range(j + 2, GROUP):
                        v[g][k] = v[g][k] - w0 * v_rows[k][0] - w1 * v_rows[k][1]
                    for x in range(len(top)):
                        r[g][x] = r[g][x] - w0 * r_rows[x][0] - w1 * r_rows[x][1]
            second_row = sub % 2 == 1
            over = invert(pivots)
            ratio = jnp.where(second_row, cross * over, 0.0)
            scale = lax.rsqrt(jnp.where(second_row, dets * over, pivots))
            for x, (ref, c) in enumerate(parts):
                done = (top[x] - ratio * leading[x]) * scale
                if ref is a and c == ch:
                    done = jnp.where(lane >= sub + at, done, 0.0)
                r[g0][x] = done
                ref[:, rows[g0], c * LANES : (c + 1) * LANES] = done
        end = (ch + 1) * LANES
        if p + PANEL == end:
            join_chunks(a, m, ch)
            continue
        for b in range(batch):
            panel = jnp.concatenate(
                [jnp.concatenate([r[g][x][b] for g in range(groups)], axis=0) for x in range(len(parts))], axis=1
            )
            high, low = split_two(panel)
            left = jnp.concatenate([high[:, :LANES], high[:, :LANES], low[:, :LANES]], axis=0)
            right = jnp.concatenate([high, low, high], axis=0)
            update = dot(left, right, TN)[p + PANEL - ch * LANES :, :]
            for x, (ref, e) in enumerate(parts):
                lanes = slice(e * LANES, (e + 1) * LANES)
                ref[b, p + PANEL : end, lanes] = ref[b, p + PANEL : end, lanes] - update[:, x * LANES : (x + 1) * LANES]


def join_chunks(a, m, ch):
    batch, n, _ = a.shape
    here = slice(ch * LANES, (ch + 1) * LANES)
    for b in range(batch):
        inverse = split_two(m[b, here, here])
        if ch > 0:
            before = slice(0, ch * LANES)
            m[b, here, before] = -dot_split(inverse, split_two(m[b, here, before]), NN)
        later = slice((ch + 1) * LANES, n)
        if later.start == n:
            continue
        upper = dot_split(inverse, split_two(a[b, here, later]), NN)
        a[b, here, later] = upper
        upper = split_two(upper)
        done = split_two(m[b, here, : (ch + 1) * LANES])
        both = tuple(jnp.concatenate(pair, axis=1) for pair in zip(upper, done))
        update = dot_split(upper, both, TN)
        a[b, later, later] = a[b, later, later] - update[:, : n - later.start]
        m[b, later, : later.start] = m[b, later, : later.start] + update[:, n - later.start :]


def invert(x):
    guess = pl.reciprocal(x, approx=True)
    return guess * (2.0 - x * guess)


def own_rows(place, own):
    return pl.ds(pl.multiple_of(place[1] * own, own), own)


def first_kernel(stop, packed_zero, packed_one, a, m):
    unpack_symmetric(packed_zero, a, 0)
    unpack_symmetric(packed_one, a, 1)
    start_inverse(m)
    factor(a, m, 0, stop)


def second_kernel(start, scale, place, packed_zero, packed_one, a_in, m_in, own_high, own_low, rest_high, rest_low,
                  bases, transfer, upper_own, a, m):
    del a_in, m_in
    n = a.shape[1]
    factor(a, m, start, n)
    clear_lower(a)
    own = upper_own.shape[0]
    rows = own_rows(place, own)
    size_zero, size_one = largest(packed_zero), largest(packed_one)
    upper_own[...] = a[1, rows, :] * jnp.sqrt(size_one)
    child = a[0, rows, :] * (jnp.sqrt(size_zero) * lax.rsqrt(size_one))
    transfer[...] = dot_split(split_two(m[1]), split_two(child), NT)
    turned = pltpu.roll(m[0, rows, :] * (lax.rsqrt(size_zero) * scale), lax.rem(n - place[1] * own, n), 1)
    inverse = split_two(turned)
    for c in range(0, own_high.shape[1], 512):
        lanes = slice(c, c + 512)
        high = jnp.concatenate([own_high[:, lanes], rest_high[:, lanes]], axis=0)
        low = jnp.concatenate([own_low[:, lanes], rest_low[:, lanes]], axis=0)
        bases[:, lanes] = dot_split(inverse, (high, low), NN)


def tree_kernel(top_scale, place, upper_own, *refs):
    levels = (len(refs) - 3) // 2
    packed = refs[:levels]
    transfers = refs[levels : 2 * levels]
    top, a, m = refs[2 * levels :]
    for b in range(levels):
        unpack_symmetric(packed[b], a, b)
    start_inverse(m)
    factor(a, m, 0, a.shape[1])
    clear_lower(a)
    own = upper_own.shape[0]
    rows = own_rows(place, own)
    sizes = [largest(ref) for ref in packed]
    child = upper_own[...]
    for b in range(levels):
        child = child * lax.rsqrt(sizes[b])
        transfers[b][...] = dot_split(split_two(m[b]), split_two(child), NT)
        child = a[b, rows, :] * jnp.sqrt(sizes[b])
    top[...] = (child * top_scale).T


def whole():
    return pl.BlockSpec(memory_space=pltpu.VMEM)


def params(limit=VMEM_LIMIT):
    return pltpu.CompilerParams(vmem_limit_bytes=limit)


def from_partner(block, axis, bit):
    count = lax.axis_size(axis)
    route = []
    for low in range(count):
        high = low | 1 << bit
        if high != low and high < count:
            route += [(low, high), (high, low)]
    return lax.ppermute(block, axis, route)


def swap_across(block, odd_start):
    count = lax.axis_size("leaf")
    route = []
    for low in range(odd_start, count - 1, 2):
        route += [(low, low + 1), (low + 1, low)]
    return lax.ppermute(block, "leaf", route)


def sample_shift(block, d):
    count = lax.axis_size("samp")
    return lax.ppermute(block, "samp", [(i, (i - d) % count) for i in range(count)])


def shards(stiffness, columns, samples):
    blocks_here, slots, width, _ = stiffness.shape
    own, row_count = samples.shape
    parts = lax.axis_size("samp")
    total = own * parts
    reach = HB * width
    leaf = lax.axis_index("leaf")
    place = jnp.stack([leaf, lax.axis_index("samp")]).astype(jnp.int32)
    shape = jax.ShapeDtypeStruct
    columns = columns.T

    smem = pl.BlockSpec(memory_space=pltpu.SMEM)
    hbm = pl.BlockSpec(memory_space=pltpu.HBM)
    rest = total - own
    window_lanes = 2 * reach + width
    far_end = row_count - reach
    odd = lax.rem(leaf, 2)
    reach_shape = shape((own, reach), BF16)
    samples, first, second = pl.pallas_call(
        prepare_kernel,
        in_specs=[smem, hbm],
        out_specs=[whole()] * 3,
        out_shape=[shape(samples.shape, BF16), reach_shape, reach_shape],
        scratch_shapes=[pltpu.SemaphoreType.DMA((3,))],
        compiler_params=params(VMEM_NEAR),
        name="prepare",
    )(jnp.stack([far_end * (1 - odd), far_end * odd]).astype(jnp.int32), samples)

    halos = [swap_across(first, 0), swap_across(second, 1)]
    other_halos = [sample_shift(halo, d) for d in range(1, parts) for halo in halos]

    products, blocks, own_high, own_low, own_gram = pl.pallas_call(
        own_kernel,
        in_specs=[smem, smem, hbm] + [whole()] * 3,
        out_specs=[hbm] + [whole()] * 4,
        out_shape=[
            shape((own, row_count), F32),
            shape(stiffness.shape, BF16),
            shape((own, row_count), BF16),
            shape((own, row_count), BF16),
            shape((own, own), F32),
        ],
        scratch_shapes=[
            pltpu.VMEM((own, row_count + width), BF16),
            pltpu.VMEM((own, window_lanes), BF16),
            pltpu.VMEM((own, row_count), F32),
            pltpu.SemaphoreType.DMA((blocks_here // ROWS_A_STEP,)),
            pltpu.SemaphoreType.DMA,
        ],
        compiler_params=params(VMEM_NEAR),
        cost_estimate=pl.CostEstimate(
            flops=4 * own * slots * width * row_count, bytes_accessed=6 * 1024 * 1024, transcendentals=0
        ),
        name="own",
    )(place, columns, stiffness, samples, *halos)

    packed_shape = (total + GROUP, total // 2)
    rest_high, rest_low, packed = pl.pallas_call(
        functools.partial(others_kernel, parts),
        in_specs=[smem, smem] + [whole()] * (2 * parts + 2),
        out_specs=[whole()] * 3,
        out_shape=[shape((rest, row_count), BF16), shape((rest, row_count), BF16), shape(packed_shape, F32)],
        scratch_shapes=[pltpu.VMEM((rest, window_lanes), BF16), pltpu.VMEM((total, total), F32)],
        compiler_params=params(),
        name="others",
    )(place, columns, blocks, *other_halos, own_high, own_low, own_gram)

    square = shape((2, total, total), F32)
    split_row = total * FIRST_EIGHTHS // 8 // PANEL * PANEL
    transfer_shape = shape((total, own), F32)
    gram_one = packed + from_partner(packed, "leaf", 0)
    gram_two = gram_one + from_partner(gram_one, "leaf", 1)
    a, m = pl.pallas_call(
        functools.partial(first_kernel, split_row),
        in_specs=[whole()] * 2,
        out_specs=[whole()] * 2,
        out_shape=[square] * 2,
        compiler_params=params(),
        cost_estimate=pl.CostEstimate(flops=3 * 10**9, bytes_accessed=1024 * 1024, transcendentals=0),
        name="first",
    )(packed, gram_one)
    gram_three = gram_two + from_partner(gram_two, "leaf", 2)
    bases, transfer_one, upper_own, _, _ = pl.pallas_call(
        functools.partial(second_kernel, split_row, math.sqrt(row_count)),
        in_specs=[smem] + [whole()] * 8,
        out_specs=[whole()] * 5,
        out_shape=[shape((own, row_count), F32), transfer_shape, shape((own, total), F32), square, square],
        input_output_aliases={3: 3, 4: 4},
        compiler_params=params(),
        cost_estimate=pl.CostEstimate(flops=3 * 10**9, bytes_accessed=1024 * 1024, transcendentals=0),
        name="second",
    )(place, packed, gram_one, a, m, own_high, own_low, rest_high, rest_low)
    transfer_two, transfer_three, top_factor = pl.pallas_call(
        functools.partial(tree_kernel, 1.0 / math.sqrt(2**LEVELS * row_count)),
        in_specs=[smem] + [whole()] * 3,
        out_specs=[whole()] * 3,
        out_shape=[transfer_shape] * 3,
        scratch_shapes=[pltpu.VMEM((2, total, total), F32)] * 2,
        compiler_params=params(),
        name="tree",
    )(place, upper_own, gram_two, gram_three)
    return (products, bases, transfer_one, transfer_two, transfer_three, top_factor)


def solution(mesh):
    return jax.shard_map(
        shards,
        mesh=mesh,
        in_specs=(P("leaf", None, None, None), P("leaf", None), P("samp", "leaf")),
        out_specs=(
            P("samp", "leaf"),
            P("samp", "leaf"),
            P("leaf", "samp"),
            P("leaf", "samp"),
            P("leaf", "samp"),
            P("leaf", "samp"),
        ),
        check_vma=False,
    )
```

```python
import functools
import math

import jax
import jax.numpy as jnp
from jax import lax
from jax.experimental import pallas as pl
from jax.experimental.pallas import tpu as pltpu
from jax.sharding import PartitionSpec as P

HB = 4
LEVELS = 3
LANES = 128
GROUP = 8
PANEL = 32
FIRST_EIGHTHS = 5
ROWS_A_STEP = 4
VMEM_LIMIT = 20 * 1024 * 1024
VMEM_NEAR = 48 * 1024 * 1024
F32 = jnp.float32
BF16 = jnp.bfloat16
NN = (((1,), (0,)), ((), ()))
NT = (((1,), (1,)), ((), ()))
TN = (((0,), (0,)), ((), ()))


def dot(a, b, dims):
    return lax.dot_general(a, b, dims, preferred_element_type=F32)


def split_two(x):
    high = x.astype(BF16)
    return high, (x - high.astype(F32)).astype(BF16)


def dot_split(a, b, dims):
    (a_high, a_low), (b_high, b_low) = a, b
    return dot(a_high, b_high, dims) + (dot(a_high, b_low, dims) + dot(a_low, b_high, dims))


def far_position(local, count, odd):
    lower = jnp.where(odd, 0, HB)
    below = jnp.clip(local + HB, 0, HB - 1) + lower
    above = jnp.clip(local - count, 0, HB - 1) + (HB - lower)
    return jnp.where(local < 0, below, jnp.where(local < count, 2 * HB, above))


def block_rows(place, columns, blocks, windows, emit, before=None):
    count, slots, width, _ = blocks.shape

    def body(step, carry):
        if before is not None:
            before(step)
        for rr in range(ROWS_A_STEP):
            row = step * ROWS_A_STEP + rr
            local = [columns[k, row] - place[0] * count for k in range(slots)]
            picked = []
            for window, position in windows:
                ats = [pl.multiple_of(position(at) * width, LANES) for at in local]
                picked.append(jnp.concatenate([window[:, pl.ds(at, width)] for at in ats], axis=1))
            stored = jnp.concatenate([blocks[row, k] for k in range(slots)], axis=1)
            product = dot(jnp.concatenate(picked, axis=0), stored, NT)
            emit(pl.ds(pl.multiple_of(row * width, LANES), width), product)
        return carry

    lax.fori_loop(0, count // ROWS_A_STEP, body, 0)


def prepare_kernel(at, samples, copied, first, second, arrived):
    reach = first.shape[1]
    copies = [
        pltpu.make_async_copy(samples.at[:, pl.ds(pl.multiple_of(at[0], LANES), reach)], first, arrived.at[0]),
        pltpu.make_async_copy(samples.at[:, pl.ds(pl.multiple_of(at[1], LANES), reach)], second, arrived.at[1]),
        pltpu.make_async_copy(samples, copied, arrived.at[2]),
    ]
    for copy in copies:
        copy.start()
    for copy in copies:
        copy.wait()


def fill_window(window, halos):
    own, reach = halos[0].shape
    for at in range(0, len(halos), 2):
        rows = slice(at // 2 * own, (at // 2 + 1) * own)
        window[rows, :reach] = halos[at][...]
        window[rows, reach : 2 * reach] = halos[at + 1][...]
    window[:, 2 * reach :] = jnp.zeros((window.shape[0], window.shape[1] - 2 * reach), BF16)


def far_pick(place, blocks, window):
    odd = lax.rem(place[0], 2) == 1
    count = blocks.shape[0]
    return window, lambda local: far_position(local, count, odd)


def own_kernel(
    place, columns, blocks_hbm, samples, first, second,
    products, blocks, z_high, z_low, gram, near_window, far_window, sums, arrived, leaving,
):
    count, _, width, _ = blocks.shape
    own = samples.shape[0]

    def chunk(step):
        rows = pl.ds(step * ROWS_A_STEP, ROWS_A_STEP)
        return pltpu.make_async_copy(blocks_hbm.at[rows], blocks.at[rows], arrived.at[step])

    for step in range(count // ROWS_A_STEP):
        chunk(step).start()
    near_window[:, : samples.shape[1]] = samples[...]
    near_window[:, samples.shape[1] :] = jnp.zeros((own, width), BF16)
    fill_window(far_window, (first, second))

    def near_position(local):
        return jnp.where((local >= 0) & (local < count), local, count)

    def emit(lanes, both):
        remote = both[own:]
        sums[:, lanes] = both[:own] + remote
        z_high[:, lanes], z_low[:, lanes] = split_two(remote)

    windows = [(near_window, near_position), far_pick(place, blocks, far_window)]
    block_rows(place, columns, blocks, windows, emit, lambda step: chunk(step).wait())
    leave = pltpu.make_async_copy(sums, products, leaving)
    leave.start()
    halves = z_high[...], z_low[...]
    gram[...] = dot_split(halves, halves, NT)
    leave.wait()


def others_kernel(parts, place, columns, blocks, *refs):
    halos = refs[: 2 * (parts - 1)]
    own_high, own_low, own_gram, z_high, z_low, packed, window, full = refs[2 * (parts - 1) :]
    own = own_high.shape[0]
    fill_window(window, halos)

    def emit(lanes, remote):
        z_high[:, lanes], z_low[:, lanes] = split_two(remote)

    block_rows(place, columns, blocks, [far_pick(place, blocks, window)], emit)
    high, low = z_high[...], z_low[...]
    all_high = jnp.concatenate([own_high[...], high], axis=0)
    all_low = jnp.concatenate([own_low[...], low], axis=0)
    gram_rows = dot_split((high, low), (all_high, all_low), NT)
    full[:own, :own] = own_gram[...]
    full[own:, :] = gram_rows
    full[:own, own:] = gram_rows[:, :own].T
    shift = place[1] * own
    pack_symmetric(packed, pltpu.roll(pltpu.roll(full[...], shift, 0), shift, 1))


def square_iota(n):
    return lax.broadcasted_iota(jnp.int32, (n, n), 0), lax.broadcasted_iota(jnp.int32, (n, n), 1)


def pack_symmetric(packed, full):
    h = full.shape[0] // 2
    row, col = square_iota(h)
    first = full[:h, :h]
    packed[:h, :] = full[:h, h:]
    packed[h : 2 * h, :] = jnp.where(row > col, first, full[h:, h:])
    diagonal = jnp.sum(jnp.where(row == col, first, 0.0), axis=0, keepdims=True)
    packed[2 * h :, :] = jnp.broadcast_to(diagonal, (GROUP, h))


def largest(packed):
    h = packed.shape[1]
    row, col = square_iota(h)
    on_diagonal = jnp.where(row == col, packed[h : 2 * h, :], 0.0)
    rows = jnp.maximum(jnp.max(on_diagonal, axis=0, keepdims=True), packed[2 * h : 2 * h + 1, :])
    return jnp.max(rows, axis=1, keepdims=True)


def unpack_symmetric(packed, full, b):
    h = packed.shape[1]
    row, col = square_iota(h)
    over = 1.0 / largest(packed)
    shared = packed[h : 2 * h, :] * over
    lower = jnp.where(row > col, shared, 0.0)
    diagonal = jnp.where(row == col, jnp.broadcast_to(packed[2 * h : 2 * h + 1, :] * over, (h, h)), 0.0)
    upper = jnp.where(row <= col, shared, 0.0)
    full[b, :h, :h] = lower + lower.T + diagonal
    full[b, h:, h:] = upper + jnp.where(row < col, upper, 0.0).T
    full[b, :h, h:] = packed[:h, :] * over


def row_of(x, j):
    return jnp.broadcast_to(x[:, j : j + 1, :], x.shape)


def start_inverse(m):
    batch, n, _ = m.shape
    row, col = square_iota(LANES)
    for b in range(batch):
        for c in range(0, n, LANES):
            for e in range(0, n, LANES):
                m[b, c : c + LANES, e : e + LANES] = (
                    (row == col).astype(F32) if e == c else jnp.zeros((LANES, LANES), F32)
                )


def clear_lower(a):
    batch, n, _ = a.shape
    for b in range(batch):
        for c in range(LANES, n, LANES):
            a[b, c : c + LANES, :c] = jnp.zeros((LANES, c), F32)


def factor(a, m, first, last):
    batch, n, _ = a.shape
    groups = PANEL // GROUP
    tile = (batch, GROUP, LANES)
    sub = lax.broadcasted_iota(jnp.int32, tile, 1)
    lane = lax.broadcasted_iota(jnp.int32, tile, 2)

    def panel(p, ch):
        at = p - ch * LANES
        parts = [(a, slice(ch * LANES, (ch + 1) * LANES)), (m, slice(ch * LANES, (ch + 1) * LANES))]
        rows = [pl.ds(pl.multiple_of(p + GROUP * g, GROUP), GROUP) for g in range(groups)]
        r = [[ref[:, rows[g], lanes] for ref, lanes in parts] for g in range(groups)]
        for g in range(groups):
            r[g][0] = turn(r[g][0], lax.rem(LANES - at, LANES))
        for g0 in range(groups):
            base = GROUP * g0
            v = [
                [jnp.broadcast_to(r[g][0][:, :, base + k : base + k + 1], tile) for k in range(GROUP)]
                if g >= g0
                else None
                for g in range(groups)
            ]
            head, top = v[g0], r[g0]
            steps, leading = [], [None] * len(top)
            pivots = cross = dets = None
            for j in range(0, GROUP, 2):
                p00, p10, p11 = row_of(head[j], j), row_of(head[j], j + 1), row_of(head[j + 1], j + 1)
                det = p00 * p11 - p10 * p10
                guess = pl.reciprocal(det, approx=True)
                refine = 2.0 - det * guess
                later = range(j + 2, GROUP)
                v_rows = {k: (row_of(head[k], j), row_of(head[k], j + 1)) for k in later}
                r_rows = [(row_of(x, j), row_of(x, j + 1)) for x in top]
                here = sub >= j
                pivots = p00 if j == 0 else jnp.where(here, p00, pivots)
                cross = p10 if j == 0 else jnp.where(here, p10, cross)
                dets = det if j == 0 else jnp.where(here, det, dets)
                leading = [x0 if j == 0 else jnp.where(here, x0, old) for (x0, _), old in zip(r_rows, leading)]
                c0 = jnp.where(sub > j + 1, head[j], 0.0)
                c1 = jnp.where(sub > j + 1, head[j + 1], 0.0)
                for k in later[:2]:
                    x0, x1 = v_rows[k]
                    term = c0 * (p11 * x0 - p10 * x1) + c1 * (p00 * x1 - p10 * x0)
                    head[k] = head[k] - (term * guess) * refine
                inverse = guess * refine
                q00, q10, q11 = p11 * inverse, p10 * inverse, p00 * inverse
                steps.append((j, q00, q10, q11, v_rows, r_rows))
                if j + 2 < GROUP:
                    w0, w1 = c0 * q00 - c1 * q10, c1 * q11 - c0 * q10
                    for k in later[2:]:
                        head[k] = head[k] - w0 * v_rows[k][0] - w1 * v_rows[k][1]
                    for x in range(len(top)):
                        top[x] = top[x] - w0 * r_rows[x][0] - w1 * r_rows[x][1]
            for g in range(g0 + 1, groups):
                for j, q00, q10, q11, v_rows, r_rows in steps:
                    c0, c1 = v[g][j], v[g][j + 1]
                    w0, w1 = c0 * q00 - c1 * q10, c1 * q11 - c0 * q10
                    for k in range(j + 2, GROUP):
                        v[g][k] = v[g][k] - w0 * v_rows[k][0] - w1 * v_rows[k][1]
                    for x in range(len(top)):
                        r[g][x] = r[g][x] - w0 * r_rows[x][0] - w1 * r_rows[x][1]
            second_row = sub % 2 == 1
            over = invert(pivots)
            ratio = jnp.where(second_row, cross * over, 0.0)
            scale = lax.rsqrt(jnp.where(second_row, dets * over, pivots))
            for x, (ref, lanes) in enumerate(parts):
                done = (top[x] - ratio * leading[x]) * scale
                if x == 0:
                    done = jnp.where(lane >= sub + (at + base), turn(done, at), 0.0)
                r[g0][x] = done
                ref[:, rows[g0], lanes] = done
        for b in range(batch):
            wide = jnp.concatenate(
                [jnp.concatenate([r[g][x][b] for g in range(groups)], axis=0) for x in range(len(parts))], axis=1
            )
            high, low = split_two(wide)
            left = jnp.concatenate([high[:, :LANES], high[:, :LANES], low[:, :LANES]], axis=0)
            right = jnp.concatenate([high, low, high], axis=0)
            update = dot(left, right, TN)
            below = lax.broadcasted_iota(jnp.int32, (LANES, LANES), 0) >= at + PANEL
            for x, (ref, lanes) in enumerate(parts):
                rest = ref[b, lanes, lanes]
                ref[b, lanes, lanes] = rest - jnp.where(below, update[:, x * LANES : (x + 1) * LANES], 0.0)

    for ch in range(first // LANES, -(-last // LANES)):
        start, stop = max(first, ch * LANES), min(last, (ch + 1) * LANES)

        def step(i, carry, start=start, ch=ch):
            panel(pl.multiple_of(start + i * PANEL, PANEL), ch)
            return carry

        lax.fori_loop(0, (stop - start) // PANEL, step, 0)
        if stop == (ch + 1) * LANES:
            join_chunks(a, m, ch)


def turn(x, shift):
    return pltpu.roll(x.reshape(-1, x.shape[-1]), shift, 1).reshape(x.shape)


def join_chunks(a, m, ch):
    batch, n, _ = a.shape
    here = slice(ch * LANES, (ch + 1) * LANES)
    for b in range(batch):
        inverse = split_two(m[b, here, here])
        if ch > 0:
            before = slice(0, ch * LANES)
            m[b, here, before] = -dot_split(inverse, split_two(m[b, here, before]), NN)
        later = slice((ch + 1) * LANES, n)
        if later.start == n:
            continue
        upper = dot_split(inverse, split_two(a[b, here, later]), NN)
        a[b, here, later] = upper
        upper = split_two(upper)
        done = split_two(m[b, here, : (ch + 1) * LANES])
        both = tuple(jnp.concatenate(pair, axis=1) for pair in zip(upper, done))
        update = dot_split(upper, both, TN)
        a[b, later, later] = a[b, later, later] - update[:, : n - later.start]
        m[b, later, : later.start] = m[b, later, : later.start] + update[:, n - later.start :]


def invert(x):
    guess = pl.reciprocal(x, approx=True)
    return guess * (2.0 - x * guess)


def own_rows(place, own):
    return pl.ds(pl.multiple_of(place[1] * own, own), own)


def first_kernel(stop, packed_zero, packed_one, a, m):
    unpack_symmetric(packed_zero, a, 0)
    unpack_symmetric(packed_one, a, 1)
    start_inverse(m)
    factor(a, m, 0, stop)


def second_kernel(start, scale, place, packed_zero, packed_one, a_in, m_in, own_high, own_low, rest_high, rest_low,
                  bases, transfer, upper_own, a, m):
    del a_in, m_in
    n = a.shape[1]
    factor(a, m, start, n)
    clear_lower(a)
    own = upper_own.shape[0]
    rows = own_rows(place, own)
    size_zero, size_one = largest(packed_zero), largest(packed_one)
    upper_own[...] = a[1, rows, :] * jnp.sqrt(size_one)
    child = a[0, rows, :] * (jnp.sqrt(size_zero) * lax.rsqrt(size_one))
    transfer[...] = dot_split(split_two(m[1]), split_two(child), NT)
    turned = pltpu.roll(m[0, rows, :] * (lax.rsqrt(size_zero) * scale), lax.rem(n - place[1] * own, n), 1)
    inverse = split_two(turned)
    for c in range(0, own_high.shape[1], 512):
        lanes = slice(c, c + 512)
        high = jnp.concatenate([own_high[:, lanes], rest_high[:, lanes]], axis=0)
        low = jnp.concatenate([own_low[:, lanes], rest_low[:, lanes]], axis=0)
        bases[:, lanes] = dot_split(inverse, (high, low), NN)


def tree_kernel(top_scale, place, upper_own, *refs):
    levels = (len(refs) - 3) // 2
    packed = refs[:levels]
    transfers = refs[levels : 2 * levels]
    top, a, m = refs[2 * levels :]
    for b in range(levels):
        unpack_symmetric(packed[b], a, b)
    start_inverse(m)
    factor(a, m, 0, a.shape[1])
    clear_lower(a)
    own = upper_own.shape[0]
    rows = own_rows(place, own)
    sizes = [largest(ref) for ref in packed]
    child = upper_own[...]
    for b in range(levels):
        child = child * lax.rsqrt(sizes[b])
        transfers[b][...] = dot_split(split_two(m[b]), split_two(child), NT)
        child = a[b, rows, :] * jnp.sqrt(sizes[b])
    top[...] = (child * top_scale).T


def whole():
    return pl.BlockSpec(memory_space=pltpu.VMEM)


def params(limit=VMEM_LIMIT):
    return pltpu.CompilerParams(vmem_limit_bytes=limit)


def from_partner(block, axis, bit):
    count = lax.axis_size(axis)
    route = []
    for low in range(count):
        high = low | 1 << bit
        if high != low and high < count:
            route += [(low, high), (high, low)]
    return lax.ppermute(block, axis, route)


def swap_across(block, odd_start):
    count = lax.axis_size("leaf")
    route = []
    for low in range(odd_start, count - 1, 2):
        route += [(low, low + 1), (low + 1, low)]
    return lax.ppermute(block, "leaf", route)


def sample_shift(block, d):
    count = lax.axis_size("samp")
    return lax.ppermute(block, "samp", [(i, (i - d) % count) for i in range(count)])


def shards(stiffness, columns, samples):
    blocks_here, slots, width, _ = stiffness.shape
    own, row_count = samples.shape
    parts = lax.axis_size("samp")
    total = own * parts
    reach = HB * width
    leaf = lax.axis_index("leaf")
    place = jnp.stack([leaf, lax.axis_index("samp")]).astype(jnp.int32)
    shape = jax.ShapeDtypeStruct
    columns = columns.T

    smem = pl.BlockSpec(memory_space=pltpu.SMEM)
    hbm = pl.BlockSpec(memory_space=pltpu.HBM)
    rest = total - own
    window_lanes = 2 * reach + width
    far_end = row_count - reach
    odd = lax.rem(leaf, 2)
    reach_shape = shape((own, reach), BF16)
    samples, first, second = pl.pallas_call(
        prepare_kernel,
        in_specs=[smem, hbm],
        out_specs=[whole()] * 3,
        out_shape=[shape(samples.shape, BF16), reach_shape, reach_shape],
        scratch_shapes=[pltpu.SemaphoreType.DMA((3,))],
        compiler_params=params(VMEM_NEAR),
        name="prepare",
    )(jnp.stack([far_end * (1 - odd), far_end * odd]).astype(jnp.int32), samples)

    halos = [swap_across(first, 0), swap_across(second, 1)]
    other_halos = [sample_shift(halo, d) for d in range(1, parts) for halo in halos]

    products, blocks, own_high, own_low, own_gram = pl.pallas_call(
        own_kernel,
        in_specs=[smem, smem, hbm] + [whole()] * 3,
        out_specs=[hbm] + [whole()] * 4,
        out_shape=[
            shape((own, row_count), F32),
            shape(stiffness.shape, BF16),
            shape((own, row_count), BF16),
            shape((own, row_count), BF16),
            shape((own, own), F32),
        ],
        scratch_shapes=[
            pltpu.VMEM((own, row_count + width), BF16),
            pltpu.VMEM((own, window_lanes), BF16),
            pltpu.VMEM((own, row_count), F32),
            pltpu.SemaphoreType.DMA((blocks_here // ROWS_A_STEP,)),
            pltpu.SemaphoreType.DMA,
        ],
        compiler_params=params(VMEM_NEAR),
        cost_estimate=pl.CostEstimate(
            flops=4 * own * slots * width * row_count, bytes_accessed=6 * 1024 * 1024, transcendentals=0
        ),
        name="own",
    )(place, columns, stiffness, samples, *halos)

    packed_shape = (total + GROUP, total // 2)
    rest_high, rest_low, packed = pl.pallas_call(
        functools.partial(others_kernel, parts),
        in_specs=[smem, smem] + [whole()] * (2 * parts + 2),
        out_specs=[whole()] * 3,
        out_shape=[shape((rest, row_count), BF16), shape((rest, row_count), BF16), shape(packed_shape, F32)],
        scratch_shapes=[pltpu.VMEM((rest, window_lanes), BF16), pltpu.VMEM((total, total), F32)],
        compiler_params=params(),
        name="others",
    )(place, columns, blocks, *other_halos, own_high, own_low, own_gram)

    square = shape((2, total, total), F32)
    split_row = total * FIRST_EIGHTHS // 8 // PANEL * PANEL
    transfer_shape = shape((total, own), F32)
    gram_one = packed + from_partner(packed, "leaf", 0)
    gram_two = gram_one + from_partner(gram_one, "leaf", 1)
    a, m = pl.pallas_call(
        functools.partial(first_kernel, split_row),
        in_specs=[whole()] * 2,
        out_specs=[whole()] * 2,
        out_shape=[square] * 2,
        compiler_params=params(),
        cost_estimate=pl.CostEstimate(flops=3 * 10**9, bytes_accessed=1024 * 1024, transcendentals=0),
        name="first",
    )(packed, gram_one)
    gram_three = gram_two + from_partner(gram_two, "leaf", 2)
    bases, transfer_one, upper_own, _, _ = pl.pallas_call(
        functools.partial(second_kernel, split_row, math.sqrt(row_count)),
        in_specs=[smem] + [whole()] * 8,
        out_specs=[whole()] * 5,
        out_shape=[shape((own, row_count), F32), transfer_shape, shape((own, total), F32), square, square],
        input_output_aliases={3: 3, 4: 4},
        compiler_params=params(),
        cost_estimate=pl.CostEstimate(flops=3 * 10**9, bytes_accessed=1024 * 1024, transcendentals=0),
        name="second",
    )(place, packed, gram_one, a, m, own_high, own_low, rest_high, rest_low)
    transfer_two, transfer_three, top_factor = pl.pallas_call(
        functools.partial(tree_kernel, 1.0 / math.sqrt(2**LEVELS * row_count)),
        in_specs=[smem] + [whole()] * 3,
        out_specs=[whole()] * 3,
        out_shape=[transfer_shape] * 3,
        scratch_shapes=[pltpu.VMEM((2, total, total), F32)] * 2,
        compiler_params=params(),
        name="tree",
    )(place, upper_own, gram_two, gram_three)
    return (products, bases, transfer_one, transfer_two, transfer_three, top_factor)


def solution(mesh):
    return jax.shard_map(
        shards,
        mesh=mesh,
        in_specs=(P("leaf", None, None, None), P("leaf", None), P("samp", "leaf")),
        out_specs=(
            P("samp", "leaf"),
            P("samp", "leaf"),
            P("leaf", "samp"),
            P("leaf", "samp"),
            P("leaf", "samp"),
            P("leaf", "samp"),
        ),
        check_vma=False,
    )
```

```python
import functools
import math

import jax
import jax.numpy as jnp
from jax import lax
from jax.experimental import pallas as pl
from jax.experimental.pallas import tpu as pltpu
from jax.sharding import PartitionSpec as P

HB = 4
LEVELS = 3
LANES = 128
GROUP = 8
PANEL = 16
FIRST_EIGHTHS = 5
ROWS_A_STEP = 4
VMEM_LIMIT = 20 * 1024 * 1024
VMEM_NEAR = 48 * 1024 * 1024
F32 = jnp.float32
BF16 = jnp.bfloat16
NN = (((1,), (0,)), ((), ()))
NT = (((1,), (1,)), ((), ()))
TN = (((0,), (0,)), ((), ()))


def dot(a, b, dims):
    return lax.dot_general(a, b, dims, preferred_element_type=F32)


def split_two(x):
    high = x.astype(BF16)
    return high, (x - high.astype(F32)).astype(BF16)


def dot_split(a, b, dims):
    (a_high, a_low), (b_high, b_low) = a, b
    return dot(a_high, b_high, dims) + (dot(a_high, b_low, dims) + dot(a_low, b_high, dims))


def far_position(local, count, odd):
    lower = jnp.where(odd, 0, HB)
    below = jnp.clip(local + HB, 0, HB - 1) + lower
    above = jnp.clip(local - count, 0, HB - 1) + (HB - lower)
    return jnp.where(local < 0, below, jnp.where(local < count, 2 * HB, above))


def block_rows(place, columns, blocks, windows, emit, before=None):
    count, slots, width, _ = blocks.shape

    def body(step, carry):
        if before is not None:
            before(step)
        for rr in range(ROWS_A_STEP):
            row = step * ROWS_A_STEP + rr
            local = [columns[k, row] - place[0] * count for k in range(slots)]
            picked = []
            for window, position in windows:
                ats = [pl.multiple_of(position(at) * width, LANES) for at in local]
                picked.append(jnp.concatenate([window[:, pl.ds(at, width)] for at in ats], axis=1))
            stored = jnp.concatenate([blocks[row, k] for k in range(slots)], axis=1)
            product = dot(jnp.concatenate(picked, axis=0), stored, NT)
            emit(pl.ds(pl.multiple_of(row * width, LANES), width), product)
        return carry

    lax.fori_loop(0, count // ROWS_A_STEP, body, 0)


def prepare_kernel(at, samples, copied, first, second, arrived):
    reach = first.shape[1]
    copies = [
        pltpu.make_async_copy(samples.at[:, pl.ds(pl.multiple_of(at[0], LANES), reach)], first, arrived.at[0]),
        pltpu.make_async_copy(samples.at[:, pl.ds(pl.multiple_of(at[1], LANES), reach)], second, arrived.at[1]),
        pltpu.make_async_copy(samples, copied, arrived.at[2]),
    ]
    for copy in copies:
        copy.start()
    for copy in copies:
        copy.wait()


def fill_window(window, halos):
    own, reach = halos[0].shape
    for at in range(0, len(halos), 2):
        rows = slice(at // 2 * own, (at // 2 + 1) * own)
        window[rows, :reach] = halos[at][...]
        window[rows, reach : 2 * reach] = halos[at + 1][...]
    window[:, 2 * reach :] = jnp.zeros((window.shape[0], window.shape[1] - 2 * reach), BF16)


def far_pick(place, blocks, window):
    odd = lax.rem(place[0], 2) == 1
    count = blocks.shape[0]
    return window, lambda local: far_position(local, count, odd)


def own_kernel(
    place, columns, blocks_hbm, samples, first, second,
    products, blocks, z_high, z_low, gram, near_window, far_window, sums, arrived, leaving,
):
    count, _, width, _ = blocks.shape
    own = samples.shape[0]

    def chunk(step):
        rows = pl.ds(step * ROWS_A_STEP, ROWS_A_STEP)
        return pltpu.make_async_copy(blocks_hbm.at[rows], blocks.at[rows], arrived.at[step])

    for step in range(count // ROWS_A_STEP):
        chunk(step).start()
    near_window[:, : samples.shape[1]] = samples[...]
    near_window[:, samples.shape[1] :] = jnp.zeros((own, width), BF16)
    fill_window(far_window, (first, second))

    def near_position(local):
        return jnp.where((local >= 0) & (local < count), local, count)

    def emit(lanes, both):
        remote = both[own:]
        sums[:, lanes] = both[:own] + remote
        z_high[:, lanes], z_low[:, lanes] = split_two(remote)

    windows = [(near_window, near_position), far_pick(place, blocks, far_window)]
    block_rows(place, columns, blocks, windows, emit, lambda step: chunk(step).wait())
    leave = pltpu.make_async_copy(sums, products, leaving)
    leave.start()
    halves = z_high[...], z_low[...]
    gram[...] = dot_split(halves, halves, NT)
    leave.wait()


def others_kernel(parts, place, columns, blocks, *refs):
    halos = refs[: 2 * (parts - 1)]
    own_high, own_low, own_gram, z_high, z_low, packed, window, full = refs[2 * (parts - 1) :]
    own = own_high.shape[0]
    fill_window(window, halos)

    def emit(lanes, remote):
        z_high[:, lanes], z_low[:, lanes] = split_two(remote)

    block_rows(place, columns, blocks, [far_pick(place, blocks, window)], emit)
    high, low = z_high[...], z_low[...]
    all_high = jnp.concatenate([own_high[...], high], axis=0)
    all_low = jnp.concatenate([own_low[...], low], axis=0)
    gram_rows = dot_split((high, low), (all_high, all_low), NT)
    full[:own, :own] = own_gram[...]
    full[own:, :] = gram_rows
    full[:own, own:] = gram_rows[:, :own].T
    shift = place[1] * own
    pack_symmetric(packed, pltpu.roll(pltpu.roll(full[...], shift, 0), shift, 1))


def square_iota(n):
    return lax.broadcasted_iota(jnp.int32, (n, n), 0), lax.broadcasted_iota(jnp.int32, (n, n), 1)


def pack_symmetric(packed, full):
    h = full.shape[0] // 2
    row, col = square_iota(h)
    first = full[:h, :h]
    packed[:h, :] = full[:h, h:]
    packed[h : 2 * h, :] = jnp.where(row > col, first, full[h:, h:])
    diagonal = jnp.sum(jnp.where(row == col, first, 0.0), axis=0, keepdims=True)
    packed[2 * h :, :] = jnp.broadcast_to(diagonal, (GROUP, h))


def largest(packed):
    h = packed.shape[1]
    row, col = square_iota(h)
    on_diagonal = jnp.where(row == col, packed[h : 2 * h, :], 0.0)
    rows = jnp.maximum(jnp.max(on_diagonal, axis=0, keepdims=True), packed[2 * h : 2 * h + 1, :])
    return jnp.max(rows, axis=1, keepdims=True)


def unpack_symmetric(packed, full, b):
    h = packed.shape[1]
    row, col = square_iota(h)
    over = 1.0 / largest(packed)
    shared = packed[h : 2 * h, :] * over
    lower = jnp.where(row > col, shared, 0.0)
    diagonal = jnp.where(row == col, jnp.broadcast_to(packed[2 * h : 2 * h + 1, :] * over, (h, h)), 0.0)
    upper = jnp.where(row <= col, shared, 0.0)
    full[b, :h, :h] = lower + lower.T + diagonal
    full[b, h:, h:] = upper + jnp.where(row < col, upper, 0.0).T
    full[b, :h, h:] = packed[:h, :] * over


def row_of(x, j):
    return jnp.broadcast_to(x[:, j : j + 1, :], x.shape)


def start_inverse(m):
    batch, n, _ = m.shape
    row, col = square_iota(LANES)
    for b in range(batch):
        for c in range(0, n, LANES):
            for e in range(0, n, LANES):
                m[b, c : c + LANES, e : e + LANES] = (
                    (row == col).astype(F32) if e == c else jnp.zeros((LANES, LANES), F32)
                )


def clear_lower(a):
    batch, n, _ = a.shape
    for b in range(batch):
        for c in range(LANES, n, LANES):
            a[b, c : c + LANES, :c] = jnp.zeros((LANES, c), F32)


def factor(a, m, first, last):
    batch, n, _ = a.shape
    groups = PANEL // GROUP
    tile = (batch, GROUP, LANES)
    sub = lax.broadcasted_iota(jnp.int32, tile, 1)
    lane = lax.broadcasted_iota(jnp.int32, tile, 2)
    for p in range(first, last, PANEL):
        ch = p // LANES
        parts = [(a, ch), (m, ch)]
        rows = [slice(p + GROUP * g, p + GROUP * (g + 1)) for g in range(groups)]
        r = [[ref[:, rows[g], c * LANES : (c + 1) * LANES] for ref, c in parts] for g in range(groups)]
        for g0 in range(groups):
            at = p - ch * LANES + GROUP * g0
            v = [
                [jnp.broadcast_to(r[g][0][:, :, at + k : at + k + 1], tile) for k in range(GROUP)]
                if g >= g0
                else None
                for g in range(groups)
            ]
            head, top = v[g0], r[g0]
            steps, leading = [], [None] * len(top)
            pivots = cross = dets = None
            for j in range(0, GROUP, 2):
                p00, p10, p11 = row_of(head[j], j), row_of(head[j], j + 1), row_of(head[j + 1], j + 1)
                det = p00 * p11 - p10 * p10
                guess = pl.reciprocal(det, approx=True)
                refine = 2.0 - det * guess
                later = range(j + 2, GROUP)
                v_rows = {k: (row_of(head[k], j), row_of(head[k], j + 1)) for k in later}
                r_rows = [(row_of(x, j), row_of(x, j + 1)) for x in top]
                here = sub >= j
                pivots = p00 if j == 0 else jnp.where(here, p00, pivots)
                cross = p10 if j == 0 else jnp.where(here, p10, cross)
                dets = det if j == 0 else jnp.where(here, det, dets)
                leading = [x0 if j == 0 else jnp.where(here, x0, old) for (x0, _), old in zip(r_rows, leading)]
                c0 = jnp.where(sub > j + 1, head[j], 0.0)
                c1 = jnp.where(sub > j + 1, head[j + 1], 0.0)
                for k in later[:2]:
                    x0, x1 = v_rows[k]
                    term = c0 * (p11 * x0 - p10 * x1) + c1 * (p00 * x1 - p10 * x0)
                    head[k] = head[k] - (term * guess) * refine
                inverse = guess * refine
                q00, q10, q11 = p11 * inverse, p10 * inverse, p00 * inverse
                steps.append((j, q00, q10, q11, v_rows, r_rows))
                if j + 2 < GROUP:
                    w0, w1 = c0 * q00 - c1 * q10, c1 * q11 - c0 * q10
                    for k in later[2:]:
                        head[k] = head[k] - w0 * v_rows[k][0] - w1 * v_rows[k][1]
                    for x in range(len(top)):
                        top[x] = top[x] - w0 * r_rows[x][0] - w1 * r_rows[x][1]
            for g in range(g0 + 1, groups):
                for j, q00, q10, q11, v_rows, r_rows in steps:
                    c0, c1 = v[g][j], v[g][j + 1]
                    w0, w1 = c0 * q00 - c1 * q10, c1 * q11 - c0 * q10
                    for k in range(j + 2, GROUP):
                        v[g][k] = v[g][k] - w0 * v_rows[k][0] - w1 * v_rows[k][1]
                    for x in range(len(top)):
                        r[g][x] = r[g][x] - w0 * r_rows[x][0] - w1 * r_rows[x][1]
            second_row = sub % 2 == 1
            over = invert(pivots)
            ratio = jnp.where(second_row, cross * over, 0.0)
            scale = lax.rsqrt(jnp.where(second_row, dets * over, pivots))
            for x, (ref, c) in enumerate(parts):
                done = (top[x] - ratio * leading[x]) * scale
                if ref is a and c == ch:
                    done = jnp.where(lane >= sub + at, done, 0.0)
                r[g0][x] = done
                ref[:, rows[g0], c * LANES : (c + 1) * LANES] = done
        end = (ch + 1) * LANES
        if p + PANEL == end:
            join_chunks(a, m, ch)
            continue
        for b in range(batch):
            panel = jnp.concatenate(
                [jnp.concatenate([r[g][x][b] for g in range(groups)], axis=0) for x in range(len(parts))], axis=1
            )
            high, low = split_two(panel)
            left = jnp.concatenate([high[:, :LANES], high[:, :LANES], low[:, :LANES]], axis=0)
            right = jnp.concatenate([high, low, high], axis=0)
            update = dot(left, right, TN)[p + PANEL - ch * LANES :, :]
            for x, (ref, e) in enumerate(parts):
                lanes = slice(e * LANES, (e + 1) * LANES)
                ref[b, p + PANEL : end, lanes] = ref[b, p + PANEL : end, lanes] - update[:, x * LANES : (x + 1) * LANES]


def join_chunks(a, m, ch):
    batch, n, _ = a.shape
    here = slice(ch * LANES, (ch + 1) * LANES)
    for b in range(batch):
        inverse = split_two(m[b, here, here])
        if ch > 0:
            before = slice(0, ch * LANES)
            m[b, here, before] = -dot_split(inverse, split_two(m[b, here, before]), NN)
        later = slice((ch + 1) * LANES, n)
        if later.start == n:
            continue
        upper = dot_split(inverse, split_two(a[b, here, later]), NN)
        a[b, here, later] = upper
        upper = split_two(upper)
        done = split_two(m[b, here, : (ch + 1) * LANES])
        both = tuple(jnp.concatenate(pair, axis=1) for pair in zip(upper, done))
        update = dot_split(upper, both, TN)
        a[b, later, later] = a[b, later, later] - update[:, : n - later.start]
        m[b, later, : later.start] = m[b, later, : later.start] + update[:, n - later.start :]


def invert(x):
    guess = pl.reciprocal(x, approx=True)
    return guess * (2.0 - x * guess)


def own_rows(place, own):
    return pl.ds(pl.multiple_of(place[1] * own, own), own)


def first_kernel(stop, packed_zero, packed_one, a, m):
    unpack_symmetric(packed_zero, a, 0)
    unpack_symmetric(packed_one, a, 1)
    start_inverse(m)
    factor(a, m, 0, stop)


def second_kernel(start, scale, place, packed_zero, packed_one, a_in, m_in, own_high, own_low, rest_high, rest_low,
                  bases, transfer, upper_own, a, m):
    del a_in, m_in
    n = a.shape[1]
    factor(a, m, start, n)
    clear_lower(a)
    own = upper_own.shape[0]
    rows = own_rows(place, own)
    size_zero, size_one = largest(packed_zero), largest(packed_one)
    upper_own[...] = a[1, rows, :] * jnp.sqrt(size_one)
    child = a[0, rows, :] * (jnp.sqrt(size_zero) * lax.rsqrt(size_one))
    transfer[...] = dot_split(split_two(m[1]), split_two(child), NT)
    turned = pltpu.roll(m[0, rows, :] * (lax.rsqrt(size_zero) * scale), lax.rem(n - place[1] * own, n), 1)
    inverse = split_two(turned)
    for c in range(0, own_high.shape[1], 512):
        lanes = slice(c, c + 512)
        high = jnp.concatenate([own_high[:, lanes], rest_high[:, lanes]], axis=0)
        low = jnp.concatenate([own_low[:, lanes], rest_low[:, lanes]], axis=0)
        bases[:, lanes] = dot_split(inverse, (high, low), NN)


def tree_kernel(top_scale, place, upper_own, *refs):
    levels = (len(refs) - 3) // 2
    packed = refs[:levels]
    transfers = refs[levels : 2 * levels]
    top, a, m = refs[2 * levels :]
    for b in range(levels):
        unpack_symmetric(packed[b], a, b)
    start_inverse(m)
    factor(a, m, 0, a.shape[1])
    clear_lower(a)
    own = upper_own.shape[0]
    rows = own_rows(place, own)
    sizes = [largest(ref) for ref in packed]
    child = upper_own[...]
    for b in range(levels):
        child = child * lax.rsqrt(sizes[b])
        transfers[b][...] = dot_split(split_two(m[b]), split_two(child), NT)
        child = a[b, rows, :] * jnp.sqrt(sizes[b])
    top[...] = (child * top_scale).T


def whole():
    return pl.BlockSpec(memory_space=pltpu.VMEM)


def params(limit=VMEM_LIMIT):
    return pltpu.CompilerParams(vmem_limit_bytes=limit)


def from_partner(block, axis, bit):
    count = lax.axis_size(axis)
    route = []
    for low in range(count):
        high = low | 1 << bit
        if high != low and high < count:
            route += [(low, high), (high, low)]
    return lax.ppermute(block, axis, route)


def swap_across(block, odd_start):
    count = lax.axis_size("leaf")
    route = []
    for low in range(odd_start, count - 1, 2):
        route += [(low, low + 1), (low + 1, low)]
    return lax.ppermute(block, "leaf", route)


def sample_shift(block, d):
    count = lax.axis_size("samp")
    return lax.ppermute(block, "samp", [(i, (i - d) % count) for i in range(count)])


def shards(stiffness, columns, samples):
    blocks_here, slots, width, _ = stiffness.shape
    own, row_count = samples.shape
    parts = lax.axis_size("samp")
    total = own * parts
    reach = HB * width
    leaf = lax.axis_index("leaf")
    place = jnp.stack([leaf, lax.axis_index("samp")]).astype(jnp.int32)
    shape = jax.ShapeDtypeStruct
    columns = columns.T

    smem = pl.BlockSpec(memory_space=pltpu.SMEM)
    hbm = pl.BlockSpec(memory_space=pltpu.HBM)
    rest = total - own
    window_lanes = 2 * reach + width
    far_end = row_count - reach
    odd = lax.rem(leaf, 2)
    reach_shape = shape((own, reach), BF16)
    samples, first, second = pl.pallas_call(
        prepare_kernel,
        in_specs=[smem, hbm],
        out_specs=[whole()] * 3,
        out_shape=[shape(samples.shape, BF16), reach_shape, reach_shape],
        scratch_shapes=[pltpu.SemaphoreType.DMA((3,))],
        compiler_params=params(VMEM_NEAR),
        name="prepare",
    )(jnp.stack([far_end * (1 - odd), far_end * odd]).astype(jnp.int32), samples)

    halos = [swap_across(first, 0), swap_across(second, 1)]
    other_halos = [sample_shift(halo, d) for d in range(1, parts) for halo in halos]

    products, blocks, own_high, own_low, own_gram = pl.pallas_call(
        own_kernel,
        in_specs=[smem, smem, hbm] + [whole()] * 3,
        out_specs=[hbm] + [whole()] * 4,
        out_shape=[
            shape((own, row_count), F32),
            shape(stiffness.shape, BF16),
            shape((own, row_count), BF16),
            shape((own, row_count), BF16),
            shape((own, own), F32),
        ],
        scratch_shapes=[
            pltpu.VMEM((own, row_count + width), BF16),
            pltpu.VMEM((own, window_lanes), BF16),
            pltpu.VMEM((own, row_count), F32),
            pltpu.SemaphoreType.DMA((blocks_here // ROWS_A_STEP,)),
            pltpu.SemaphoreType.DMA,
        ],
        compiler_params=params(VMEM_NEAR),
        cost_estimate=pl.CostEstimate(
            flops=4 * own * slots * width * row_count, bytes_accessed=6 * 1024 * 1024, transcendentals=0
        ),
        name="own",
    )(place, columns, stiffness, samples, *halos)

    packed_shape = (total + GROUP, total // 2)
    rest_high, rest_low, packed = pl.pallas_call(
        functools.partial(others_kernel, parts),
        in_specs=[smem, smem] + [whole()] * (2 * parts + 2),
        out_specs=[whole()] * 3,
        out_shape=[shape((rest, row_count), BF16), shape((rest, row_count), BF16), shape(packed_shape, F32)],
        scratch_shapes=[pltpu.VMEM((rest, window_lanes), BF16), pltpu.VMEM((total, total), F32)],
        compiler_params=params(),
        name="others",
    )(place, columns, blocks, *other_halos, own_high, own_low, own_gram)

    square = shape((2, total, total), F32)
    split_row = total * FIRST_EIGHTHS // 8 // PANEL * PANEL
    transfer_shape = shape((total, own), F32)
    gram_one = packed + from_partner(packed, "leaf", 0)
    gram_two = gram_one + from_partner(gram_one, "leaf", 1)
    a, m = pl.pallas_call(
        functools.partial(first_kernel, split_row),
        in_specs=[whole()] * 2,
        out_specs=[whole()] * 2,
        out_shape=[square] * 2,
        compiler_params=params(),
        cost_estimate=pl.CostEstimate(flops=3 * 10**9, bytes_accessed=1024 * 1024, transcendentals=0),
        name="first",
    )(packed, gram_one)
    gram_three = gram_two + from_partner(gram_two, "leaf", 2)
    bases, transfer_one, upper_own, _, _ = pl.pallas_call(
        functools.partial(second_kernel, split_row, math.sqrt(row_count)),
        in_specs=[smem] + [whole()] * 8,
        out_specs=[whole()] * 5,
        out_shape=[shape((own, row_count), F32), transfer_shape, shape((own, total), F32), square, square],
        input_output_aliases={3: 3, 4: 4},
        compiler_params=params(),
        cost_estimate=pl.CostEstimate(flops=3 * 10**9, bytes_accessed=1024 * 1024, transcendentals=0),
        name="second",
    )(place, packed, gram_one, a, m, own_high, own_low, rest_high, rest_low)
    transfer_two, transfer_three, top_factor = pl.pallas_call(
        functools.partial(tree_kernel, 1.0 / math.sqrt(2**LEVELS * row_count)),
        in_specs=[smem] + [whole()] * 3,
        out_specs=[whole()] * 3,
        out_shape=[transfer_shape] * 3,
        scratch_shapes=[pltpu.VMEM((2, total, total), F32)] * 2,
        compiler_params=params(),
        name="tree",
    )(place, upper_own, gram_two, gram_three)
    return (products, bases, transfer_one, transfer_two, transfer_three, top_factor)


def solution(mesh):
    return jax.shard_map(
        shards,
        mesh=mesh,
        in_specs=(P("leaf", None, None, None), P("leaf", None), P("samp", "leaf")),
        out_specs=(
            P("samp", "leaf"),
            P("samp", "leaf"),
            P("leaf", "samp"),
            P("leaf", "samp"),
            P("leaf", "samp"),
            P("leaf", "samp"),
        ),
        check_vma=False,
    )
```

```python
import functools
import math

import jax
import jax.numpy as jnp
from jax import lax
from jax.experimental import pallas as pl
from jax.experimental.pallas import tpu as pltpu
from jax.sharding import PartitionSpec as P

HB = 4
LEVELS = 3
LANES = 128
GROUP = 8
PANEL = 16
FIRST_EIGHTHS = 5
ROWS_A_STEP = 4
VMEM_LIMIT = 20 * 1024 * 1024
VMEM_NEAR = 48 * 1024 * 1024
F32 = jnp.float32
BF16 = jnp.bfloat16
NN = (((1,), (0,)), ((), ()))
NT = (((1,), (1,)), ((), ()))
TN = (((0,), (0,)), ((), ()))


def dot(a, b, dims):
    return lax.dot_general(a, b, dims, preferred_element_type=F32)


def split_two(x):
    high = x.astype(BF16)
    return high, (x - high.astype(F32)).astype(BF16)


def dot_split(a, b, dims):
    (a_high, a_low), (b_high, b_low) = a, b
    return dot(a_high, b_high, dims) + (dot(a_high, b_low, dims) + dot(a_low, b_high, dims))


def far_position(local, count, odd):
    lower = jnp.where(odd, 0, HB)
    below = jnp.clip(local + HB, 0, HB - 1) + lower
    above = jnp.clip(local - count, 0, HB - 1) + (HB - lower)
    return jnp.where(local < 0, below, jnp.where(local < count, 2 * HB, above))


def block_rows(place, columns, blocks, windows, emit, before=None):
    count, slots, width, _ = blocks.shape

    def body(step, carry):
        if before is not None:
            before(step)
        for rr in range(ROWS_A_STEP):
            row = step * ROWS_A_STEP + rr
            local = [columns[k, row] - place[0] * count for k in range(slots)]
            picked = []
            for window, position in windows:
                ats = [pl.multiple_of(position(at) * width, LANES) for at in local]
                picked.append(jnp.concatenate([window[:, pl.ds(at, width)] for at in ats], axis=1))
            stored = jnp.concatenate([blocks[row, k] for k in range(slots)], axis=1)
            product = dot(jnp.concatenate(picked, axis=0), stored, NT)
            emit(pl.ds(pl.multiple_of(row * width, LANES), width), product)
        return carry

    lax.fori_loop(0, count // ROWS_A_STEP, body, 0)


def prepare_kernel(at, samples, copied, first, second, arrived):
    reach = first.shape[1]
    copies = [
        pltpu.make_async_copy(samples.at[:, pl.ds(pl.multiple_of(at[0], LANES), reach)], first, arrived.at[0]),
        pltpu.make_async_copy(samples.at[:, pl.ds(pl.multiple_of(at[1], LANES), reach)], second, arrived.at[1]),
        pltpu.make_async_copy(samples, copied, arrived.at[2]),
    ]
    for copy in copies:
        copy.start()
    for copy in copies:
        copy.wait()


def fill_window(window, halos):
    own, reach = halos[0].shape
    for at in range(0, len(halos), 2):
        rows = slice(at // 2 * own, (at // 2 + 1) * own)
        window[rows, :reach] = halos[at][...]
        window[rows, reach : 2 * reach] = halos[at + 1][...]
    window[:, 2 * reach :] = jnp.zeros((window.shape[0], window.shape[1] - 2 * reach), BF16)


def far_pick(place, blocks, window):
    odd = lax.rem(place[0], 2) == 1
    count = blocks.shape[0]
    return window, lambda local: far_position(local, count, odd)


def own_kernel(
    place, columns, blocks_hbm, samples, first, second,
    products, blocks, z_high, z_low, gram, near_window, far_window, sums, arrived, leaving,
):
    count, _, width, _ = blocks.shape
    own = samples.shape[0]

    def chunk(step):
        rows = pl.ds(step * ROWS_A_STEP, ROWS_A_STEP)
        return pltpu.make_async_copy(blocks_hbm.at[rows], blocks.at[rows], arrived.at[step])

    for step in range(count // ROWS_A_STEP):
        chunk(step).start()
    near_window[:, : samples.shape[1]] = samples[...]
    near_window[:, samples.shape[1] :] = jnp.zeros((own, width), BF16)
    fill_window(far_window, (first, second))

    def near_position(local):
        return jnp.where((local >= 0) & (local < count), local, count)

    def emit(lanes, both):
        remote = both[own:]
        sums[:, lanes] = both[:own] + remote
        z_high[:, lanes], z_low[:, lanes] = split_two(remote)

    windows = [(near_window, near_position), far_pick(place, blocks, far_window)]
    block_rows(place, columns, blocks, windows, emit, lambda step: chunk(step).wait())
    leave = pltpu.make_async_copy(sums, products, leaving)
    leave.start()
    halves = z_high[...], z_low[...]
    gram[...] = dot_split(halves, halves, NT)
    leave.wait()


def others_kernel(parts, place, columns, blocks, *refs):
    halos = refs[: 2 * (parts - 1)]
    own_high, own_low, own_gram, z_high, z_low, packed, window, full = refs[2 * (parts - 1) :]
    own = own_high.shape[0]
    fill_window(window, halos)

    def emit(lanes, remote):
        z_high[:, lanes], z_low[:, lanes] = split_two(remote)

    block_rows(place, columns, blocks, [far_pick(place, blocks, window)], emit)
    high, low = z_high[...], z_low[...]
    all_high = jnp.concatenate([own_high[...], high], axis=0)
    all_low = jnp.concatenate([own_low[...], low], axis=0)
    gram_rows = dot_split((high, low), (all_high, all_low), NT)
    full[:own, :own] = own_gram[...]
    full[own:, :] = gram_rows
    full[:own, own:] = gram_rows[:, :own].T
    shift = place[1] * own
    pack_symmetric(packed, pltpu.roll(pltpu.roll(full[...], shift, 0), shift, 1))


def square_iota(n):
    return lax.broadcasted_iota(jnp.int32, (n, n), 0), lax.broadcasted_iota(jnp.int32, (n, n), 1)


def pack_symmetric(packed, full):
    h = full.shape[0] // 2
    row, col = square_iota(h)
    first = full[:h, :h]
    packed[:h, :] = full[:h, h:]
    packed[h : 2 * h, :] = jnp.where(row > col, first, full[h:, h:])
    diagonal = jnp.sum(jnp.where(row == col, first, 0.0), axis=0, keepdims=True)
    packed[2 * h :, :] = jnp.broadcast_to(diagonal, (GROUP, h))


def largest(packed):
    h = packed.shape[1]
    row, col = square_iota(h)
    on_diagonal = jnp.where(row == col, packed[h : 2 * h, :], 0.0)
    rows = jnp.maximum(jnp.max(on_diagonal, axis=0, keepdims=True), packed[2 * h : 2 * h + 1, :])
    return jnp.max(rows, axis=1, keepdims=True)


def unpack_symmetric(packed, full, b):
    h = packed.shape[1]
    row, col = square_iota(h)
    over = 1.0 / largest(packed)
    shared = packed[h : 2 * h, :] * over
    lower = jnp.where(row > col, shared, 0.0)
    diagonal = jnp.where(row == col, jnp.broadcast_to(packed[2 * h : 2 * h + 1, :] * over, (h, h)), 0.0)
    upper = jnp.where(row <= col, shared, 0.0)
    full[b, :h, :h] = lower + lower.T + diagonal
    full[b, h:, h:] = upper + jnp.where(row < col, upper, 0.0).T
    full[b, :h, h:] = packed[:h, :] * over


def row_of(x, j):
    return jnp.broadcast_to(x[:, j : j + 1, :], x.shape)


def start_inverse(m):
    batch, n, _ = m.shape
    row, col = square_iota(LANES)
    for b in range(batch):
        for c in range(0, n, LANES):
            for e in range(0, n, LANES):
                m[b, c : c + LANES, e : e + LANES] = (
                    (row == col).astype(F32) if e == c else jnp.zeros((LANES, LANES), F32)
                )


def clear_lower(a):
    batch, n, _ = a.shape
    for b in range(batch):
        for c in range(LANES, n, LANES):
            a[b, c : c + LANES, :c] = jnp.zeros((LANES, c), F32)


def factor(a, m, first, last):
    batch, n, _ = a.shape
    groups = PANEL // GROUP
    tile = (batch, GROUP, LANES)
    sub = lax.broadcasted_iota(jnp.int32, tile, 1)
    lane = lax.broadcasted_iota(jnp.int32, tile, 2)
    carried = None
    for p in range(first, last, PANEL):
        ch = p // LANES
        end = (ch + 1) * LANES
        parts = [(a, ch), (m, ch)]
        ahead = GROUP if p + PANEL < end else 0
        reached = groups + ahead // GROUP
        rows = [slice(p + GROUP * g, p + GROUP * (g + 1)) for g in range(reached)]
        r = [[ref[:, rows[g], c * LANES : (c + 1) * LANES] for ref, c in parts] for g in range(reached)]
        if carried is not None:
            r[0] = carried
        for g0 in range(groups):
            at = p - ch * LANES + GROUP * g0
            v = [
                [jnp.broadcast_to(r[g][0][:, :, at + k : at + k + 1], tile) for k in range(GROUP)]
                if g >= g0
                else None
                for g in range(reached)
            ]
            head, top = v[g0], r[g0]
            steps, leading = [], [None] * len(top)
            pivots = cross = dets = None
            for j in range(0, GROUP, 2):
                p00, p10, p11 = row_of(head[j], j), row_of(head[j], j + 1), row_of(head[j + 1], j + 1)
                det = p00 * p11 - p10 * p10
                guess = pl.reciprocal(det, approx=True)
                refine = 2.0 - det * guess
                later = range(j + 2, GROUP)
                v_rows = {k: (row_of(head[k], j), row_of(head[k], j + 1)) for k in later}
                r_rows = [(row_of(x, j), row_of(x, j + 1)) for x in top]
                here = sub >= j
                pivots = p00 if j == 0 else jnp.where(here, p00, pivots)
                cross = p10 if j == 0 else jnp.where(here, p10, cross)
                dets = det if j == 0 else jnp.where(here, det, dets)
                leading = [x0 if j == 0 else jnp.where(here, x0, old) for (x0, _), old in zip(r_rows, leading)]
                c0 = jnp.where(sub > j + 1, head[j], 0.0)
                c1 = jnp.where(sub > j + 1, head[j + 1], 0.0)
                for k in later[:2]:
                    x0, x1 = v_rows[k]
                    term = c0 * (p11 * x0 - p10 * x1) + c1 * (p00 * x1 - p10 * x0)
                    head[k] = head[k] - (term * guess) * refine
                inverse = guess * refine
                q00, q10, q11 = p11 * inverse, p10 * inverse, p00 * inverse
                steps.append((j, q00, q10, q11, v_rows, r_rows))
                if j + 2 < GROUP:
                    w0, w1 = c0 * q00 - c1 * q10, c1 * q11 - c0 * q10
                    for k in later[2:]:
                        head[k] = head[k] - w0 * v_rows[k][0] - w1 * v_rows[k][1]
                    for x in range(len(top)):
                        top[x] = top[x] - w0 * r_rows[x][0] - w1 * r_rows[x][1]
            for g in range(g0 + 1, reached):
                for j, q00, q10, q11, v_rows, r_rows in steps:
                    c0, c1 = v[g][j], v[g][j + 1]
                    w0, w1 = c0 * q00 - c1 * q10, c1 * q11 - c0 * q10
                    for k in range(j + 2, GROUP):
                        v[g][k] = v[g][k] - w0 * v_rows[k][0] - w1 * v_rows[k][1]
                    for x in range(len(top)):
                        r[g][x] = r[g][x] - w0 * r_rows[x][0] - w1 * r_rows[x][1]
            second_row = sub % 2 == 1
            over = invert(pivots)
            ratio = jnp.where(second_row, cross * over, 0.0)
            scale = lax.rsqrt(jnp.where(second_row, dets * over, pivots))
            for x, (ref, c) in enumerate(parts):
                done = (top[x] - ratio * leading[x]) * scale
                if ref is a and c == ch:
                    done = jnp.where(lane >= sub + at, done, 0.0)
                r[g0][x] = done
                ref[:, rows[g0], c * LANES : (c + 1) * LANES] = done
        carried = None
        if p + PANEL == end:
            join_chunks(a, m, ch)
            continue
        carried = r[groups]
        if p + PANEL >= last:
            for x, (ref, c) in enumerate(parts):
                ref[:, rows[groups], c * LANES : (c + 1) * LANES] = carried[x]
        for b in range(batch):
            panel = jnp.concatenate(
                [jnp.concatenate([r[g][x][b] for g in range(groups)], axis=0) for x in range(len(parts))], axis=1
            )
            high, low = split_two(panel)
            left = jnp.concatenate([high[:, :LANES], high[:, :LANES], low[:, :LANES]], axis=0)
            right = jnp.concatenate([high, low, high], axis=0)
            start = p + PANEL + ahead
            if start == end:
                continue
            update = dot(left, right, TN)[start - ch * LANES :, :]
            for x, (ref, e) in enumerate(parts):
                lanes = slice(e * LANES, (e + 1) * LANES)
                ref[b, start:end, lanes] = ref[b, start:end, lanes] - update[:, x * LANES : (x + 1) * LANES]


def join_chunks(a, m, ch):
    batch, n, _ = a.shape
    here = slice(ch * LANES, (ch + 1) * LANES)
    for b in range(batch):
        inverse = split_two(m[b, here, here])
        if ch > 0:
            before = slice(0, ch * LANES)
            m[b, here, before] = -dot_split(inverse, split_two(m[b, here, before]), NN)
        later = slice((ch + 1) * LANES, n)
        if later.start == n:
            continue
        upper = dot_split(inverse, split_two(a[b, here, later]), NN)
        a[b, here, later] = upper
        upper = split_two(upper)
        done = split_two(m[b, here, : (ch + 1) * LANES])
        both = tuple(jnp.concatenate(pair, axis=1) for pair in zip(upper, done))
        update = dot_split(upper, both, TN)
        a[b, later, later] = a[b, later, later] - update[:, : n - later.start]
        m[b, later, : later.start] = m[b, later, : later.start] + update[:, n - later.start :]


def invert(x):
    guess = pl.reciprocal(x, approx=True)
    return guess * (2.0 - x * guess)


def own_rows(place, own):
    return pl.ds(pl.multiple_of(place[1] * own, own), own)


def first_kernel(stop, packed_zero, packed_one, a, m):
    unpack_symmetric(packed_zero, a, 0)
    unpack_symmetric(packed_one, a, 1)
    start_inverse(m)
    factor(a, m, 0, stop)


def second_kernel(start, scale, place, packed_zero, packed_one, a_in, m_in, own_high, own_low, rest_high, rest_low,
                  bases, transfer, upper_own, a, m):
    del a_in, m_in
    n = a.shape[1]
    factor(a, m, start, n)
    clear_lower(a)
    own = upper_own.shape[0]
    rows = own_rows(place, own)
    size_zero, size_one = largest(packed_zero), largest(packed_one)
    upper_own[...] = a[1, rows, :] * jnp.sqrt(size_one)
    child = a[0, rows, :] * (jnp.sqrt(size_zero) * lax.rsqrt(size_one))
    transfer[...] = dot_split(split_two(m[1]), split_two(child), NT)
    turned = pltpu.roll(m[0, rows, :] * (lax.rsqrt(size_zero) * scale), lax.rem(n - place[1] * own, n), 1)
    inverse = split_two(turned)
    for c in range(0, own_high.shape[1], 512):
        lanes = slice(c, c + 512)
        high = jnp.concatenate([own_high[:, lanes], rest_high[:, lanes]], axis=0)
        low = jnp.concatenate([own_low[:, lanes], rest_low[:, lanes]], axis=0)
        bases[:, lanes] = dot_split(inverse, (high, low), NN)


def tree_kernel(top_scale, place, upper_own, *refs):
    levels = (len(refs) - 3) // 2
    packed = refs[:levels]
    transfers = refs[levels : 2 * levels]
    top, a, m = refs[2 * levels :]
    for b in range(levels):
        unpack_symmetric(packed[b], a, b)
    start_inverse(m)
    factor(a, m, 0, a.shape[1])
    clear_lower(a)
    own = upper_own.shape[0]
    rows = own_rows(place, own)
    sizes = [largest(ref) for ref in packed]
    child = upper_own[...]
    for b in range(levels):
        child = child * lax.rsqrt(sizes[b])
        transfers[b][...] = dot_split(split_two(m[b]), split_two(child), NT)
        child = a[b, rows, :] * jnp.sqrt(sizes[b])
    top[...] = (child * top_scale).T


def whole():
    return pl.BlockSpec(memory_space=pltpu.VMEM)


def params(limit=VMEM_LIMIT):
    return pltpu.CompilerParams(vmem_limit_bytes=limit)


def from_partner(block, axis, bit):
    count = lax.axis_size(axis)
    route = []
    for low in range(count):
        high = low | 1 << bit
        if high != low and high < count:
            route += [(low, high), (high, low)]
    return lax.ppermute(block, axis, route)


def swap_across(block, odd_start):
    count = lax.axis_size("leaf")
    route = []
    for low in range(odd_start, count - 1, 2):
        route += [(low, low + 1), (low + 1, low)]
    return lax.ppermute(block, "leaf", route)


def sample_shift(block, d):
    count = lax.axis_size("samp")
    return lax.ppermute(block, "samp", [(i, (i - d) % count) for i in range(count)])


def shards(stiffness, columns, samples):
    blocks_here, slots, width, _ = stiffness.shape
    own, row_count = samples.shape
    parts = lax.axis_size("samp")
    total = own * parts
    reach = HB * width
    leaf = lax.axis_index("leaf")
    place = jnp.stack([leaf, lax.axis_index("samp")]).astype(jnp.int32)
    shape = jax.ShapeDtypeStruct
    columns = columns.T

    smem = pl.BlockSpec(memory_space=pltpu.SMEM)
    hbm = pl.BlockSpec(memory_space=pltpu.HBM)
    rest = total - own
    window_lanes = 2 * reach + width
    far_end = row_count - reach
    odd = lax.rem(leaf, 2)
    reach_shape = shape((own, reach), BF16)
    samples, first, second = pl.pallas_call(
        prepare_kernel,
        in_specs=[smem, hbm],
        out_specs=[whole()] * 3,
        out_shape=[shape(samples.shape, BF16), reach_shape, reach_shape],
        scratch_shapes=[pltpu.SemaphoreType.DMA((3,))],
        compiler_params=params(VMEM_NEAR),
        name="prepare",
    )(jnp.stack([far_end * (1 - odd), far_end * odd]).astype(jnp.int32), samples)

    halos = [swap_across(first, 0), swap_across(second, 1)]
    other_halos = [sample_shift(halo, d) for d in range(1, parts) for halo in halos]

    products, blocks, own_high, own_low, own_gram = pl.pallas_call(
        own_kernel,
        in_specs=[smem, smem, hbm] + [whole()] * 3,
        out_specs=[hbm] + [whole()] * 4,
        out_shape=[
            shape((own, row_count), F32),
            shape(stiffness.shape, BF16),
            shape((own, row_count), BF16),
            shape((own, row_count), BF16),
            shape((own, own), F32),
        ],
        scratch_shapes=[
            pltpu.VMEM((own, row_count + width), BF16),
            pltpu.VMEM((own, window_lanes), BF16),
            pltpu.VMEM((own, row_count), F32),
            pltpu.SemaphoreType.DMA((blocks_here // ROWS_A_STEP,)),
            pltpu.SemaphoreType.DMA,
        ],
        compiler_params=params(VMEM_NEAR),
        cost_estimate=pl.CostEstimate(
            flops=4 * own * slots * width * row_count, bytes_accessed=6 * 1024 * 1024, transcendentals=0
        ),
        name="own",
    )(place, columns, stiffness, samples, *halos)

    packed_shape = (total + GROUP, total // 2)
    rest_high, rest_low, packed = pl.pallas_call(
        functools.partial(others_kernel, parts),
        in_specs=[smem, smem] + [whole()] * (2 * parts + 2),
        out_specs=[whole()] * 3,
        out_shape=[shape((rest, row_count), BF16), shape((rest, row_count), BF16), shape(packed_shape, F32)],
        scratch_shapes=[pltpu.VMEM((rest, window_lanes), BF16), pltpu.VMEM((total, total), F32)],
        compiler_params=params(),
        name="others",
    )(place, columns, blocks, *other_halos, own_high, own_low, own_gram)

    square = shape((2, total, total), F32)
    split_row = total * FIRST_EIGHTHS // 8 // PANEL * PANEL
    transfer_shape = shape((total, own), F32)
    gram_one = packed + from_partner(packed, "leaf", 0)
    gram_two = gram_one + from_partner(gram_one, "leaf", 1)
    a, m = pl.pallas_call(
        functools.partial(first_kernel, split_row),
        in_specs=[whole()] * 2,
        out_specs=[whole()] * 2,
        out_shape=[square] * 2,
        compiler_params=params(),
        cost_estimate=pl.CostEstimate(flops=3 * 10**9, bytes_accessed=1024 * 1024, transcendentals=0),
        name="first",
    )(packed, gram_one)
    gram_three = gram_two + from_partner(gram_two, "leaf", 2)
    bases, transfer_one, upper_own, _, _ = pl.pallas_call(
        functools.partial(second_kernel, split_row, math.sqrt(row_count)),
        in_specs=[smem] + [whole()] * 8,
        out_specs=[whole()] * 5,
        out_shape=[shape((own, row_count), F32), transfer_shape, shape((own, total), F32), square, square],
        input_output_aliases={3: 3, 4: 4},
        compiler_params=params(),
        cost_estimate=pl.CostEstimate(flops=3 * 10**9, bytes_accessed=1024 * 1024, transcendentals=0),
        name="second",
    )(place, packed, gram_one, a, m, own_high, own_low, rest_high, rest_low)
    transfer_two, transfer_three, top_factor = pl.pallas_call(
        functools.partial(tree_kernel, 1.0 / math.sqrt(2**LEVELS * row_count)),
        in_specs=[smem] + [whole()] * 3,
        out_specs=[whole()] * 3,
        out_shape=[transfer_shape] * 3,
        scratch_shapes=[pltpu.VMEM((2, total, total), F32)] * 2,
        compiler_params=params(),
        name="tree",
    )(place, upper_own, gram_two, gram_three)
    return (products, bases, transfer_one, transfer_two, transfer_three, top_factor)


def solution(mesh):
    return jax.shard_map(
        shards,
        mesh=mesh,
        in_specs=(P("leaf", None, None, None), P("leaf", None), P("samp", "leaf")),
        out_specs=(
            P("samp", "leaf"),
            P("samp", "leaf"),
            P("leaf", "samp"),
            P("leaf", "samp"),
            P("leaf", "samp"),
            P("leaf", "samp"),
        ),
        check_vma=False,
    )
```

```python
import functools
import math

import jax
import jax.numpy as jnp
from jax import lax
from jax.experimental import pallas as pl
from jax.experimental.pallas import tpu as pltpu
from jax.sharding import PartitionSpec as P

HB = 4
LEVELS = 3
LANES = 128
GROUP = 8
PANEL = 32
FIRST_EIGHTHS = 5
ROWS_A_STEP = 4
VMEM_LIMIT = 20 * 1024 * 1024
VMEM_NEAR = 48 * 1024 * 1024
F32 = jnp.float32
BF16 = jnp.bfloat16
NN = (((1,), (0,)), ((), ()))
NT = (((1,), (1,)), ((), ()))
TN = (((0,), (0,)), ((), ()))


def dot(a, b, dims):
    return lax.dot_general(a, b, dims, preferred_element_type=F32)


def split_two(x):
    high = x.astype(BF16)
    return high, (x - high.astype(F32)).astype(BF16)


def dot_split(a, b, dims):
    (a_high, a_low), (b_high, b_low) = a, b
    return dot(a_high, b_high, dims) + (dot(a_high, b_low, dims) + dot(a_low, b_high, dims))


def far_position(local, count, odd):
    lower = jnp.where(odd, 0, HB)
    below = jnp.clip(local + HB, 0, HB - 1) + lower
    above = jnp.clip(local - count, 0, HB - 1) + (HB - lower)
    return jnp.where(local < 0, below, jnp.where(local < count, 2 * HB, above))


def block_rows(place, columns, blocks, windows, emit, before=None):
    count, slots, width, _ = blocks.shape

    def body(step, carry):
        if before is not None:
            before(step)
        for rr in range(ROWS_A_STEP):
            row = step * ROWS_A_STEP + rr
            local = [columns[k, row] - place[0] * count for k in range(slots)]
            picked = []
            for window, position in windows:
                ats = [pl.multiple_of(position(at) * width, LANES) for at in local]
                picked.append(jnp.concatenate([window[:, pl.ds(at, width)] for at in ats], axis=1))
            stored = jnp.concatenate([blocks[row, k] for k in range(slots)], axis=1)
            product = dot(jnp.concatenate(picked, axis=0), stored, NT)
            emit(pl.ds(pl.multiple_of(row * width, LANES), width), product)
        return carry

    lax.fori_loop(0, count // ROWS_A_STEP, body, 0)


def prepare_kernel(at, samples, copied, first, second, arrived):
    reach = first.shape[1]
    copies = [
        pltpu.make_async_copy(samples.at[:, pl.ds(pl.multiple_of(at[0], LANES), reach)], first, arrived.at[0]),
        pltpu.make_async_copy(samples.at[:, pl.ds(pl.multiple_of(at[1], LANES), reach)], second, arrived.at[1]),
        pltpu.make_async_copy(samples, copied, arrived.at[2]),
    ]
    for copy in copies:
        copy.start()
    for copy in copies:
        copy.wait()


def fill_window(window, halos):
    own, reach = halos[0].shape
    for at in range(0, len(halos), 2):
        rows = slice(at // 2 * own, (at // 2 + 1) * own)
        window[rows, :reach] = halos[at][...]
        window[rows, reach : 2 * reach] = halos[at + 1][...]
    window[:, 2 * reach :] = jnp.zeros((window.shape[0], window.shape[1] - 2 * reach), BF16)


def far_pick(place, blocks, window):
    odd = lax.rem(place[0], 2) == 1
    count = blocks.shape[0]
    return window, lambda local: far_position(local, count, odd)


def own_kernel(
    place, columns, blocks_hbm, samples, first, second,
    products, blocks, z_high, z_low, gram, near_window, far_window, sums, arrived, leaving,
):
    count, _, width, _ = blocks.shape
    own = samples.shape[0]

    def chunk(step):
        rows = pl.ds(step * ROWS_A_STEP, ROWS_A_STEP)
        return pltpu.make_async_copy(blocks_hbm.at[rows], blocks.at[rows], arrived.at[step])

    for step in range(count // ROWS_A_STEP):
        chunk(step).start()
    near_window[:, : samples.shape[1]] = samples[...]
    near_window[:, samples.shape[1] :] = jnp.zeros((own, width), BF16)
    fill_window(far_window, (first, second))

    def near_position(local):
        return jnp.where((local >= 0) & (local < count), local, count)

    def emit(lanes, both):
        remote = both[own:]
        sums[:, lanes] = both[:own] + remote
        z_high[:, lanes], z_low[:, lanes] = split_two(remote)

    windows = [(near_window, near_position), far_pick(place, blocks, far_window)]
    block_rows(place, columns, blocks, windows, emit, lambda step: chunk(step).wait())
    leave = pltpu.make_async_copy(sums, products, leaving)
    leave.start()
    halves = z_high[...], z_low[...]
    gram[...] = dot_split(halves, halves, NT)
    leave.wait()


def others_kernel(parts, place, columns, blocks, *refs):
    halos = refs[: 2 * (parts - 1)]
    own_high, own_low, own_gram, z_high, z_low, packed, window, full = refs[2 * (parts - 1) :]
    own = own_high.shape[0]
    fill_window(window, halos)

    def emit(lanes, remote):
        z_high[:, lanes], z_low[:, lanes] = split_two(remote)

    block_rows(place, columns, blocks, [far_pick(place, blocks, window)], emit)
    high, low = z_high[...], z_low[...]
    all_high = jnp.concatenate([own_high[...], high], axis=0)
    all_low = jnp.concatenate([own_low[...], low], axis=0)
    gram_rows = dot_split((high, low), (all_high, all_low), NT)
    full[:own, :own] = own_gram[...]
    full[own:, :] = gram_rows
    full[:own, own:] = gram_rows[:, :own].T
    shift = place[1] * own
    pack_symmetric(packed, pltpu.roll(pltpu.roll(full[...], shift, 0), shift, 1))


def square_iota(n):
    return lax.broadcasted_iota(jnp.int32, (n, n), 0), lax.broadcasted_iota(jnp.int32, (n, n), 1)


def pack_symmetric(packed, full):
    h = full.shape[0] // 2
    row, col = square_iota(h)
    first = full[:h, :h]
    packed[:h, :] = full[:h, h:]
    packed[h : 2 * h, :] = jnp.where(row > col, first, full[h:, h:])
    diagonal = jnp.sum(jnp.where(row == col, first, 0.0), axis=0, keepdims=True)
    packed[2 * h :, :] = jnp.broadcast_to(diagonal, (GROUP, h))


def largest(packed):
    h = packed.shape[1]
    row, col = square_iota(h)
    on_diagonal = jnp.where(row == col, packed[h : 2 * h, :], 0.0)
    rows = jnp.maximum(jnp.max(on_diagonal, axis=0, keepdims=True), packed[2 * h : 2 * h + 1, :])
    return jnp.max(rows, axis=1, keepdims=True)


def unpack_symmetric(packed, full, b):
    h = packed.shape[1]
    row, col = square_iota(h)
    over = 1.0 / largest(packed)
    shared = packed[h : 2 * h, :] * over
    lower = jnp.where(row > col, shared, 0.0)
    diagonal = jnp.where(row == col, jnp.broadcast_to(packed[2 * h : 2 * h + 1, :] * over, (h, h)), 0.0)
    upper = jnp.where(row <= col, shared, 0.0)
    full[b, :h, :h] = lower + lower.T + diagonal
    full[b, h:, h:] = upper + jnp.where(row < col, upper, 0.0).T
    full[b, :h, h:] = packed[:h, :] * over


def row_of(x, j):
    return jnp.broadcast_to(x[:, j : j + 1, :], x.shape)


def start_inverse(m):
    batch, n, _ = m.shape
    row, col = square_iota(LANES)
    for b in range(batch):
        for c in range(0, n, LANES):
            for e in range(0, n, LANES):
                m[b, c : c + LANES, e : e + LANES] = (
                    (row == col).astype(F32) if e == c else jnp.zeros((LANES, LANES), F32)
                )


def clear_lower(a):
    batch, n, _ = a.shape
    for b in range(batch):
        for c in range(LANES, n, LANES):
            a[b, c : c + LANES, :c] = jnp.zeros((LANES, c), F32)


def factor(a, m, first, last):
    batch, n, _ = a.shape
    groups = PANEL // GROUP
    tile = (batch, GROUP, LANES)
    sub = lax.broadcasted_iota(jnp.int32, tile, 1)
    lane = lax.broadcasted_iota(jnp.int32, tile, 2)
    for p in range(first, last, PANEL):
        ch = p // LANES
        parts = [(a, ch), (m, ch)]
        rows = [slice(p + GROUP * g, p + GROUP * (g + 1)) for g in range(groups)]
        r = [[ref[:, rows[g], c * LANES : (c + 1) * LANES] for ref, c in parts] for g in range(groups)]
        for g0 in range(groups):
            at = p - ch * LANES + GROUP * g0
            v = [
                [jnp.broadcast_to(r[g][0][:, :, at + k : at + k + 1], tile) for k in range(GROUP)]
                if g >= g0
                else None
                for g in range(groups)
            ]
            head, top = v[g0], r[g0]
            steps, leading = [], [None] * len(top)
            pivots = cross = dets = None
            for j in range(0, GROUP, 2):
                p00, p10, p11 = row_of(head[j], j), row_of(head[j], j + 1), row_of(head[j + 1], j + 1)
                det = p00 * p11 - p10 * p10
                guess = pl.reciprocal(det, approx=True)
                refine = 2.0 - det * guess
                later = range(j + 2, GROUP)
                v_rows = {k: (row_of(head[k], j), row_of(head[k], j + 1)) for k in later}
                r_rows = [(row_of(x, j), row_of(x, j + 1)) for x in top]
                here = sub >= j
                pivots = p00 if j == 0 else jnp.where(here, p00, pivots)
                cross = p10 if j == 0 else jnp.where(here, p10, cross)
                dets = det if j == 0 else jnp.where(here, det, dets)
                leading = [x0 if j == 0 else jnp.where(here, x0, old) for (x0, _), old in zip(r_rows, leading)]
                c0 = jnp.where(sub > j + 1, head[j], 0.0)
                c1 = jnp.where(sub > j + 1, head[j + 1], 0.0)
                for k in later[:2]:
                    x0, x1 = v_rows[k]
                    term = c0 * (p11 * x0 - p10 * x1) + c1 * (p00 * x1 - p10 * x0)
                    head[k] = head[k] - (term * guess) * refine
                inverse = guess * refine
                q00, q10, q11 = p11 * inverse, p10 * inverse, p00 * inverse
                steps.append((j, q00, q10, q11, v_rows, r_rows))
                if j + 2 < GROUP:
                    w0, w1 = c0 * q00 - c1 * q10, c1 * q11 - c0 * q10
                    for k in later[2:]:
                        head[k] = head[k] - w0 * v_rows[k][0] - w1 * v_rows[k][1]
                    for x in range(len(top)):
                        top[x] = top[x] - w0 * r_rows[x][0] - w1 * r_rows[x][1]
            for g in range(g0 + 1, groups):
                for j, q00, q10, q11, v_rows, r_rows in steps:
                    c0, c1 = v[g][j], v[g][j + 1]
                    w0, w1 = c0 * q00 - c1 * q10, c1 * q11 - c0 * q10
                    for k in range(j + 2, GROUP):
                        v[g][k] = v[g][k] - w0 * v_rows[k][0] - w1 * v_rows[k][1]
                    for x in range(len(top)):
                        r[g][x] = r[g][x] - w0 * r_rows[x][0] - w1 * r_rows[x][1]
            second_row = sub % 2 == 1
            over = invert(pivots)
            ratio = jnp.where(second_row, cross * over, 0.0)
            scale = lax.rsqrt(jnp.where(second_row, dets * over, pivots))
            for x, (ref, c) in enumerate(parts):
                done = (top[x] - ratio * leading[x]) * scale
                if ref is a and c == ch:
                    done = jnp.where(lane >= sub + at, done, 0.0)
                r[g0][x] = done
                ref[:, rows[g0], c * LANES : (c + 1) * LANES] = done
        end = (ch + 1) * LANES
        if p + PANEL == end:
            join_chunks(a, m, ch)
            continue
        for b in range(batch):
            panel = jnp.concatenate(
                [jnp.concatenate([r[g][x][b] for g in range(groups)], axis=0) for x in range(len(parts))], axis=1
            )
            high, low = split_two(panel)
            left = jnp.concatenate([high[:, :LANES], high[:, :LANES], low[:, :LANES]], axis=0)
            right = jnp.concatenate([high, low, high], axis=0)
            update = dot(left, right, TN)[p + PANEL - ch * LANES :, :]
            for x, (ref, e) in enumerate(parts):
                lanes = slice(e * LANES, (e + 1) * LANES)
                ref[b, p + PANEL : end, lanes] = ref[b, p + PANEL : end, lanes] - update[:, x * LANES : (x + 1) * LANES]


def join_chunks(a, m, ch):
    batch, n, _ = a.shape
    here = slice(ch * LANES, (ch + 1) * LANES)
    for b in range(batch):
        inverse = split_two(m[b, here, here])
        if ch > 0:
            before = slice(0, ch * LANES)
            m[b, here, before] = -dot_split(inverse, split_two(m[b, here, before]), NN)
        later = slice((ch + 1) * LANES, n)
        if later.start == n:
            continue
        upper = dot_split(inverse, split_two(a[b, here, later]), NN)
        a[b, here, later] = upper
        upper = split_two(upper)
        done = split_two(m[b, here, : (ch + 1) * LANES])
        both = tuple(jnp.concatenate(pair, axis=1) for pair in zip(upper, done))
        update = dot_split(upper, both, TN)
        a[b, later, later] = a[b, later, later] - update[:, : n - later.start]
        m[b, later, : later.start] = m[b, later, : later.start] + update[:, n - later.start :]


def invert(x):
    guess = pl.reciprocal(x, approx=True)
    return guess * (2.0 - x * guess)


def own_rows(place, own):
    return pl.ds(pl.multiple_of(place[1] * own, own), own)


def first_kernel(stop, packed_zero, packed_one, a, m):
    unpack_symmetric(packed_zero, a, 0)
    unpack_symmetric(packed_one, a, 1)
    start_inverse(m)
    factor(a, m, 0, stop)


def second_kernel(start, a_in, m_in, a, m):
    del a_in, m_in
    factor(a, m, start, a.shape[1])
    clear_lower(a)


def tree_kernel(
    scale, top_scale, place, packed_zero, packed_one, packed_two, packed_three, a_low, m_low,
    own_high, own_low, rest_high, rest_low,
    bases, transfer_one, transfer_two, transfer_three, top, a, m, basis_rows, leaving,
):
    n = a.shape[1]
    own = own_high.shape[0]
    rows = own_rows(place, own)
    sizes = [largest(ref) for ref in (packed_zero, packed_one, packed_two, packed_three)]
    turned = pltpu.roll(m_low[0, rows, :] * (lax.rsqrt(sizes[0]) * scale), lax.rem(n - place[1] * own, n), 1)
    inverse = split_two(turned)
    for c in range(0, own_high.shape[1], 512):
        lanes = slice(c, c + 512)
        high = jnp.concatenate([own_high[:, lanes], rest_high[:, lanes]], axis=0)
        low = jnp.concatenate([own_low[:, lanes], rest_low[:, lanes]], axis=0)
        basis_rows[:, lanes] = dot_split(inverse, (high, low), NN)
    leave = pltpu.make_async_copy(basis_rows, bases, leaving)
    leave.start()
    unpack_symmetric(packed_two, a, 0)
    unpack_symmetric(packed_three, a, 1)
    start_inverse(m)
    factor(a, m, 0, n)
    clear_lower(a)
    uppers = [a_low[0, rows, :], a_low[1, rows, :], a[0, rows, :], a[1, rows, :]]
    inverses = [m_low[1], m[0], m[1]]
    transfers = [transfer_one, transfer_two, transfer_three]
    for b in range(LEVELS):
        child = uppers[b] * (jnp.sqrt(sizes[b]) * lax.rsqrt(sizes[b + 1]))
        transfers[b][...] = dot_split(split_two(inverses[b]), split_two(child), NT)
    top[...] = (uppers[LEVELS] * (jnp.sqrt(sizes[LEVELS]) * top_scale)).T
    leave.wait()


def whole():
    return pl.BlockSpec(memory_space=pltpu.VMEM)


def params(limit=VMEM_LIMIT):
    return pltpu.CompilerParams(vmem_limit_bytes=limit)


def from_partner(block, axis, bit):
    count = lax.axis_size(axis)
    route = []
    for low in range(count):
        high = low | 1 << bit
        if high != low and high < count:
            route += [(low, high), (high, low)]
    return lax.ppermute(block, axis, route)


def swap_across(block, odd_start):
    count = lax.axis_size("leaf")
    route = []
    for low in range(odd_start, count - 1, 2):
        route += [(low, low + 1), (low + 1, low)]
    return lax.ppermute(block, "leaf", route)


def sample_shift(block, d):
    count = lax.axis_size("samp")
    return lax.ppermute(block, "samp", [(i, (i - d) % count) for i in range(count)])


def shards(stiffness, columns, samples):
    blocks_here, slots, width, _ = stiffness.shape
    own, row_count = samples.shape
    parts = lax.axis_size("samp")
    total = own * parts
    reach = HB * width
    leaf = lax.axis_index("leaf")
    place = jnp.stack([leaf, lax.axis_index("samp")]).astype(jnp.int32)
    shape = jax.ShapeDtypeStruct
    columns = columns.T

    smem = pl.BlockSpec(memory_space=pltpu.SMEM)
    hbm = pl.BlockSpec(memory_space=pltpu.HBM)
    rest = total - own
    window_lanes = 2 * reach + width
    far_end = row_count - reach
    odd = lax.rem(leaf, 2)
    reach_shape = shape((own, reach), BF16)
    samples, first, second = pl.pallas_call(
        prepare_kernel,
        in_specs=[smem, hbm],
        out_specs=[whole()] * 3,
        out_shape=[shape(samples.shape, BF16), reach_shape, reach_shape],
        scratch_shapes=[pltpu.SemaphoreType.DMA((3,))],
        compiler_params=params(VMEM_NEAR),
        name="prepare",
    )(jnp.stack([far_end * (1 - odd), far_end * odd]).astype(jnp.int32), samples)

    halos = [swap_across(first, 0), swap_across(second, 1)]
    other_halos = [sample_shift(halo, d) for d in range(1, parts) for halo in halos]

    products, blocks, own_high, own_low, own_gram = pl.pallas_call(
        own_kernel,
        in_specs=[smem, smem, hbm] + [whole()] * 3,
        out_specs=[hbm] + [whole()] * 4,
        out_shape=[
            shape((own, row_count), F32),
            shape(stiffness.shape, BF16),
            shape((own, row_count), BF16),
            shape((own, row_count), BF16),
            shape((own, own), F32),
        ],
        scratch_shapes=[
            pltpu.VMEM((own, row_count + width), BF16),
            pltpu.VMEM((own, window_lanes), BF16),
            pltpu.VMEM((own, row_count), F32),
            pltpu.SemaphoreType.DMA((blocks_here // ROWS_A_STEP,)),
            pltpu.SemaphoreType.DMA,
        ],
        compiler_params=params(VMEM_NEAR),
        cost_estimate=pl.CostEstimate(
            flops=4 * own * slots * width * row_count, bytes_accessed=6 * 1024 * 1024, transcendentals=0
        ),
        name="own",
    )(place, columns, stiffness, samples, *halos)

    packed_shape = (total + GROUP, total // 2)
    rest_high, rest_low, packed = pl.pallas_call(
        functools.partial(others_kernel, parts),
        in_specs=[smem, smem] + [whole()] * (2 * parts + 2),
        out_specs=[whole()] * 3,
        out_shape=[shape((rest, row_count), BF16), shape((rest, row_count), BF16), shape(packed_shape, F32)],
        scratch_shapes=[pltpu.VMEM((rest, window_lanes), BF16), pltpu.VMEM((total, total), F32)],
        compiler_params=params(),
        name="others",
    )(place, columns, blocks, *other_halos, own_high, own_low, own_gram)

    square = shape((2, total, total), F32)
    split_row = total * FIRST_EIGHTHS // 8 // PANEL * PANEL
    transfer_shape = shape((total, own), F32)
    gram_one = packed + from_partner(packed, "leaf", 0)
    gram_two = gram_one + from_partner(gram_one, "leaf", 1)
    a, m = pl.pallas_call(
        functools.partial(first_kernel, split_row),
        in_specs=[whole()] * 2,
        out_specs=[whole()] * 2,
        out_shape=[square] * 2,
        compiler_params=params(),
        cost_estimate=pl.CostEstimate(flops=3 * 10**9, bytes_accessed=1024 * 1024, transcendentals=0),
        name="first",
    )(packed, gram_one)
    gram_three = gram_two + from_partner(gram_two, "leaf", 2)
    a, m = pl.pallas_call(
        functools.partial(second_kernel, split_row),
        in_specs=[whole()] * 2,
        out_specs=[whole()] * 2,
        out_shape=[square] * 2,
        input_output_aliases={0: 0, 1: 1},
        compiler_params=params(),
        cost_estimate=pl.CostEstimate(flops=3 * 10**9, bytes_accessed=1024 * 1024, transcendentals=0),
        name="second",
    )(a, m)
    bases, transfer_one, transfer_two, transfer_three, top_factor = pl.pallas_call(
        functools.partial(tree_kernel, math.sqrt(row_count), 1.0 / math.sqrt(2**LEVELS * row_count)),
        in_specs=[smem] + [whole()] * 10,
        out_specs=[hbm] + [whole()] * (LEVELS + 1),
        out_shape=[shape((own, row_count), F32)] + [transfer_shape] * (LEVELS + 1),
        scratch_shapes=[pltpu.VMEM((2, total, total), F32)] * 2
        + [pltpu.VMEM((own, row_count), F32), pltpu.SemaphoreType.DMA],
        compiler_params=params(),
        name="tree",
    )(place, packed, gram_one, gram_two, gram_three, a, m, own_high, own_low, rest_high, rest_low)
    return (products, bases, transfer_one, transfer_two, transfer_three, top_factor)


def solution(mesh):
    return jax.shard_map(
        shards,
        mesh=mesh,
        in_specs=(P("leaf", None, None, None), P("leaf", None), P("samp", "leaf")),
        out_specs=(
            P("samp", "leaf"),
            P("samp", "leaf"),
            P("leaf", "samp"),
            P("leaf", "samp"),
            P("leaf", "samp"),
            P("leaf", "samp"),
        ),
        check_vma=False,
    )
```

```python
import functools
import math

import jax
import jax.numpy as jnp
from jax import lax
from jax.experimental import pallas as pl
from jax.experimental.pallas import tpu as pltpu
from jax.sharding import PartitionSpec as P

HB = 4
LEVELS = 3
LANES = 128
GROUP = 8
PANEL = 32
FIRST_EIGHTHS = 5
ROWS_A_STEP = 4
VMEM_LIMIT = 20 * 1024 * 1024
VMEM_NEAR = 48 * 1024 * 1024
F32 = jnp.float32
BF16 = jnp.bfloat16
NN = (((1,), (0,)), ((), ()))
NT = (((1,), (1,)), ((), ()))
TN = (((0,), (0,)), ((), ()))


def dot(a, b, dims):
    return lax.dot_general(a, b, dims, preferred_element_type=F32)


def split_two(x):
    high = x.astype(BF16)
    return high, (x - high.astype(F32)).astype(BF16)


def dot_split(a, b, dims):
    (a_high, a_low), (b_high, b_low) = a, b
    return dot(a_high, b_high, dims) + (dot(a_high, b_low, dims) + dot(a_low, b_high, dims))


def far_position(local, count, odd):
    lower = jnp.where(odd, 0, HB)
    below = jnp.clip(local + HB, 0, HB - 1) + lower
    above = jnp.clip(local - count, 0, HB - 1) + (HB - lower)
    return jnp.where(local < 0, below, jnp.where(local < count, 2 * HB, above))


def block_rows(place, columns, blocks, windows, emit, before=None):
    count, slots, width, _ = blocks.shape

    def body(step, carry):
        if before is not None:
            before(step)
        for rr in range(ROWS_A_STEP):
            row = step * ROWS_A_STEP + rr
            local = [columns[k, row] - place[0] * count for k in range(slots)]
            picked = []
            for window, position in windows:
                ats = [pl.multiple_of(position(at) * width, LANES) for at in local]
                picked.append(jnp.concatenate([window[:, pl.ds(at, width)] for at in ats], axis=1))
            stored = jnp.concatenate([blocks[row, k] for k in range(slots)], axis=1)
            product = dot(jnp.concatenate(picked, axis=0), stored, NT)
            emit(pl.ds(pl.multiple_of(row * width, LANES), width), product)
        return carry

    lax.fori_loop(0, count // ROWS_A_STEP, body, 0)


def prepare_kernel(at, samples, copied, first, second, arrived):
    reach = first.shape[1]
    copies = [
        pltpu.make_async_copy(samples.at[:, pl.ds(pl.multiple_of(at[0], LANES), reach)], first, arrived.at[0]),
        pltpu.make_async_copy(samples.at[:, pl.ds(pl.multiple_of(at[1], LANES), reach)], second, arrived.at[1]),
        pltpu.make_async_copy(samples, copied, arrived.at[2]),
    ]
    for copy in copies:
        copy.start()
    for copy in copies:
        copy.wait()


def fill_window(window, halos):
    own, reach = halos[0].shape
    for at in range(0, len(halos), 2):
        rows = slice(at // 2 * own, (at // 2 + 1) * own)
        window[rows, :reach] = halos[at][...]
        window[rows, reach : 2 * reach] = halos[at + 1][...]
    window[:, 2 * reach :] = jnp.zeros((window.shape[0], window.shape[1] - 2 * reach), BF16)


def far_pick(place, blocks, window):
    odd = lax.rem(place[0], 2) == 1
    count = blocks.shape[0]
    return window, lambda local: far_position(local, count, odd)


def own_kernel(
    place, columns, blocks_hbm, samples, first, second,
    products, blocks, z_high, z_low, gram, near_window, far_window, sums, arrived, leaving,
):
    count, _, width, _ = blocks.shape
    own = samples.shape[0]

    def chunk(step):
        rows = pl.ds(step * ROWS_A_STEP, ROWS_A_STEP)
        return pltpu.make_async_copy(blocks_hbm.at[rows], blocks.at[rows], arrived.at[step])

    for step in range(count // ROWS_A_STEP):
        chunk(step).start()
    near_window[:, : samples.shape[1]] = samples[...]
    near_window[:, samples.shape[1] :] = jnp.zeros((own, width), BF16)
    fill_window(far_window, (first, second))

    def near_position(local):
        return jnp.where((local >= 0) & (local < count), local, count)

    def emit(lanes, both):
        remote = both[own:]
        sums[:, lanes] = both[:own] + remote
        z_high[:, lanes], z_low[:, lanes] = split_two(remote)

    windows = [(near_window, near_position), far_pick(place, blocks, far_window)]
    block_rows(place, columns, blocks, windows, emit, lambda step: chunk(step).wait())
    leave = pltpu.make_async_copy(sums, products, leaving)
    leave.start()
    halves = z_high[...], z_low[...]
    gram[...] = dot_split(halves, halves, NT)
    leave.wait()


def others_kernel(parts, place, columns, blocks, *refs):
    halos = refs[: 2 * (parts - 1)]
    own_high, own_low, own_gram, z_high, z_low, packed, window, full = refs[2 * (parts - 1) :]
    own = own_high.shape[0]
    fill_window(window, halos)

    def emit(lanes, remote):
        z_high[:, lanes], z_low[:, lanes] = split_two(remote)

    block_rows(place, columns, blocks, [far_pick(place, blocks, window)], emit)
    high, low = z_high[...], z_low[...]
    all_high = jnp.concatenate([own_high[...], high], axis=0)
    all_low = jnp.concatenate([own_low[...], low], axis=0)
    gram_rows = dot_split((high, low), (all_high, all_low), NT)
    full[:own, :own] = own_gram[...]
    full[own:, :] = gram_rows
    full[:own, own:] = gram_rows[:, :own].T
    shift = place[1] * own
    pack_symmetric(packed, pltpu.roll(pltpu.roll(full[...], shift, 0), shift, 1))


def square_iota(n):
    return lax.broadcasted_iota(jnp.int32, (n, n), 0), lax.broadcasted_iota(jnp.int32, (n, n), 1)


def pack_symmetric(packed, full):
    h = full.shape[0] // 2
    row, col = square_iota(h)
    first = full[:h, :h]
    packed[:h, :] = full[:h, h:]
    packed[h : 2 * h, :] = jnp.where(row > col, first, full[h:, h:])
    diagonal = jnp.sum(jnp.where(row == col, first, 0.0), axis=0, keepdims=True)
    packed[2 * h :, :] = jnp.broadcast_to(diagonal, (GROUP, h))


def largest(packed):
    h = packed.shape[1]
    row, col = square_iota(h)
    on_diagonal = jnp.where(row == col, packed[h : 2 * h, :], 0.0)
    rows = jnp.maximum(jnp.max(on_diagonal, axis=0, keepdims=True), packed[2 * h : 2 * h + 1, :])
    return jnp.max(rows, axis=1, keepdims=True)


def unpack_symmetric(packed, full, b):
    h = packed.shape[1]
    row, col = square_iota(h)
    over = 1.0 / largest(packed)
    shared = packed[h : 2 * h, :] * over
    lower = jnp.where(row > col, shared, 0.0)
    diagonal = jnp.where(row == col, jnp.broadcast_to(packed[2 * h : 2 * h + 1, :] * over, (h, h)), 0.0)
    upper = jnp.where(row <= col, shared, 0.0)
    full[b, :h, :h] = lower + lower.T + diagonal
    full[b, h:, h:] = upper + jnp.where(row < col, upper, 0.0).T
    full[b, :h, h:] = packed[:h, :] * over


def row_of(x, j):
    return jnp.broadcast_to(x[:, j : j + 1, :], x.shape)


def start_inverse(m):
    batch, n, _ = m.shape
    row, col = square_iota(LANES)
    for b in range(batch):
        for c in range(0, n, LANES):
            for e in range(0, n, LANES):
                m[b, c : c + LANES, e : e + LANES] = (
                    (row == col).astype(F32) if e == c else jnp.zeros((LANES, LANES), F32)
                )


def clear_lower(a):
    batch, n, _ = a.shape
    for b in range(batch):
        for c in range(LANES, n, LANES):
            a[b, c : c + LANES, :c] = jnp.zeros((LANES, c), F32)


def factor(a, m, first, last):
    batch, n, _ = a.shape
    groups = PANEL // GROUP
    tile = (batch, GROUP, LANES)
    sub = lax.broadcasted_iota(jnp.int32, tile, 1)
    lane = lax.broadcasted_iota(jnp.int32, tile, 2)
    for p in range(first, last, PANEL):
        ch = p // LANES
        parts = [(a, ch), (m, ch)]
        rows = [slice(p + GROUP * g, p + GROUP * (g + 1)) for g in range(groups)]
        r = [[ref[:, rows[g], c * LANES : (c + 1) * LANES] for ref, c in parts] for g in range(groups)]
        for g0 in range(groups):
            at = p - ch * LANES + GROUP * g0
            v = [
                [jnp.broadcast_to(r[g][0][:, :, at + k : at + k + 1], tile) for k in range(GROUP)]
                if g >= g0
                else None
                for g in range(groups)
            ]
            head, top = v[g0], r[g0]
            steps, leading = [], [None] * len(top)
            pivots = cross = dets = None
            for j in range(0, GROUP, 2):
                p00, p10, p11 = row_of(head[j], j), row_of(head[j], j + 1), row_of(head[j + 1], j + 1)
                det = p00 * p11 - p10 * p10
                guess = pl.reciprocal(det, approx=True)
                refine = 2.0 - det * guess
                later = range(j + 2, GROUP)
                v_rows = {k: (row_of(head[k], j), row_of(head[k], j + 1)) for k in later}
                r_rows = [(row_of(x, j), row_of(x, j + 1)) for x in top]
                here = sub >= j
                pivots = p00 if j == 0 else jnp.where(here, p00, pivots)
                cross = p10 if j == 0 else jnp.where(here, p10, cross)
                dets = det if j == 0 else jnp.where(here, det, dets)
                leading = [x0 if j == 0 else jnp.where(here, x0, old) for (x0, _), old in zip(r_rows, leading)]
                c0 = jnp.where(sub > j + 1, head[j], 0.0)
                c1 = jnp.where(sub > j + 1, head[j + 1], 0.0)
                for k in later[:2]:
                    x0, x1 = v_rows[k]
                    term = c0 * (p11 * x0 - p10 * x1) + c1 * (p00 * x1 - p10 * x0)
                    head[k] = head[k] - (term * guess) * refine
                inverse = guess * refine
                q00, q10, q11 = p11 * inverse, p10 * inverse, p00 * inverse
                steps.append((j, q00, q10, q11, v_rows, r_rows))
                if j + 2 < GROUP:
                    w0, w1 = c0 * q00 - c1 * q10, c1 * q11 - c0 * q10
                    for k in later[2:]:
                        head[k] = head[k] - w0 * v_rows[k][0] - w1 * v_rows[k][1]
                    for x in range(len(top)):
                        top[x] = top[x] - w0 * r_rows[x][0] - w1 * r_rows[x][1]
            for g in range(g0 + 1, groups):
                for j, q00, q10, q11, v_rows, r_rows in steps:
                    c0, c1 = v[g][j], v[g][j + 1]
                    w0, w1 = c0 * q00 - c1 * q10, c1 * q11 - c0 * q10
                    for k in range(j + 2, GROUP):
                        v[g][k] = v[g][k] - w0 * v_rows[k][0] - w1 * v_rows[k][1]
                    for x in range(len(top)):
                        r[g][x] = r[g][x] - w0 * r_rows[x][0] - w1 * r_rows[x][1]
            second_row = sub % 2 == 1
            over = invert(pivots)
            ratio = jnp.where(second_row, cross * over, 0.0)
            scale = lax.rsqrt(jnp.where(second_row, dets * over, pivots))
            for x, (ref, c) in enumerate(parts):
                done = (top[x] - ratio * leading[x]) * scale
                if ref is a and c == ch:
                    done = jnp.where(lane >= sub + at, done, 0.0)
                r[g0][x] = done
                ref[:, rows[g0], c * LANES : (c + 1) * LANES] = done
        end = (ch + 1) * LANES
        if p + PANEL == end:
            join_chunks(a, m, ch)
            continue
        for b in range(batch):
            panel = jnp.concatenate(
                [jnp.concatenate([r[g][x][b] for g in range(groups)], axis=0) for x in range(len(parts))], axis=1
            )
            high, low = split_two(panel)
            left = jnp.concatenate([high[:, :LANES], high[:, :LANES], low[:, :LANES]], axis=0)
            right = jnp.concatenate([high, low, high], axis=0)
            update = dot(left, right, TN)[p + PANEL - ch * LANES :, :]
            for x, (ref, e) in enumerate(parts):
                lanes = slice(e * LANES, (e + 1) * LANES)
                ref[b, p + PANEL : end, lanes] = ref[b, p + PANEL : end, lanes] - update[:, x * LANES : (x + 1) * LANES]


def join_chunks(a, m, ch):
    batch, n, _ = a.shape
    here = slice(ch * LANES, (ch + 1) * LANES)
    for b in range(batch):
        inverse = split_two(m[b, here, here])
        if ch > 0:
            before = slice(0, ch * LANES)
            m[b, here, before] = -dot_split(inverse, split_two(m[b, here, before]), NN)
        later = slice((ch + 1) * LANES, n)
        if later.start == n:
            continue
        upper = dot_split(inverse, split_two(a[b, here, later]), NN)
        a[b, here, later] = upper
        upper = split_two(upper)
        done = split_two(m[b, here, : (ch + 1) * LANES])
        both = tuple(jnp.concatenate(pair, axis=1) for pair in zip(upper, done))
        update = dot_split(upper, both, TN)
        a[b, later, later] = a[b, later, later] - update[:, : n - later.start]
        m[b, later, : later.start] = m[b, later, : later.start] + update[:, n - later.start :]


def invert(x):
    guess = pl.reciprocal(x, approx=True)
    return guess * (2.0 - x * guess)


def own_rows(place, own):
    return pl.ds(pl.multiple_of(place[1] * own, own), own)


def first_kernel(stop, packed_zero, packed_one, a, m):
    unpack_symmetric(packed_zero, a, 0)
    unpack_symmetric(packed_one, a, 1)
    start_inverse(m)
    factor(a, m, 0, stop)


def second_kernel(start, place, packed_zero, packed_one, a_in, m_in, transfer, a, m):
    del a_in, m_in
    factor(a, m, start, a.shape[1])
    clear_lower(a)
    child = a[0, own_rows(place, transfer.shape[1]), :]
    child = child * (jnp.sqrt(largest(packed_zero)) * lax.rsqrt(largest(packed_one)))
    transfer[...] = dot_split(split_two(m[1]), split_two(child), NT)


def tree_kernel(
    scale, top_scale, place, packed_zero, packed_one, packed_two, packed_three, a_low, m_low,
    own_high, own_low, rest_high, rest_low,
    bases, transfer_two, transfer_three, top, a, m, basis_rows, leaving,
):
    n = a.shape[1]
    own = own_high.shape[0]
    rows = own_rows(place, own)
    sizes = [largest(ref) for ref in (packed_zero, packed_one, packed_two, packed_three)]
    turned = pltpu.roll(m_low[0, rows, :] * (lax.rsqrt(sizes[0]) * scale), lax.rem(n - place[1] * own, n), 1)
    inverse = split_two(turned)
    for c in range(0, own_high.shape[1], 512):
        lanes = slice(c, c + 512)
        high = jnp.concatenate([own_high[:, lanes], rest_high[:, lanes]], axis=0)
        low = jnp.concatenate([own_low[:, lanes], rest_low[:, lanes]], axis=0)
        basis_rows[:, lanes] = dot_split(inverse, (high, low), NN)
    leave = pltpu.make_async_copy(basis_rows, bases, leaving)
    leave.start()
    unpack_symmetric(packed_two, a, 0)
    unpack_symmetric(packed_three, a, 1)
    start_inverse(m)
    factor(a, m, 0, n)
    clear_lower(a)
    uppers = [a_low[1, rows, :], a[0, rows, :], a[1, rows, :]]
    for b, transfer in enumerate((transfer_two, transfer_three)):
        child = uppers[b] * (jnp.sqrt(sizes[b + 1]) * lax.rsqrt(sizes[b + 2]))
        transfer[...] = dot_split(split_two(m[b]), split_two(child), NT)
    top[...] = (uppers[-1] * (jnp.sqrt(sizes[-1]) * top_scale)).T
    leave.wait()


def whole():
    return pl.BlockSpec(memory_space=pltpu.VMEM)


def params(limit=VMEM_LIMIT):
    return pltpu.CompilerParams(vmem_limit_bytes=limit)


def from_partner(block, axis, bit):
    count = lax.axis_size(axis)
    route = []
    for low in range(count):
        high = low | 1 << bit
        if high != low and high < count:
            route += [(low, high), (high, low)]
    return lax.ppermute(block, axis, route)


def swap_across(block, odd_start):
    count = lax.axis_size("leaf")
    route = []
    for low in range(odd_start, count - 1, 2):
        route += [(low, low + 1), (low + 1, low)]
    return lax.ppermute(block, "leaf", route)


def sample_shift(block, d):
    count = lax.axis_size("samp")
    return lax.ppermute(block, "samp", [(i, (i - d) % count) for i in range(count)])


def shards(stiffness, columns, samples):
    blocks_here, slots, width, _ = stiffness.shape
    own, row_count = samples.shape
    parts = lax.axis_size("samp")
    total = own * parts
    reach = HB * width
    leaf = lax.axis_index("leaf")
    place = jnp.stack([leaf, lax.axis_index("samp")]).astype(jnp.int32)
    shape = jax.ShapeDtypeStruct
    columns = columns.T

    smem = pl.BlockSpec(memory_space=pltpu.SMEM)
    hbm = pl.BlockSpec(memory_space=pltpu.HBM)
    rest = total - own
    window_lanes = 2 * reach + width
    far_end = row_count - reach
    odd = lax.rem(leaf, 2)
    reach_shape = shape((own, reach), BF16)
    samples, first, second = pl.pallas_call(
        prepare_kernel,
        in_specs=[smem, hbm],
        out_specs=[whole()] * 3,
        out_shape=[shape(samples.shape, BF16), reach_shape, reach_shape],
        scratch_shapes=[pltpu.SemaphoreType.DMA((3,))],
        compiler_params=params(VMEM_NEAR),
        name="prepare",
    )(jnp.stack([far_end * (1 - odd), far_end * odd]).astype(jnp.int32), samples)

    halos = [swap_across(first, 0), swap_across(second, 1)]
    other_halos = [sample_shift(halo, d) for d in range(1, parts) for halo in halos]

    products, blocks, own_high, own_low, own_gram = pl.pallas_call(
        own_kernel,
        in_specs=[smem, smem, hbm] + [whole()] * 3,
        out_specs=[hbm] + [whole()] * 4,
        out_shape=[
            shape((own, row_count), F32),
            shape(stiffness.shape, BF16),
            shape((own, row_count), BF16),
            shape((own, row_count), BF16),
            shape((own, own), F32),
        ],
        scratch_shapes=[
            pltpu.VMEM((own, row_count + width), BF16),
            pltpu.VMEM((own, window_lanes), BF16),
            pltpu.VMEM((own, row_count), F32),
            pltpu.SemaphoreType.DMA((blocks_here // ROWS_A_STEP,)),
            pltpu.SemaphoreType.DMA,
        ],
        compiler_params=params(VMEM_NEAR),
        cost_estimate=pl.CostEstimate(
            flops=4 * own * slots * width * row_count, bytes_accessed=6 * 1024 * 1024, transcendentals=0
        ),
        name="own",
    )(place, columns, stiffness, samples, *halos)

    packed_shape = (total + GROUP, total // 2)
    rest_high, rest_low, packed = pl.pallas_call(
        functools.partial(others_kernel, parts),
        in_specs=[smem, smem] + [whole()] * (2 * parts + 2),
        out_specs=[whole()] * 3,
        out_shape=[shape((rest, row_count), BF16), shape((rest, row_count), BF16), shape(packed_shape, F32)],
        scratch_shapes=[pltpu.VMEM((rest, window_lanes), BF16), pltpu.VMEM((total, total), F32)],
        compiler_params=params(),
        name="others",
    )(place, columns, blocks, *other_halos, own_high, own_low, own_gram)

    square = shape((2, total, total), F32)
    split_row = total * FIRST_EIGHTHS // 8 // PANEL * PANEL
    transfer_shape = shape((total, own), F32)
    gram_one = packed + from_partner(packed, "leaf", 0)
    gram_two = gram_one + from_partner(gram_one, "leaf", 1)
    a, m = pl.pallas_call(
        functools.partial(first_kernel, split_row),
        in_specs=[whole()] * 2,
        out_specs=[whole()] * 2,
        out_shape=[square] * 2,
        compiler_params=params(),
        cost_estimate=pl.CostEstimate(flops=3 * 10**9, bytes_accessed=1024 * 1024, transcendentals=0),
        name="first",
    )(packed, gram_one)
    gram_three = gram_two + from_partner(gram_two, "leaf", 2)
    transfer_one, a, m = pl.pallas_call(
        functools.partial(second_kernel, split_row),
        in_specs=[smem] + [whole()] * 4,
        out_specs=[whole()] * 3,
        out_shape=[transfer_shape, square, square],
        input_output_aliases={3: 1, 4: 2},
        compiler_params=params(),
        cost_estimate=pl.CostEstimate(flops=3 * 10**9, bytes_accessed=1024 * 1024, transcendentals=0),
        name="second",
    )(place, packed, gram_one, a, m)
    bases, transfer_two, transfer_three, top_factor = pl.pallas_call(
        functools.partial(tree_kernel, math.sqrt(row_count), 1.0 / math.sqrt(2**LEVELS * row_count)),
        in_specs=[smem] + [whole()] * 10,
        out_specs=[hbm] + [whole()] * LEVELS,
        out_shape=[shape((own, row_count), F32)] + [transfer_shape] * LEVELS,
        scratch_shapes=[pltpu.VMEM((2, total, total), F32)] * 2
        + [pltpu.VMEM((own, row_count), F32), pltpu.SemaphoreType.DMA],
        compiler_params=params(),
        name="tree",
    )(place, packed, gram_one, gram_two, gram_three, a, m, own_high, own_low, rest_high, rest_low)
    return (products, bases, transfer_one, transfer_two, transfer_three, top_factor)


def solution(mesh):
    return jax.shard_map(
        shards,
        mesh=mesh,
        in_specs=(P("leaf", None, None, None), P("leaf", None), P("samp", "leaf")),
        out_specs=(
            P("samp", "leaf"),
            P("samp", "leaf"),
            P("leaf", "samp"),
            P("leaf", "samp"),
            P("leaf", "samp"),
            P("leaf", "samp"),
        ),
        check_vma=False,
    )
```
